32 devices in a mesh: tile: 16 (over z, x, core), freq: 2 (over y).
Axes of the slice: x: 2, y: 2, z: 4, core: 2. Of those that a mesh axis runs over, the one named last changes fastest.
Arguments:
- u_factors: bfloat16 [2, 4096, 8, 128], P('freq', 'tile'), may hold values from -0.25 to 0.25
- v_factors: bfloat16 [2, 4096, 8, 128], P('freq', 'tile'), may hold values from -0.1875 to 0.1875
- ranks: int32 [2, 8, 8], P('freq'), may hold values from 8 to 64, as said below
- observed: float32 [2, 4096, 128], P('freq', 'tile'), may hold values from -6 to 6
- start: float32 [2, 4096, 128], P('freq', 'tile'), may hold values from -6 to 6
Outputs:
- estimate: float32 [2, 4096, 128], P('freq', 'tile')
The draws below stay inside these ranges and needn't reach their ends.
Inputs may be any that keep to these rules, and one draw needn't show every extreme that they name: `ranks`: every frequency has a tile of rank 64 and a tile of rank 64 // 8.
All inputs are finite; a program needn't handle non-finite values.
Results may differ from the reference program's by a relative error of at most 0.0031.
Values may be sent and summed in bfloat16 or wider, within the bound.
No kernel may reach another device: no remote copies, remote signals or barrier semaphores. Data moves between devices by JAX's collectives and lax.ppermute only.
A program may use at most 64 MiB of HBM per device.

```python
import math
import jax
import jax.numpy as jnp
from jax import lax

NS = 64
TILE = 512
RMAX = 64
ROUNDS = 1
STEPS = 1
TR = 8
TC = 8
NCOL = 4096
NROW = 4096
FREQS = 2
N_TILE = 16


def draw_ranks(key, part):
    least = RMAX // 8
    values = jax.random.randint(key, (FREQS, TR, TC), least, RMAX - least + 1)
    values = values.at[:, 0, 0].set(RMAX)
    values = values.at[:, 0, 1].set(least)
    return values.astype(jnp.int32)


def level_of(stream_key, extent, shards, low, high):
    factor_of, own = 1.0, jax.random.fold_in(stream_key, 6)
    for axis_at, shards_of in shards:
        draws = jnp.exp(jax.random.uniform(jax.random.fold_in(own, axis_at), (shards_of,), jnp.float32, low / len(shards), high / len(shards)))
        factor_of = factor_of * jnp.repeat(draws, extent[axis_at] // shards_of).reshape([-1 if axis == axis_at else 1 for axis in range(len(extent))])
    return factor_of


def normal_values(stream_key, dims, width, most, split=(), kind=jnp.bfloat16):
    result = jax.random.normal(stream_key, dims, jnp.float32) * width
    if len(split) > 0:
        result = level_of(stream_key, dims, split, -0.22, 0.18) * result
    return jnp.clip(result, min=-most, max=most).astype(kind)


def setup_inputs(seed: int = 0) -> dict:
    key_of = jax.random.split(jax.random.key(seed), 6)
    return {
        "u_factors": normal_values(key_of[0], (FREQS, NROW, TC, 2 * RMAX), (TC * RMAX) ** -0.5, 0.25, ((0, 2), (1, 16))),
        "v_factors": normal_values(key_of[1], (FREQS, NCOL, TR, 2 * RMAX), (2 * TILE) ** -0.5, 0.1875, ((0, 2), (1, 16))),
        "ranks": draw_ranks(jax.random.fold_in(key_of[5], 71), 0),
        "observed": normal_values(key_of[3], (FREQS, NROW, 2 * NS), 1.0, 6.0, ((0, 2), (1, 16)), jnp.float32),
        "start": normal_values(key_of[4], (FREQS, NCOL, 2 * NS), 1.0, 6.0, ((0, 2), (1, 16)), jnp.float32),
    }


STEP_SIZE = 0.2
LEVEL = 0.5
TOP_PRECISION = lax.Precision.HIGHEST

def round_low(values):
    return lax.optimization_barrier(values.astype(jnp.bfloat16))

def conj_product(blocks, rank_half, source_half):
    real_part = blocks[..., :rank_half, :source_half] + blocks[..., rank_half:, source_half:]
    imaginary = blocks[..., :rank_half, source_half:] - blocks[..., rank_half:, :source_half]
    return jnp.concatenate([real_part, imaginary], axis=-1)

def complex_stack(coeffs, source_half):
    lower_rows = jnp.concatenate([-coeffs[..., source_half:], coeffs[..., :source_half]], axis=-1)
    return jnp.concatenate([coeffs, lower_rows], axis=-2)

def band_tables(band_ids, band_size):
    phases = 2.0 * jnp.pi * band_ids.astype(jnp.float32)[:, None] * jnp.arange(band_size, dtype=jnp.float32)[None, :] / band_size
    return (jnp.cos(phases), jnp.sin(phases))

def to_time(spectra, cosine_matrix, sine_matrix):
    source_half = spectra.shape[-1] // 2
    factor = 1.0 / math.sqrt(cosine_matrix.shape[1])
    input_real = spectra[..., :source_half]
    imaginary_input = spectra[..., source_half:]
    output_real = jnp.einsum('bg,biq->giq', cosine_matrix, input_real, precision=TOP_PRECISION) - jnp.einsum('bg,biq->giq', sine_matrix, imaginary_input, precision=TOP_PRECISION)
    imaginary_output = jnp.einsum('bg,biq->giq', sine_matrix, input_real, precision=TOP_PRECISION) + jnp.einsum('bg,biq->giq', cosine_matrix, imaginary_input, precision=TOP_PRECISION)
    return jnp.concatenate([output_real, imaginary_output], axis=-1) * factor

def to_freq(samples, cosine_matrix, sine_matrix):
    source_half = samples.shape[-1] // 2
    factor = 1.0 / math.sqrt(cosine_matrix.shape[1])
    input_real = samples[..., :source_half]
    imaginary_input = samples[..., source_half:]
    output_real = jnp.einsum('be,evi->bvi', cosine_matrix, input_real, precision=TOP_PRECISION) + jnp.einsum('be,evi->bvi', sine_matrix, imaginary_input, precision=TOP_PRECISION)
    imaginary_output = jnp.einsum('be,evi->bvi', cosine_matrix, imaginary_input, precision=TOP_PRECISION) - jnp.einsum('be,evi->bvi', sine_matrix, input_real, precision=TOP_PRECISION)
    return jnp.concatenate([output_real, imaginary_output], axis=-1) * factor

def thin_out(values):
    return values - jnp.clip(values, -LEVEL, LEVEL)

def descend(operands):
    left_factor, right_factor, rank_table, observed_rows, estimate = operands
    half_tile = TILE // 2
    group_size = N_TILE // TR
    row_span = TR * TILE // N_TILE
    mask_table = (jnp.arange(RMAX, dtype=jnp.int32)[None, None, :] < rank_table[:, :, None]).astype(jnp.float32)[..., None]
    mask_columns = jnp.swapaxes(mask_table, 0, 1)
    right_halves = right_factor.astype(jnp.float32).reshape(TC, 2, half_tile, TR, 2 * RMAX)
    right_tiles = right_factor.astype(jnp.float32).reshape(TC, TILE, TR, 2 * RMAX)
    left_tiles = left_factor.astype(jnp.float32).reshape(TR, TILE, TC, 2 * RMAX)
    left_groups = left_factor.astype(jnp.float32).reshape(TR, group_size, row_span, TC, 2 * RMAX)
    for turn_index in range(STEPS):
        low = round_low(estimate).astype(jnp.float32).reshape(TC, 2, half_tile, 2 * NS)
        blocks = jnp.einsum('jhcik,jhcs->jhiks', right_halves, low)
        partial_value = round_low(conj_product(blocks, RMAX, NS)).astype(jnp.float32)
        coeffs = round_low((partial_value[:, 0] + partial_value[:, 1]) * mask_columns)
        image_rows = jnp.einsum('itjk,jiks->its', left_tiles, complex_stack(coeffs, NS).astype(jnp.float32)).reshape(TR * TILE, 2 * NS)
        misfit = image_rows - observed_rows
        misfit_low = round_low(misfit).astype(jnp.float32).reshape(TR, group_size, row_span, 2 * NS)
        back_blocks = jnp.einsum('igrjk,igrs->igjks', left_groups, misfit_low)
        back_part = round_low(conj_product(back_blocks, RMAX, NS)).astype(jnp.float32)
        back_coeffs = round_low(lax.optimization_barrier(jnp.sum(back_part, axis=1)) * mask_table)
        gradient = jnp.einsum('jcik,ijks->jcs', right_tiles, complex_stack(back_coeffs, NS).astype(jnp.float32)).reshape(TC * TILE, 2 * NS)
        estimate = estimate - STEP_SIZE * gradient
    return estimate

def reference(u_factors, v_factors, ranks, observed, start):
    estimate = start
    cosine_matrix, sine_matrix = band_tables(jnp.arange(FREQS, dtype=jnp.int32), FREQS)
    for round_index in range(ROUNDS):
        estimate = lax.map(descend, (u_factors, v_factors, ranks, observed, estimate))
        thinned = thin_out(to_time(estimate, cosine_matrix, sine_matrix))
        estimate = to_freq(thinned, cosine_matrix, sine_matrix)
    return estimate
```

```python
import functools
import math

import jax
import jax.numpy as jnp
from jax import lax
from jax.experimental import pallas as pl
from jax.experimental.pallas import tpu as pltpu
from jax.sharding import PartitionSpec as P

STEP_SIZE = 0.2
LEVEL = 0.5
LANES = 128
F32 = jnp.float32
BF16 = jnp.bfloat16
VMEM_LIMIT = 32 * 1024 * 1024


def place():
    position = lax.axis_index("tile")
    return position // 2, position % 2


def signs(rows):
    lane = lax.broadcasted_iota(jnp.int32, (rows, LANES), 1)
    return jnp.where(lane < LANES // 2, 1.0, -1.0).astype(F32)


def separate(source, wide, target, masks=None):
    rows, columns = target.shape
    tiles = columns // LANES
    wide[...] = source[...].astype(F32)
    for tile in range(tiles):
        part = wide[pl.ds(tile, rows, stride=tiles), :]
        if masks is not None:
            part = jnp.where(masks[tile], part, 0.0)
        target[:, tile * LANES : (tile + 1) * LANES] = part.astype(BF16)


def adjoint_block(product, half, tile):
    columns = slice(tile * LANES, (tile + 1) * LANES)
    real, imaginary = product[:half, columns], product[half:, columns]
    return real * signs(half) + pltpu.roll(imaginary, LANES // 2, 1)


def spread_block(block, left, tile):
    half = block.shape[0]
    block = block.astype(F32)
    columns = pl.ds(pl.multiple_of(tile * LANES, LANES), LANES)
    left[:half, columns] = (block * signs(half)).astype(BF16)
    left[half:, columns] = pltpu.roll(block, LANES // 2, 1).astype(BF16)


def times_transposed(left, right):
    return lax.dot_general(left, right, (((1,), (1,)), ((), ())), preferred_element_type=F32)


def forward_kernel(start, factors, own, other, separated, wide, turned):
    chip, core = place()
    tiles = own.shape[0]
    half = own.shape[1]
    separate(factors, wide, separated)
    turned[...] = start[...].T.astype(BF16).astype(F32)
    for side, out in ((core, own), (1 - core, other)):
        rows = pl.multiple_of(side * half, half)
        values = jnp.concatenate(
            [turned[pl.ds(rows, half), :], turned[pl.ds(rows + 2 * half, half), :]], axis=0
        ).astype(BF16)
        product = jnp.dot(values, separated[...], preferred_element_type=F32)
        for tile in range(tiles):
            out[chip ^ tile] = adjoint_block(product, half, tile).astype(BF16)


def add_kernel(own, arrived, *outs):
    for shift, out in enumerate(outs):
        out[...] = (own[shift].astype(F32) + arrived[shift].astype(F32)).astype(BF16)


def rows_kernel(ranks, own, mate, observed, mate_observed, own_out, mate_out, observed_out, wide, turned):
    chip, core = place()
    half = observed_out.shape[1] // 2
    tiles = own_out.shape[1] // LANES
    lane = lax.broadcasted_iota(jnp.int32, (1, LANES), 1) % (LANES // 2)
    masks = [lane < ranks[0, chip, tile] for tile in range(tiles)]
    separate(own, wide, own_out, masks)
    separate(mate, wide, mate_out, masks)
    for index, values in enumerate((observed, mate_observed)):
        turned[...] = values[...].T
        rows = pl.multiple_of(core * half, half)
        observed_out[index, :half] = turned[pl.ds(rows, half), :]
        observed_out[index, half:] = turned[pl.ds(rows + 2 * half, half), :]


def columns_kernel(mate, mate_out, wide):
    separate(mate, wide, mate_out)


def image_kernel(tiles, *refs):
    blocks, (own, mate, observed), outs, (left,) = (
        refs[:tiles],
        refs[tiles : tiles + 3],
        refs[tiles + 3 : -1],
        refs[-1:],
    )
    chip, _ = place()
    half = blocks[0].shape[0]
    for shift in range(tiles):
        spread_block(blocks[shift][...], left, chip ^ shift)
    products = []
    for index, factors in enumerate((own, mate)):
        misfit = times_transposed(left[...], factors[...]) - observed[index]
        products.append(jnp.dot(misfit.astype(BF16), factors[...], preferred_element_type=F32))
    for tile in range(tiles):
        parts = [adjoint_block(product, half, tile).astype(BF16).astype(F32) for product in products]
        left[:half, tile * LANES : (tile + 1) * LANES] = (parts[0] + parts[1]).astype(BF16)
    for shift in range(tiles):
        columns = pl.ds(pl.multiple_of((chip ^ shift) * LANES, LANES), LANES)
        outs[shift][...] = left[:half, columns]


def gradient_kernel(tiles, *refs):
    blocks, (own, mate), (own_out, mate_out), (left,) = (
        refs[:tiles],
        refs[tiles : tiles + 2],
        refs[tiles + 2 : -1],
        refs[-1:],
    )
    chip, _ = place()
    for shift in range(tiles):
        spread_block(blocks[shift][...], left, chip ^ shift)
    mate_out[...] = times_transposed(left[...], mate[...]).astype(BF16)
    own_out[...] = times_transposed(left[...], own[...]).astype(BF16)


def shrink_kernel(band, tables, *refs):
    starts, gradients, (out, spectra) = refs[:band], refs[band : 3 * band], refs[3 * band :]
    _, core = place()
    quarter = out.shape[1] // 4
    rows = out.shape[0]
    for index in range(band):
        for side, part in ((core, gradients[2 * index]), (1 - core, gradients[2 * index + 1])):
            at = pl.multiple_of(side * quarter, quarter)
            spectra[pl.ds(at, quarter), :] = part[:quarter].astype(F32)
            spectra[pl.ds(at + 2 * quarter, quarter), :] = part[quarter:].astype(F32)
        estimate = starts[index][...] - STEP_SIZE * spectra[...].T
        starts_real, starts_imaginary = estimate[:, : 2 * quarter], estimate[:, 2 * quarter :]
        if index == 0:
            real, imaginary = [starts_real], [starts_imaginary]
        else:
            real.append(starts_real)
            imaginary.append(starts_imaginary)
    scale = 1.0 / math.sqrt(band)

    def thin(values):
        return values - jnp.clip(values, -LEVEL, LEVEL)

    if band == 2:
        def both(parts):
            return (thin((parts[0] + parts[1]) * scale) + thin((parts[0] - parts[1]) * scale)) * scale

        out[...] = jnp.concatenate([both(real), both(imaginary)], axis=1)
        return
    total_real, total_imaginary = jnp.zeros_like(real[0]), jnp.zeros_like(real[0])
    for time in range(band):
        sample_real, sample_imaginary = jnp.zeros_like(real[0]), jnp.zeros_like(real[0])
        for index in range(band):
            cosine, sine = tables[0, index, time], tables[1, index, time]
            sample_real += cosine * real[index] - sine * imaginary[index]
            sample_imaginary += sine * real[index] + cosine * imaginary[index]
        thin_real, thin_imaginary = thin(sample_real * scale), thin(sample_imaginary * scale)
        cosine, sine = tables[0, 0, time], tables[1, 0, time]
        total_real += cosine * thin_real + sine * thin_imaginary
        total_imaginary += cosine * thin_imaginary - sine * thin_real
    out[...] = jnp.concatenate([total_real, total_imaginary], axis=1) * scale


def call(kernel, name, outs, inputs, scratch=(), flops=0, smem=0):
    vmem = pl.BlockSpec(memory_space=pltpu.VMEM)
    in_specs = [pl.BlockSpec(memory_space=pltpu.SMEM)] * smem + [vmem] * (len(inputs) - smem)
    moved = sum(x.size * x.dtype.itemsize for x in [*inputs, *outs])
    return pl.pallas_call(
        kernel,
        out_shape=outs,
        in_specs=in_specs,
        out_specs=[vmem] * len(outs),
        scratch_shapes=scratch,
        compiler_params=pltpu.CompilerParams(vmem_limit_bytes=VMEM_LIMIT),
        cost_estimate=pl.CostEstimate(flops=flops, bytes_accessed=moved, transcendentals=0),
        name=name,
    )(*inputs)


def body(u_factors, v_factors, ranks, observed, start):
    count = lax.axis_size("tile")
    band = lax.axis_size("freq")
    rows, tiles, width = u_factors.shape[1:]
    sources = start.shape[2]
    half = sources // 4
    columns = tiles * width
    left_rows = u_factors.reshape(rows * tiles, width)
    right_rows = v_factors.reshape(rows * tiles, width)
    observed = observed.reshape(rows, sources)
    start = start.reshape(rows, sources)

    def shape(*dims, dtype=BF16):
        return jax.ShapeDtypeStruct(dims, dtype)

    def to_chip(value, shift):
        return lax.ppermute(value, "tile", [(i, i ^ 2 * shift) for i in range(count)])

    def to_mate(value):
        return lax.ppermute(value, "tile", [(i, i ^ 1) for i in range(count)])

    def to_band(value, shift, flip):
        pairs = [
            (i * band + f, (i ^ flip) * band + (f - shift) % band) for i in range(count) for f in range(band)
        ]
        return lax.ppermute(value, ("tile", "freq"), pairs)

    wide = pltpu.VMEM((rows * tiles, width), F32)
    turned = pltpu.VMEM((sources, rows), F32)
    factor = shape(rows, columns)
    block = shape(half, width)
    product = 2 * rows * columns * sources

    mate_left = to_mate(left_rows)
    mate_right = to_mate(right_rows)
    mate_observed = to_mate(observed)
    starts = [start] + [to_band(start, shift, 0) for shift in range(1, band)]

    own, other, own_right = call(
        forward_kernel,
        "forward",
        [shape(tiles, half, width), shape(tiles, half, width), factor],
        [start, right_rows],
        [wide, turned],
        product,
    )
    blocks = call(add_kernel, "add", [block] * tiles, [own, to_mate(other)])
    blocks = [blocks[0]] + [to_chip(blocks[shift], shift) for shift in range(1, tiles)]
    own_left, mate_left, turned_observed = call(
        rows_kernel,
        "rows",
        [factor, factor, shape(2, 2 * half, rows, dtype=F32)],
        [ranks, left_rows, mate_left, observed, mate_observed],
        [wide, turned],
        smem=1,
    )
    spread = pltpu.VMEM((2 * half, columns), BF16)
    blocks = call(
        functools.partial(image_kernel, tiles),
        "image",
        [block] * tiles,
        [*blocks, own_left, mate_left, turned_observed],
        [spread],
        2 * product,
    )
    blocks = [blocks[0]] + [to_chip(blocks[shift], shift) for shift in range(1, tiles)]
    (mate_right,) = call(columns_kernel, "columns", [factor], [mate_right], [wide])
    own_part, mate_part = call(
        functools.partial(gradient_kernel, tiles),
        "gradient",
        [shape(2 * half, rows)] * 2,
        [*blocks, own_right, mate_right],
        [spread],
        product,
    )
    gradients = [own_part, to_mate(mate_part)]
    for shift in range(1, band):
        gradients += [to_band(own_part, shift, 0), to_band(mate_part, shift, 1)]
    bands = jnp.arange(band, dtype=jnp.int32)
    phases = (2.0 * math.pi / band) * (
        (bands[:, None] + lax.axis_index("freq")) % band * bands[None, :] % band
    ).astype(F32)
    tables = jnp.stack([jnp.cos(phases), jnp.sin(phases)])
    (estimate,) = call(
        functools.partial(shrink_kernel, band),
        "shrink",
        [shape(rows, sources, dtype=F32)],
        [tables, *starts, *gradients],
        [turned],
        smem=1,
    )
    return estimate[None]


def solution(mesh):
    in_specs = (
        P("freq", "tile", None, None),
        P("freq", "tile", None, None),
        P("freq", None, None),
        P("freq", "tile", None),
        P("freq", "tile", None),
    )
    out_specs = P("freq", "tile", None)
    return jax.shard_map(body, mesh=mesh, in_specs=in_specs, out_specs=out_specs, check_vma=False)
```

```python
import functools
import math

import jax
import jax.numpy as jnp
from jax import lax
from jax.experimental import pallas as pl
from jax.experimental.pallas import tpu as pltpu
from jax.sharding import Mesh
from jax.sharding import PartitionSpec as P

STEP_SIZE = 0.2
LEVEL = 0.5
LANES = 128
F32 = jnp.float32
BF16 = jnp.bfloat16
VMEM_LIMIT = 32 * 1024 * 1024


def place():
    return lax.axis_index("chip"), lax.axis_index("core")


def signs(rows):
    lane = lax.broadcasted_iota(jnp.int32, (rows, LANES), 1)
    return jnp.where(lane < LANES // 2, 1.0, -1.0).astype(F32)


def separate(source, wide, target, masks=None):
    rows, columns = target.shape
    tiles = columns // LANES
    wide[...] = source[...].astype(F32)
    for tile in range(tiles):
        part = wide[pl.ds(tile, rows, stride=tiles), :]
        if masks is not None:
            part = jnp.where(masks[tile], part, 0.0)
        target[:, tile * LANES : (tile + 1) * LANES] = part.astype(BF16)


def adjoint_block(product, half, tile):
    columns = slice(tile * LANES, (tile + 1) * LANES)
    real, imaginary = product[:half, columns], product[half:, columns]
    return real * signs(half) + pltpu.roll(imaginary, LANES // 2, 1)


def spread_block(block, left, tile):
    half = block.shape[0]
    block = block.astype(F32)
    columns = slice(tile * LANES, (tile + 1) * LANES)
    left[:half, columns] = (block * signs(half)).astype(BF16)
    left[half:, columns] = pltpu.roll(block, LANES // 2, 1).astype(BF16)


def times_transposed(left, right):
    return lax.dot_general(left, right, (((1,), (1,)), ((), ())), preferred_element_type=F32)


def forward_kernel(start, factors, own, other, separated, wide, turned):
    _, core = place()
    tiles = own.shape[0]
    half = own.shape[1]
    separate(factors, wide, separated)
    turned[...] = start[...].T.astype(BF16).astype(F32)
    for side, out in ((core, own), (1 - core, other)):
        rows = pl.multiple_of(side * half, half)
        values = jnp.concatenate(
            [turned[pl.ds(rows, half), :], turned[pl.ds(rows + 2 * half, half), :]], axis=0
        ).astype(BF16)
        product = jnp.dot(values, separated[...], preferred_element_type=F32)
        for tile in range(tiles):
            out[tile] = adjoint_block(product, half, tile).astype(BF16)


def add_kernel(own, arrived, out):
    out[...] = (own[...].astype(F32) + arrived[...].astype(F32)).astype(BF16)


def rows_kernel(ranks, own, mate, observed, mate_observed, own_out, mate_out, observed_out, wide, turned):
    chip, core = place()
    half = observed_out.shape[1] // 2
    tiles = own_out.shape[1] // LANES
    lane = lax.broadcasted_iota(jnp.int32, (1, LANES), 1) % (LANES // 2)
    masks = [lane < ranks[0, chip, tile] for tile in range(tiles)]
    separate(own, wide, own_out, masks)
    separate(mate, wide, mate_out, masks)
    for index, values in enumerate((observed, mate_observed)):
        turned[...] = values[...].T
        rows = pl.multiple_of(core * half, half)
        observed_out[index, :half] = turned[pl.ds(rows, half), :]
        observed_out[index, half:] = turned[pl.ds(rows + 2 * half, half), :]


def columns_kernel(mate, mate_out, wide):
    separate(mate, wide, mate_out)


def image_kernel(blocks, own, mate, observed, out, left):
    chip, _ = place()
    tiles, half = out.shape[:2]
    for tile in range(tiles):
        spread_block(blocks[tile, chip], left, tile)
    products = []
    for index, factors in enumerate((own, mate)):
        misfit = times_transposed(left[...], factors[...]) - observed[index]
        products.append(jnp.dot(misfit.astype(BF16), factors[...], preferred_element_type=F32))
    for tile in range(tiles):
        parts = [adjoint_block(product, half, tile).astype(BF16).astype(F32) for product in products]
        out[tile] = (parts[0] + parts[1]).astype(BF16)


def gradient_kernel(blocks, own, mate, own_out, mate_out, left):
    for tile in range(blocks.shape[0]):
        spread_block(blocks[tile], left, tile)
    mate_out[...] = times_transposed(left[...], mate[...]).astype(BF16)
    own_out[...] = times_transposed(left[...], own[...]).astype(BF16)


def shrink_kernel(band, tables, *refs):
    starts, gradients, (out, spectra) = refs[:band], refs[band : 3 * band], refs[3 * band :]
    _, core = place()
    quarter = out.shape[1] // 4
    rows = out.shape[0]
    for index in range(band):
        for side, part in ((core, gradients[2 * index]), (1 - core, gradients[2 * index + 1])):
            at = pl.multiple_of(side * quarter, quarter)
            spectra[pl.ds(at, quarter), :] = part[:quarter].astype(F32)
            spectra[pl.ds(at + 2 * quarter, quarter), :] = part[quarter:].astype(F32)
        estimate = starts[index][...] - STEP_SIZE * spectra[...].T
        starts_real, starts_imaginary = estimate[:, : 2 * quarter], estimate[:, 2 * quarter :]
        if index == 0:
            real, imaginary = [starts_real], [starts_imaginary]
        else:
            real.append(starts_real)
            imaginary.append(starts_imaginary)
    scale = 1.0 / math.sqrt(band)

    def thin(values):
        return values - jnp.clip(values, -LEVEL, LEVEL)

    if band == 2:
        def both(parts):
            return (thin((parts[0] + parts[1]) * scale) + thin((parts[0] - parts[1]) * scale)) * scale

        out[...] = jnp.concatenate([both(real), both(imaginary)], axis=1)
        return
    total_real, total_imaginary = jnp.zeros_like(real[0]), jnp.zeros_like(real[0])
    for time in range(band):
        sample_real, sample_imaginary = jnp.zeros_like(real[0]), jnp.zeros_like(real[0])
        for index in range(band):
            cosine, sine = tables[0, index, time], tables[1, index, time]
            sample_real += cosine * real[index] - sine * imaginary[index]
            sample_imaginary += sine * real[index] + cosine * imaginary[index]
        thin_real, thin_imaginary = thin(sample_real * scale), thin(sample_imaginary * scale)
        cosine, sine = tables[0, 0, time], tables[1, 0, time]
        total_real += cosine * thin_real + sine * thin_imaginary
        total_imaginary += cosine * thin_imaginary - sine * thin_real
    out[...] = jnp.concatenate([total_real, total_imaginary], axis=1) * scale


def call(kernel, name, outs, inputs, scratch=(), flops=0, smem=0):
    vmem = pl.BlockSpec(memory_space=pltpu.VMEM)
    in_specs = [pl.BlockSpec(memory_space=pltpu.SMEM)] * smem + [vmem] * (len(inputs) - smem)
    moved = sum(x.size * x.dtype.itemsize for x in [*inputs, *outs])
    return pl.pallas_call(
        kernel,
        out_shape=outs,
        in_specs=in_specs,
        out_specs=[vmem] * len(outs),
        scratch_shapes=scratch,
        compiler_params=pltpu.CompilerParams(vmem_limit_bytes=VMEM_LIMIT),
        cost_estimate=pl.CostEstimate(flops=flops, bytes_accessed=moved, transcendentals=0),
        name=name,
    )(*inputs)


def body(u_factors, v_factors, ranks, observed, start):
    band = lax.axis_size("freq")
    rows, tiles, width = u_factors.shape[1:]
    sources = start.shape[2]
    half = sources // 4
    columns = tiles * width
    left_rows = u_factors.reshape(rows * tiles, width)
    right_rows = v_factors.reshape(rows * tiles, width)
    observed = observed.reshape(rows, sources)
    start = start.reshape(rows, sources)

    def shape(*dims, dtype=BF16):
        return jax.ShapeDtypeStruct(dims, dtype)

    def to_mate(value):
        return lax.ppermute(value, "core", [(0, 1), (1, 0)])

    def to_band(value, shift, flip):
        pairs = [
            (core * band + f, (core ^ flip) * band + (f - shift) % band) for core in range(2) for f in range(band)
        ]
        return lax.ppermute(value, ("core", "freq"), pairs)

    wide = pltpu.VMEM((rows * tiles, width), F32)
    turned = pltpu.VMEM((sources, rows), F32)
    factor = shape(rows, columns)
    blocks = shape(tiles, half, width)
    product = 2 * rows * columns * sources

    mate_left = to_mate(left_rows)
    mate_right = to_mate(right_rows)
    mate_observed = to_mate(observed)
    starts = [start] + [to_band(start, shift, 0) for shift in range(1, band)]

    own, other, own_right = call(
        forward_kernel, "forward", [blocks, blocks, factor], [start, right_rows], [wide, turned], product
    )
    (coeffs,) = call(add_kernel, "add", [blocks], [own, to_mate(other)])
    coeffs = lax.all_gather(coeffs, "chip")
    own_left, mate_left, turned_observed = call(
        rows_kernel,
        "rows",
        [factor, factor, shape(2, 2 * half, rows, dtype=F32)],
        [ranks, left_rows, mate_left, observed, mate_observed],
        [wide, turned],
        smem=1,
    )
    spread = pltpu.VMEM((2 * half, columns), BF16)
    (back,) = call(
        image_kernel, "image", [blocks], [coeffs, own_left, mate_left, turned_observed], [spread], 2 * product
    )
    back = lax.all_to_all(back, "chip", split_axis=0, concat_axis=0, tiled=True)
    (mate_right,) = call(columns_kernel, "columns", [factor], [mate_right], [wide])
    own_part, mate_part = call(
        gradient_kernel, "gradient", [shape(2 * half, rows)] * 2, [back, own_right, mate_right], [spread], product
    )
    gradients = [own_part, to_mate(mate_part)]
    for shift in range(1, band):
        gradients += [to_band(own_part, shift, 0), to_band(mate_part, shift, 1)]
    bands = jnp.arange(band, dtype=jnp.int32)
    phases = (2.0 * math.pi / band) * (
        (bands[:, None] + lax.axis_index("freq")) % band * bands[None, :] % band
    ).astype(F32)
    tables = jnp.stack([jnp.cos(phases), jnp.sin(phases)])
    (estimate,) = call(
        functools.partial(shrink_kernel, band),
        "shrink",
        [shape(rows, sources, dtype=F32)],
        [tables, *starts, *gradients],
        [turned],
        smem=1,
    )
    return estimate[None]


def solution(mesh):
    count, band = mesh.devices.shape
    cores = Mesh(mesh.devices.reshape(count // 2, 2, band), ("chip", "core", "freq"))
    tile = ("chip", "core")
    in_specs = (
        P("freq", tile, None, None),
        P("freq", tile, None, None),
        P("freq", None, None),
        P("freq", tile, None),
        P("freq", tile, None),
    )
    out_specs = P("freq", tile, None)
    return jax.shard_map(body, mesh=cores, in_specs=in_specs, out_specs=out_specs, check_vma=False)
```

```python
import functools
import math

import jax
import jax.numpy as jnp
from jax import lax
from jax.experimental import pallas as pl
from jax.experimental.pallas import tpu as pltpu
from jax.sharding import Mesh
from jax.sharding import PartitionSpec as P

STEP_SIZE = 0.2
LEVEL = 0.5
LANES = 128
F32 = jnp.float32
BF16 = jnp.bfloat16
VMEM_LIMIT = 32 * 1024 * 1024
FIRST_LIMIT = 55090 * 1024


def place():
    return lax.axis_index("z"), lax.axis_index("x"), lax.axis_index("core")


def signs(rows):
    lane = lax.broadcasted_iota(jnp.int32, (rows, LANES), 1)
    return jnp.where(lane < LANES // 2, 1.0, -1.0).astype(F32)


def separate(source, wide, target, masks=None):
    rows, columns = target.shape
    tiles = columns // LANES
    wide[...] = source[...].astype(F32)
    for tile in range(tiles):
        part = wide[pl.ds(tile, rows, stride=tiles), :]
        if masks is not None:
            part = jnp.where(masks[tile], part, 0.0)
        target[:, tile * LANES : (tile + 1) * LANES] = part.astype(BF16)


def adjoint_block(real, imaginary):
    return real * signs(real.shape[0]) + pltpu.roll(imaginary, LANES // 2, 1)


def spread_block(block, left, tile):
    half = block.shape[0]
    block = block.astype(F32)
    columns = pl.ds(pl.multiple_of(tile * LANES, LANES), LANES)
    left[:half, columns] = (block * signs(half)).astype(BF16)
    left[half:, columns] = pltpu.roll(block, LANES // 2, 1).astype(BF16)


def spread_blocks(arrived, left):
    z, x, _ = place()
    near = len(arrived)
    for t, blocks in enumerate(arrived):
        for s in range(blocks.shape[0]):
            spread_block(blocks[s], left, (z ^ s) * near + (x ^ t))


def times_transposed(left, right):
    return lax.dot_general(left, right, (((1,), (1,)), ((), ())), preferred_element_type=F32)


def forward_kernel(start, factors, own, other, separated, start_here, factors_here, wide, product, sems):
    _, _, core = place()
    tiles, half = own.shape[:2]
    loads = [
        pltpu.make_async_copy(factors, factors_here, sems.at[0]),
        pltpu.make_async_copy(start, start_here, sems.at[1]),
    ]
    for load in loads:
        load.start()
    for load in loads:
        load.wait()
    separate(factors_here, wide, separated)
    values = start_here[...].T.astype(BF16)
    product[...] = jnp.dot(values, separated[...], preferred_element_type=F32)
    for side, out in ((core, own), (1 - core, other)):
        real = pl.ds(pl.multiple_of(side * half, half), half)
        imaginary = pl.ds(pl.multiple_of((side + 2) * half, half), half)
        for tile in range(tiles):
            columns = slice(tile * LANES, (tile + 1) * LANES)
            out[tile] = adjoint_block(product[real, columns], product[imaginary, columns]).astype(BF16)


def add_kernel(own, arrived, *outs):
    z, _, _ = place()
    near = outs[0].shape[0]
    for s, out in enumerate(outs):
        at = pl.ds((z ^ s) * near, near)
        out[...] = (own[at].astype(F32) + arrived[at].astype(F32)).astype(BF16)


def repack_kernel(far, *refs):
    blocks, outs = refs[:far], refs[far:]
    _, x, _ = place()
    for t, out in enumerate(outs):
        for s, block in enumerate(blocks):
            out[s] = block[x ^ t]


def rows_kernel(ranks, own, mate, observed, mate_observed, own_out, mate_out, observed_out, wide, turned):
    z, x, core = place()
    half = observed_out.shape[1] // 2
    tiles = own_out.shape[1] // LANES
    chip = z * lax.axis_size("x") + x
    lane = lax.broadcasted_iota(jnp.int32, (1, LANES), 1) % (LANES // 2)
    masks = [lane < ranks[0, chip, tile] for tile in range(tiles)]
    separate(own, wide, own_out, masks)
    separate(mate, wide, mate_out, masks)
    for index, values in enumerate((observed, mate_observed)):
        turned[...] = values[...].T
        observed_out[index, :half] = turned[pl.ds(pl.multiple_of(core * half, half), half), :]
        observed_out[index, half:] = turned[pl.ds(pl.multiple_of((core + 2) * half, half), half), :]


def columns_kernel(mate, mate_out, wide):
    separate(mate, wide, mate_out)


def image_kernel(near, *refs):
    blocks, (own, mate, observed), outs, (left,) = refs[:near], refs[near : near + 3], refs[near + 3 : -1], refs[-1:]
    z, _, _ = place()
    half = left.shape[0] // 2
    spread_blocks(blocks, left)
    products = []
    for index, factors in enumerate((own, mate)):
        misfit = times_transposed(left[...], factors[...]) - observed[index]
        products.append(jnp.dot(misfit.astype(BF16), factors[...], preferred_element_type=F32))
    for tile in range(left.shape[1] // LANES):
        columns = slice(tile * LANES, (tile + 1) * LANES)
        parts = [
            adjoint_block(product[:half, columns], product[half:, columns]).astype(BF16).astype(F32)
            for product in products
        ]
        left[:half, columns] = (parts[0] + parts[1]).astype(BF16)
    for s, out in enumerate(outs):
        for k in range(near):
            at = pl.multiple_of(((z ^ s) * near + k) * LANES, LANES)
            out[k] = left[:half, pl.ds(at, LANES)]


def gradient_kernel(near, *refs):
    blocks, (own, mate, own_out, mate_out, left) = refs[:near], refs[near:]
    spread_blocks(blocks, left)
    mate_out[...] = times_transposed(left[...], mate[...]).astype(BF16)
    own_out[...] = times_transposed(left[...], own[...]).astype(BF16)


def thin_out(values):
    return values - jnp.clip(values, -LEVEL, LEVEL)


def shrink_kernel(band, *refs):
    tables, starts, gradients, (out, spectra) = (
        refs[: -3 * band - 2],
        refs[-3 * band - 2 : -2 * band - 2],
        refs[-2 * band - 2 : -2],
        refs[-2:],
    )
    _, _, core = place()
    quarter = out.shape[1] // 4
    estimates = []
    for index in range(band):
        for side, part in ((core, gradients[2 * index]), (1 - core, gradients[2 * index + 1])):
            for row in (0, 2):
                at = pl.multiple_of((side + row) * quarter, quarter)
                spectra[index, pl.ds(at, quarter), :] = part[row // 2 * quarter : (row // 2 + 1) * quarter].astype(F32)
        estimates.append(starts[index][...] - STEP_SIZE * spectra[index].T)
    scale = 1.0 / math.sqrt(band)
    if band == 2:
        here, there = estimates
        out[...] = (thin_out((here + there) * scale) + thin_out((here - there) * scale)) * scale
        return
    (tables,) = tables
    lane = lax.broadcasted_iota(jnp.int32, (1, out.shape[1]), 1)
    turn = jnp.where(lane < 2 * quarter, -1.0, 1.0).astype(F32)
    turned = [pltpu.roll(estimate, 2 * quarter, 1) * turn for estimate in estimates]
    total = jnp.zeros_like(estimates[0])
    for time in range(band):
        sample = jnp.zeros_like(estimates[0])
        for index in range(band):
            sample += tables[0, index, time] * estimates[index] + tables[1, index, time] * turned[index]
        thinned = thin_out(sample * scale)
        total += tables[0, 0, time] * thinned - tables[1, 0, time] * (pltpu.roll(thinned, 2 * quarter, 1) * turn)
    out[...] = total * scale


def call(kernel, name, outs, inputs, scratch=(), flops=0, spaces=(), limit=VMEM_LIMIT):
    spaces = (*spaces, *[pltpu.VMEM] * (len(inputs) - len(spaces)))
    moved = sum(x.size * x.dtype.itemsize for x in [*inputs, *outs])
    return pl.pallas_call(
        kernel,
        out_shape=outs,
        in_specs=[pl.BlockSpec(memory_space=space) for space in spaces],
        out_specs=[pl.BlockSpec(memory_space=pltpu.VMEM)] * len(outs),
        scratch_shapes=scratch,
        compiler_params=pltpu.CompilerParams(vmem_limit_bytes=limit),
        cost_estimate=pl.CostEstimate(flops=flops, bytes_accessed=moved, transcendentals=0),
        name=name,
    )(*inputs)


def swap(value, axis, shift):
    return lax.ppermute(value, axis, [(i, i ^ shift) for i in range(lax.axis_size(axis))])


def to_band(value, shift, flip):
    band = lax.axis_size("freq")
    pairs = [(core * band + f, (core ^ flip) * band + (f - shift) % band) for core in range(2) for f in range(band)]
    return lax.ppermute(value, ("core", "freq"), pairs)


def after(value, *others):
    return lax.optimization_barrier((value, *others))[0]


def body(u_factors, v_factors, ranks, observed, start):
    band = lax.axis_size("freq")
    far, near = lax.axis_size("z"), lax.axis_size("x")
    rows, tiles, width = u_factors.shape[1:]
    sources = start.shape[2]
    half = sources // 4
    columns = tiles * width
    left_rows = u_factors.reshape(rows * tiles, width)
    right_rows = v_factors.reshape(rows * tiles, width)
    observed = observed.reshape(rows, sources)
    start = start.reshape(rows, sources)

    def shape(*dims, dtype=BF16):
        return jax.ShapeDtypeStruct(dims, dtype)

    wide = pltpu.VMEM((rows * tiles, width), F32)
    factor = shape(rows, columns)
    blocks = shape(tiles, half, width)
    product = 2 * rows * columns * sources
    along_z = [shape(near, half, width)] * far
    along_x = [shape(far, half, width)] * near

    own, other, own_right = call(
        forward_kernel,
        "forward",
        [blocks, blocks, factor],
        [start, right_rows],
        [
            pltpu.VMEM(start.shape, F32),
            pltpu.VMEM(right_rows.shape, BF16),
            wide,
            pltpu.VMEM((sources, columns), F32),
            pltpu.SemaphoreType.DMA((2,)),
        ],
        product,
        [pltpu.HBM] * 2,
        limit=FIRST_LIMIT,
    )
    mate_left = swap(after(left_rows, other), "core", 1)
    mate_observed = swap(after(observed, other), "core", 1)
    sends = call(add_kernel, "add", along_z, [own, swap(other, "core", 1)])
    arrived = [sends[0], *[swap(sends[s], "z", s) for s in reversed(range(1, far))][::-1]]
    mate_right = swap(after(right_rows, sends[0]), "core", 1)
    sends = call(functools.partial(repack_kernel, far), "repack", along_x, arrived)
    arrived = [sends[0], *[swap(sends[t], "x", t) for t in range(1, near)]]
    starts = [start] + [to_band(after(start, sends[0]), shift, 0) for shift in range(1, band)]
    own_left, mate_left, turned_observed = call(
        rows_kernel,
        "rows",
        [factor, factor, shape(2, 2 * half, rows, dtype=F32)],
        [ranks, left_rows, mate_left, observed, mate_observed],
        [wide, pltpu.VMEM((sources, rows), F32)],
        spaces=[pltpu.SMEM],
    )
    spread = pltpu.VMEM((2 * half, columns), BF16)
    sends = call(
        functools.partial(image_kernel, near),
        "image",
        along_z,
        [*arrived, own_left, mate_left, turned_observed],
        [spread],
        2 * product,
    )
    arrived = [sends[0], *[swap(sends[s], "z", s) for s in reversed(range(1, far))][::-1]]
    sends = call(functools.partial(repack_kernel, far), "repack", along_x, arrived)
    arrived = [sends[0], *[swap(sends[t], "x", t) for t in range(1, near)]]
    (mate_right,) = call(columns_kernel, "columns", [factor], [mate_right], [wide])
    own_part, mate_part = call(
        functools.partial(gradient_kernel, near),
        "gradient",
        [shape(2 * half, rows)] * 2,
        [*arrived, own_right, mate_right],
        [spread],
        product,
    )
    gradients = [own_part, swap(mate_part, "core", 1)]
    for shift in range(1, band):
        gradients += [to_band(own_part, shift, 0), to_band(mate_part, shift, 1)]
    inputs, spaces = [*starts, *gradients], []
    if band > 2:
        bands = jnp.arange(band, dtype=jnp.int32)
        phases = (bands[:, None] + lax.axis_index("freq")) * bands[None, :] % band
        phases = (2.0 * math.pi / band) * phases.astype(F32)
        inputs, spaces = [jnp.stack([jnp.cos(phases), jnp.sin(phases)]), *inputs], [pltpu.SMEM]
    (estimate,) = call(
        functools.partial(shrink_kernel, band),
        "shrink",
        [shape(rows, sources, dtype=F32)],
        inputs,
        [pltpu.VMEM((band, sources, rows), F32)],
        spaces=spaces,
    )
    return estimate[None]


def solution(mesh):
    count, band = mesh.devices.shape
    chips = count // 2
    near = 2 ** ((chips.bit_length() - 1) // 2)
    parts = Mesh(mesh.devices.reshape(chips // near, near, 2, band), ("z", "x", "core", "freq"))
    tile = ("z", "x", "core")
    in_specs = (
        P("freq", tile, None, None),
        P("freq", tile, None, None),
        P("freq", None, None),
        P("freq", tile, None),
        P("freq", tile, None),
    )
    out_specs = P("freq", tile, None)
    return jax.shard_map(body, mesh=parts, in_specs=in_specs, out_specs=out_specs, check_vma=False)
```

```python
import functools
import math

import jax
import jax.numpy as jnp
from jax import lax
from jax.experimental import pallas as pl
from jax.experimental.pallas import tpu as pltpu
from jax.sharding import PartitionSpec as P

STEP_SIZE = 0.2
LEVEL = 0.5
LANES = 128
VMEM_LIMIT = 32 * 1024 * 1024
FIRST_LIMIT = 55050 * 1024
F32 = jnp.float32
BF16 = jnp.bfloat16


def shifts_of(chips):
    far_first = sorted(range(chips), key=lambda shift: (-shift.bit_count(), -shift))
    return [[far_first[at] for at in range(chips) if (at + 1) // 2 % 2 == core] for core in range(2)]


def place():
    position = lax.axis_index("tile")
    return position // 2, position % 2


def columns_of(tile):
    return pl.ds(pl.multiple_of(tile * LANES, LANES), LANES)


def both_shifts(shifts):
    chip, core = place()
    pairs = list(zip(*shifts))
    own = [chip ^ jnp.where(core == 0, first, second) for first, second in pairs]
    mate = [chip ^ jnp.where(core == 0, second, first) for first, second in pairs]
    return own, mate


def signs(rows):
    lane = lax.broadcasted_iota(jnp.int32, (rows, LANES), 1)
    return jnp.where(lane < LANES // 2, 1.0, -1.0).astype(F32)


def separate(source, wide, target, masks=None):
    rows, columns = target.shape
    tiles = columns // LANES
    wide[...] = source[...].astype(F32)
    for tile in range(tiles):
        part = wide[pl.ds(tile, rows, stride=tiles), :]
        if masks is not None:
            part = jnp.where(masks[tile], part, 0.0)
        target[:, tile * LANES : (tile + 1) * LANES] = part.astype(BF16)


def adjoint_blocks(product, shifts, keep, give):
    half = keep.shape[1]
    for out, tiles in zip((keep, give), both_shifts(shifts)):
        for index, tile in enumerate(tiles):
            real, imaginary = product[:half, columns_of(tile)], product[half:, columns_of(tile)]
            out[index] = (real * signs(half) + pltpu.roll(imaginary, LANES // 2, 1)).astype(BF16)


def spread_blocks(own, mate, shifts, left):
    half = own.shape[1]
    for blocks, tiles in zip((own, mate), both_shifts(shifts)):
        for index, tile in enumerate(tiles):
            block = blocks[index].astype(F32)
            left[:half, columns_of(tile)] = (block * signs(half)).astype(BF16)
            left[half:, columns_of(tile)] = pltpu.roll(block, LANES // 2, 1).astype(BF16)


def times_transposed(left, right):
    return lax.dot_general(left, right, (((1,), (1,)), ((), ())), preferred_element_type=F32)


def forward_kernel(shifts, start, factors, keep, give, start_here, factors_here, wide, separated, product, sems):
    loads = [
        pltpu.make_async_copy(factors, factors_here, sems.at[0]),
        pltpu.make_async_copy(start, start_here, sems.at[1]),
    ]
    for load in loads:
        load.start()
    for load in loads:
        load.wait()
    separate(factors_here, wide, separated)
    values = start_here[...].T.astype(BF16)
    product[...] = jnp.dot(values, separated[...], preferred_element_type=F32)
    adjoint_blocks(product, shifts, keep, give)


def add_kernel(keep, arrived, *outs):
    for index, out in enumerate(outs):
        out[...] = (keep[index].astype(F32) + arrived[index].astype(F32)).astype(BF16)


def pack_kernel(shifts, *refs):
    sent, arrived, packed = refs[0], refs[1:-1], refs[-1]
    _, core = place()
    for index, block in enumerate(arrived):
        values = block[...]
        for side in range(2):
            if shifts[side][index] == 0:
                values = jnp.where(core == side, sent[...], values)
        packed[index] = values


def rows_kernel(ranks, factors, observed, separated, turned, wide):
    chip, _ = place()
    tiles = separated.shape[1] // LANES
    lane = lax.broadcasted_iota(jnp.int32, (1, LANES), 1) % (LANES // 2)
    separate(factors, wide, separated, [lane < ranks[0, chip, tile] for tile in range(tiles)])
    turned[...] = observed[...].T


def columns_kernel(factors, separated, wide):
    separate(factors, wide, separated)


def image_kernel(shifts, own, mate, factors, observed, keep, give, left, product):
    spread_blocks(own, mate, shifts, left)
    misfit = times_transposed(left[...], factors[...]) - observed[...]
    product[...] = jnp.dot(misfit.astype(BF16), factors[...], preferred_element_type=F32)
    adjoint_blocks(product, shifts, keep, give)


def gradient_kernel(shifts, own, mate, factors, gradient, left):
    spread_blocks(own, mate, shifts, left)
    gradient[...] = times_transposed(left[...], factors[...]).astype(BF16)


def thin_out(values):
    return values - jnp.clip(values, -LEVEL, LEVEL)


def shrink_kernel(band, *refs):
    tables, starts, gradients, out = refs[: -2 * band - 1], refs[-2 * band - 1 : -band - 1], refs[-band - 1 : -1], refs[-1]
    estimates = [
        start[...] - STEP_SIZE * gradient[...].astype(F32).T for start, gradient in zip(starts, gradients)
    ]
    scale = 1.0 / math.sqrt(band)
    if band == 2:
        here, there = estimates
        out[...] = (thin_out((here + there) * scale) + thin_out((here - there) * scale)) * scale
        return
    (tables,) = tables
    half = out.shape[1] // 2
    lane = lax.broadcasted_iota(jnp.int32, (1, out.shape[1]), 1)
    turn = jnp.where(lane < half, -1.0, 1.0).astype(F32)
    turned = [pltpu.roll(estimate, half, 1) * turn for estimate in estimates]
    total = jnp.zeros_like(estimates[0])
    for time in range(band):
        sample = jnp.zeros_like(estimates[0])
        for index in range(band):
            sample += tables[0, index, time] * estimates[index] + tables[1, index, time] * turned[index]
        thinned = thin_out(sample * scale)
        total += tables[0, 0, time] * thinned - tables[1, 0, time] * (pltpu.roll(thinned, half, 1) * turn)
    out[...] = total * scale


def call(kernel, name, outs, inputs, scratch=(), flops=0, spaces=(), limit=VMEM_LIMIT):
    spaces = (*spaces, *[pltpu.VMEM] * (len(inputs) - len(spaces)))
    moved = sum(x.size * x.dtype.itemsize for x in [*inputs, *outs])
    return pl.pallas_call(
        kernel,
        out_shape=outs,
        in_specs=[pl.BlockSpec(memory_space=space) for space in spaces],
        out_specs=[pl.BlockSpec(memory_space=pltpu.VMEM)] * len(outs),
        scratch_shapes=scratch,
        compiler_params=pltpu.CompilerParams(vmem_limit_bytes=limit),
        cost_estimate=pl.CostEstimate(flops=flops, bytes_accessed=moved, transcendentals=0),
        name=name,
    )(*inputs)


def to_mate(value):
    return lax.ppermute(value, "tile", [(i, i ^ 1) for i in range(lax.axis_size("tile"))])


def after(value, *others):
    return lax.optimization_barrier((value, *others))[0]


def exchange(keep, give, shifts, beside):
    count = lax.axis_size("tile")
    members = len(shifts[0])
    block = jax.ShapeDtypeStruct(keep.shape[1:], keep.dtype)
    sends = call(add_kernel, "add", [block] * members, [keep, to_mate(give)])
    arrived = []
    for index, send in enumerate(sends):
        partners = [(i, i ^ 2 * shifts[i % 2][index]) for i in range(count)]
        arrived.append(lax.ppermute(send, "tile", [pair for pair in partners if pair[0] != pair[1]]))
    (own_index,) = [index for index in range(members) if 0 in (shifts[0][index], shifts[1][index])]
    arrived[0] = after(arrived[0], *beside)
    (own,) = call(functools.partial(pack_kernel, shifts), "pack", [keep], [sends[own_index], *arrived])
    return own, to_mate(own)


def body(u_factors, v_factors, ranks, observed, start):
    band = lax.axis_size("freq")
    rows, tiles, width = u_factors.shape[1:]
    sources = start.shape[2]
    columns = tiles * width
    left_rows = u_factors.reshape(rows * tiles, width)
    right_rows = v_factors.reshape(rows * tiles, width)
    observed = observed.reshape(rows, sources)
    start = start.reshape(rows, sources)
    shifts = shifts_of(tiles)

    def shape(*dims, dtype=BF16):
        return jax.ShapeDtypeStruct(dims, dtype)

    wide = pltpu.VMEM((rows * tiles, width), F32)
    factor = shape(rows, columns)
    blocks = shape(tiles // 2, sources // 2, width)
    product = pltpu.VMEM((sources, columns), F32)
    spread = pltpu.VMEM((sources, columns), BF16)
    spread_rows = pltpu.VMEM((rows, columns), BF16)
    flops = 2 * rows * columns * sources

    keep, give = call(
        functools.partial(forward_kernel, shifts),
        "forward",
        [blocks, blocks],
        [start, right_rows],
        [
            pltpu.VMEM(start.shape, F32),
            pltpu.VMEM(right_rows.shape, BF16),
            wide,
            spread_rows,
            product,
            pltpu.SemaphoreType.DMA((2,)),
        ],
        flops,
        [pltpu.HBM] * 2,
        FIRST_LIMIT,
    )
    left, turned = call(
        rows_kernel,
        "rows",
        [factor, shape(sources, rows, dtype=F32)],
        [ranks, after(left_rows, give), after(observed, give)],
        [wide],
        spaces=[pltpu.SMEM],
    )
    own, mate = exchange(keep, give, shifts, [left, turned])
    early = after(start, own)
    starts = [start]
    for shift in range(1, band):
        starts.append(lax.ppermute(early, "freq", [(f, (f - shift) % band) for f in range(band)]))
    keep, give = call(
        functools.partial(image_kernel, shifts),
        "image",
        [blocks, blocks],
        [own, mate, left, turned],
        [spread, product],
        2 * flops,
    )
    (right,) = call(columns_kernel, "columns", [factor], [after(right_rows, give)], [wide])
    own, mate = exchange(keep, give, shifts, [right])
    (gradient,) = call(
        functools.partial(gradient_kernel, shifts), "gradient", [shape(sources, rows)], [own, mate, right], [spread], flops
    )
    gradients = [gradient]
    for shift in range(1, band):
        gradients.append(lax.ppermute(gradient, "freq", [(f, (f - shift) % band) for f in range(band)]))
    inputs, spaces = [*starts, *gradients], []
    if band > 2:
        bands = jnp.arange(band, dtype=jnp.int32)
        phases = (bands[:, None] + lax.axis_index("freq")) * bands[None, :] % band
        phases = (2.0 * math.pi / band) * phases.astype(F32)
        inputs, spaces = [jnp.stack([jnp.cos(phases), jnp.sin(phases)]), *inputs], [pltpu.SMEM]
    (estimate,) = call(
        functools.partial(shrink_kernel, band), "shrink", [shape(rows, sources, dtype=F32)], inputs, spaces=spaces
    )
    return estimate[None]


def solution(mesh):
    in_specs = (
        P("freq", "tile", None, None),
        P("freq", "tile", None, None),
        P("freq", None, None),
        P("freq", "tile", None),
        P("freq", "tile", None),
    )
    out_specs = P("freq", "tile", None)
    return jax.shard_map(body, mesh=mesh, in_specs=in_specs, out_specs=out_specs, check_vma=False)
```

```python
import functools
import math

import jax
import jax.numpy as jnp
from jax import lax
from jax.experimental import pallas as pl
from jax.experimental.pallas import tpu as pltpu
from jax.sharding import PartitionSpec as P

STEP_SIZE = 0.2
LEVEL = 0.5
LANES = 128
VMEM_LIMIT = 32 * 1024 * 1024
FIRST_LIMIT = 55050 * 1024
PIECES = 4
F32 = jnp.float32
BF16 = jnp.bfloat16


def shifts_of(chips):
    far_first = sorted(range(chips), key=lambda shift: (-shift.bit_count(), -shift))
    return [[far_first[at] for at in range(chips) if (at + 1) // 2 % 2 == core] for core in range(2)]


def place():
    position = lax.axis_index("tile")
    return position // 2, position % 2


def columns_of(tile):
    return pl.ds(pl.multiple_of(tile * LANES, LANES), LANES)


def both_shifts(shifts):
    chip, core = place()
    pairs = list(zip(*shifts))
    own = [chip ^ jnp.where(core == 0, first, second) for first, second in pairs]
    mate = [chip ^ jnp.where(core == 0, second, first) for first, second in pairs]
    return own, mate


def signs(rows):
    lane = lax.broadcasted_iota(jnp.int32, (rows, LANES), 1)
    return jnp.where(lane < LANES // 2, 1.0, -1.0).astype(F32)


def separate(source, wide, target, chosen, masks=None):
    rows = target.shape[0]
    tiles = source.shape[0] // rows
    wide[...] = source[...].astype(F32)
    for index, tile in enumerate(chosen):
        part = wide[pl.ds(tile, rows, stride=tiles), :]
        if masks is not None:
            part = jnp.where(masks[index], part, 0.0)
        target[:, index * LANES : (index + 1) * LANES] = part.astype(BF16)


def adjoint_block(product, tile):
    half = product.shape[0] // 2
    real, imaginary = product[:half, columns_of(tile)], product[half:, columns_of(tile)]
    return (real * signs(half) + pltpu.roll(imaginary, LANES // 2, 1)).astype(BF16)


def spread_block(block, left, tile):
    half = block.shape[0]
    block = block.astype(F32)
    left[:half, columns_of(tile)] = (block * signs(half)).astype(BF16)
    left[half:, columns_of(tile)] = pltpu.roll(block, LANES // 2, 1).astype(BF16)


def arrived_block(shifts, index, sent, arrived):
    _, core = place()
    values = arrived[...]
    for side in range(2):
        if shifts[side][index] == 0:
            values = jnp.where(core == side, sent[...], values)
    return values


def times_transposed(left, right):
    return lax.dot_general(left, right, (((1,), (1,)), ((), ())), preferred_element_type=F32)


def forward_kernel(shifts, start, factors, keep, give, start_here, factors_here, wide, separated, product, sems):
    pieces = sems.shape[0] - 1
    rows, columns = separated.shape
    tiles = columns // LANES
    load_start = pltpu.make_async_copy(start, start_here, sems.at[pieces])
    load_start.start()
    loads = []
    for piece in range(pieces):
        at = pl.ds(piece * (rows * tiles // pieces), rows * tiles // pieces)
        loads.append(pltpu.make_async_copy(factors.at[at], factors_here.at[at], sems.at[piece]))
        loads[-1].start()
    load_start.wait()
    values = start_here[...].T.astype(BF16)
    for piece, load in enumerate(loads):
        at = pl.ds(piece * (rows * tiles // pieces), rows * tiles // pieces)
        load.wait()
        separate(
            factors_here.at[at], wide.at[at], separated.at[pl.ds(piece * (rows // pieces), rows // pieces)], range(tiles)
        )
    product[...] = jnp.dot(values, separated[...], preferred_element_type=F32)
    for out, chosen in zip((keep, give), both_shifts(shifts)):
        for index, tile in enumerate(chosen):
            out[index] = adjoint_block(product, tile)


def add_kernel(keep, arrived, *outs):
    for index, out in enumerate(outs):
        out[...] = (keep[index].astype(F32) + arrived[index].astype(F32)).astype(BF16)


def rows_kernel(shifts, ranks, own, mate, observed, own_out, mate_out, turned, wide):
    chip, _ = place()
    chosen, _ = both_shifts(shifts)
    lane = lax.broadcasted_iota(jnp.int32, (1, LANES), 1) % (LANES // 2)
    masks = [lane < ranks[0, chip, tile] for tile in chosen]
    separate(own, wide, own_out, chosen, masks)
    separate(mate, wide, mate_out, chosen, masks)
    turned[...] = observed[...].T


def columns_kernel(factors, separated, wide):
    separate(factors, wide, separated, range(separated.shape[1] // LANES))


def image_kernel(shifts, sent, *refs):
    arrived, (own, mate, observed, misfit, left) = refs[:-5], refs[-5:]
    for index, block in enumerate(arrived):
        spread_block(arrived_block(shifts, index, sent, block), left, index)
    misfit[0] = times_transposed(left[...], own[...]) - observed[...]
    misfit[1] = times_transposed(left[...], mate[...])


def back_kernel(here, there, own, mate, *refs):
    outs, products = refs[:-1], refs[-1]
    for rows, factors in ((0, own), (1, mate)):
        misfit = (here[rows] + there[1 - rows]).astype(BF16)
        products[rows] = jnp.dot(misfit, factors[...], preferred_element_type=F32)
    for index, out in enumerate(outs):
        parts = [adjoint_block(products.at[rows], index).astype(F32) for rows in range(2)]
        out[...] = (parts[0] + parts[1]).astype(BF16)


def pack_kernel(shifts, sent, *refs):
    arrived, packed = refs[:-1], refs[-1]
    for index, block in enumerate(arrived):
        packed[index] = arrived_block(shifts, index, sent, block)


def gradient_kernel(shifts, own, mate, factors, gradient, left):
    for blocks, chosen in zip((own, mate), both_shifts(shifts)):
        for index, tile in enumerate(chosen):
            spread_block(blocks[index], left, tile)
    gradient[...] = times_transposed(left[...], factors[...]).astype(BF16)


def thin_out(values):
    return values - jnp.clip(values, -LEVEL, LEVEL)


def shrink_kernel(band, *refs):
    tables, starts, gradients, out = refs[: -2 * band - 1], refs[-2 * band - 1 : -band - 1], refs[-band - 1 : -1], refs[-1]
    estimates = [
        start[...] - STEP_SIZE * gradient[...].astype(F32).T for start, gradient in zip(starts, gradients)
    ]
    scale = 1.0 / math.sqrt(band)
    if band == 2:
        here, there = estimates
        out[...] = (thin_out((here + there) * scale) + thin_out((here - there) * scale)) * scale
        return
    (tables,) = tables
    half = out.shape[1] // 2
    lane = lax.broadcasted_iota(jnp.int32, (1, out.shape[1]), 1)
    turn = jnp.where(lane < half, -1.0, 1.0).astype(F32)
    turned = [pltpu.roll(estimate, half, 1) * turn for estimate in estimates]
    total = jnp.zeros_like(estimates[0])
    for time in range(band):
        sample = jnp.zeros_like(estimates[0])
        for index in range(band):
            sample += tables[0, index, time] * estimates[index] + tables[1, index, time] * turned[index]
        thinned = thin_out(sample * scale)
        total += tables[0, 0, time] * thinned - tables[1, 0, time] * (pltpu.roll(thinned, half, 1) * turn)
    out[...] = total * scale


def call(kernel, name, outs, inputs, scratch=(), flops=0, spaces=(), limit=VMEM_LIMIT):
    spaces = (*spaces, *[pltpu.VMEM] * (len(inputs) - len(spaces)))
    moved = sum(x.size * x.dtype.itemsize for x in [*inputs, *outs])
    return pl.pallas_call(
        kernel,
        out_shape=outs,
        in_specs=[pl.BlockSpec(memory_space=space) for space in spaces],
        out_specs=[pl.BlockSpec(memory_space=pltpu.VMEM)] * len(outs),
        scratch_shapes=scratch,
        compiler_params=pltpu.CompilerParams(vmem_limit_bytes=limit),
        cost_estimate=pl.CostEstimate(flops=flops, bytes_accessed=moved, transcendentals=0),
        name=name,
    )(*inputs)


def to_mate(value):
    return lax.ppermute(value, "tile", [(i, i ^ 1) for i in range(lax.axis_size("tile"))])


def after(value, *others):
    return lax.optimization_barrier((value, *others))[0]


def exchange(sends, shifts, beside):
    count = lax.axis_size("tile")
    arrived = []
    for index, send in enumerate(sends):
        partners = [(i, i ^ 2 * shifts[i % 2][index]) for i in range(count)]
        arrived.append(lax.ppermute(send, "tile", [pair for pair in partners if pair[0] != pair[1]]))
    arrived[0] = after(arrived[0], *beside)
    (own,) = [send for index, send in enumerate(sends) if 0 in (shifts[0][index], shifts[1][index])]
    return [own, *arrived]


def body(u_factors, v_factors, ranks, observed, start):
    band = lax.axis_size("freq")
    rows, tiles, width = u_factors.shape[1:]
    sources = start.shape[2]
    columns = tiles * width
    left_rows = u_factors.reshape(rows * tiles, width)
    right_rows = v_factors.reshape(rows * tiles, width)
    observed = observed.reshape(rows, sources)
    start = start.reshape(rows, sources)
    shifts = shifts_of(tiles)

    def shape(*dims, dtype=BF16):
        return jax.ShapeDtypeStruct(dims, dtype)

    members = tiles // 2
    wide = pltpu.VMEM((rows * tiles, width), F32)
    block = shape(sources // 2, width)
    blocks = shape(members, sources // 2, width)
    chosen = shape(rows, members * width)
    spread = pltpu.VMEM((sources, columns), BF16)
    flops = 2 * rows * columns * sources

    keep, give = call(
        functools.partial(forward_kernel, shifts),
        "forward",
        [blocks, blocks],
        [start, right_rows],
        [
            pltpu.VMEM(start.shape, F32),
            pltpu.VMEM(right_rows.shape, BF16),
            wide,
            pltpu.VMEM((rows, columns), BF16),
            pltpu.VMEM((sources, columns), F32),
            pltpu.SemaphoreType.DMA((PIECES + 1,)),
        ],
        flops,
        [pltpu.HBM] * 2,
        FIRST_LIMIT,
    )
    sends = call(add_kernel, "add", [block] * members, [keep, to_mate(give)])
    left_rows = after(left_rows, sends[0])
    own_left, mate_left, turned = call(
        functools.partial(rows_kernel, shifts),
        "rows",
        [chosen, chosen, shape(sources, rows, dtype=F32)],
        [ranks, left_rows, to_mate(left_rows), after(observed, give)],
        [wide],
        spaces=[pltpu.SMEM],
    )
    early = after(start, own_left)
    starts = [start]
    for shift in range(1, band):
        starts.append(lax.ppermute(early, "freq", [(f, (f - shift) % band) for f in range(band)]))
    (misfit,) = call(
        functools.partial(image_kernel, shifts),
        "image",
        [shape(2, sources, rows, dtype=F32)],
        [*exchange(sends, shifts, [own_left, mate_left, turned]), own_left, mate_left, turned],
        [pltpu.VMEM((sources, members * width), BF16)],
        flops,
    )
    sends = call(
        back_kernel,
        "back",
        [block] * members,
        [misfit, to_mate(misfit), own_left, mate_left],
        [pltpu.VMEM((2, sources, members * width), F32)],
        flops,
    )
    (right,) = call(columns_kernel, "columns", [shape(rows, columns)], [after(right_rows, sends[0])], [wide])
    (own,) = call(functools.partial(pack_kernel, shifts), "pack", [blocks], exchange(sends, shifts, [right, *starts[1:]]))
    (gradient,) = call(
        functools.partial(gradient_kernel, shifts),
        "gradient",
        [shape(sources, rows)],
        [own, to_mate(own), right],
        [spread],
        flops,
    )
    gradients = [gradient]
    for shift in range(1, band):
        gradients.append(lax.ppermute(gradient, "freq", [(f, (f - shift) % band) for f in range(band)]))
    inputs, spaces = [*starts, *gradients], []
    if band > 2:
        bands = jnp.arange(band, dtype=jnp.int32)
        phases = (bands[:, None] + lax.axis_index("freq")) * bands[None, :] % band
        phases = (2.0 * math.pi / band) * phases.astype(F32)
        inputs, spaces = [jnp.stack([jnp.cos(phases), jnp.sin(phases)]), *inputs], [pltpu.SMEM]
    (estimate,) = call(
        functools.partial(shrink_kernel, band), "shrink", [shape(rows, sources, dtype=F32)], inputs, spaces=spaces
    )
    return estimate[None]


def solution(mesh):
    in_specs = (
        P("freq", "tile", None, None),
        P("freq", "tile", None, None),
        P("freq", None, None),
        P("freq", "tile", None),
        P("freq", "tile", None),
    )
    out_specs = P("freq", "tile", None)
    return jax.shard_map(body, mesh=mesh, in_specs=in_specs, out_specs=out_specs, check_vma=False)
```

```python
import functools
import math

import jax
import jax.numpy as jnp
from jax import lax
from jax.experimental import pallas as pl
from jax.experimental.pallas import tpu as pltpu
from jax.sharding import PartitionSpec as P

STEP_SIZE = 0.2
LEVEL = 0.5
LANES = 128
VMEM_LIMIT = 32 * 1024 * 1024
FIRST_LIMIT = 55050 * 1024
PIECES = 4
F32 = jnp.float32
BF16 = jnp.bfloat16


def shifts_of(chips):
    far_first = sorted(range(chips), key=lambda shift: (-shift.bit_count(), -shift))
    return [[far_first[at] for at in range(chips) if (at + 1) // 2 % 2 == core] for core in range(2)]


def place():
    position = lax.axis_index("tile")
    return position // 2, position % 2


def columns_of(tile):
    return pl.ds(pl.multiple_of(tile * LANES, LANES), LANES)


def both_shifts(shifts):
    chip, core = place()
    pairs = list(zip(*shifts))
    own = [chip ^ jnp.where(core == 0, first, second) for first, second in pairs]
    mate = [chip ^ jnp.where(core == 0, second, first) for first, second in pairs]
    return own, mate


def signs(rows):
    lane = lax.broadcasted_iota(jnp.int32, (rows, LANES), 1)
    return jnp.where(lane < LANES // 2, 1.0, -1.0).astype(F32)


def separate(source, wide, target, chosen, masks=None):
    rows = target.shape[0]
    tiles = source.shape[0] // rows
    wide[...] = source[...].astype(F32)
    for index, tile in enumerate(chosen):
        part = wide[pl.ds(tile, rows, stride=tiles), :]
        if masks is not None:
            part = jnp.where(masks[index], part, 0.0)
        target[:, index * LANES : (index + 1) * LANES] = part.astype(BF16)


def adjoint_block(product, tile):
    half = product.shape[0] // 2
    real, imaginary = product[:half, columns_of(tile)], product[half:, columns_of(tile)]
    return (real * signs(half) + pltpu.roll(imaginary, LANES // 2, 1)).astype(BF16)


def spread_block(block, left, tile):
    half = block.shape[0]
    block = block.astype(F32)
    left[:half, columns_of(tile)] = (block * signs(half)).astype(BF16)
    left[half:, columns_of(tile)] = pltpu.roll(block, LANES // 2, 1).astype(BF16)


def times_transposed(left, right):
    return lax.dot_general(left, right, (((1,), (1,)), ((), ())), preferred_element_type=F32)


def forward_kernel(shifts, start, factors, keep, give, start_here, factors_here, wide, separated, product, sems):
    pieces = sems.shape[0] - 1
    rows, columns = separated.shape
    tiles = columns // LANES
    load_start = pltpu.make_async_copy(start, start_here, sems.at[pieces])
    load_start.start()
    loads = []
    for piece in range(pieces):
        at = pl.ds(piece * (rows * tiles // pieces), rows * tiles // pieces)
        loads.append(pltpu.make_async_copy(factors.at[at], factors_here.at[at], sems.at[piece]))
        loads[-1].start()
    load_start.wait()
    values = start_here[...].T.astype(BF16)
    for piece, load in enumerate(loads):
        at = pl.ds(piece * (rows * tiles // pieces), rows * tiles // pieces)
        load.wait()
        separate(
            factors_here.at[at], wide.at[at], separated.at[pl.ds(piece * (rows // pieces), rows // pieces)], range(tiles)
        )
    product[...] = jnp.dot(values, separated[...], preferred_element_type=F32)
    for out, chosen in zip((keep, give), both_shifts(shifts)):
        for index, tile in enumerate(chosen):
            out[index] = adjoint_block(product, tile)


def add_kernel(keep, arrived, *outs):
    for index, out in enumerate(outs):
        out[...] = (keep[index].astype(F32) + arrived[index].astype(F32)).astype(BF16)


def rows_kernel(shifts, ranks, own, mate, observed, own_out, mate_out, turned, wide):
    chip, _ = place()
    chosen, _ = both_shifts(shifts)
    lane = lax.broadcasted_iota(jnp.int32, (1, LANES), 1) % (LANES // 2)
    masks = [lane < ranks[0, chip, tile] for tile in chosen]
    separate(own, wide, own_out, chosen, masks)
    separate(mate, wide, mate_out, chosen, masks)
    turned[...] = observed[...].T


def columns_kernel(factors, separated, wide):
    separate(factors, wide, separated, range(separated.shape[1] // LANES))


def image_kernel(*refs):
    arrived, (own, mate, observed, misfit, left) = refs[:-5], refs[-5:]
    for index, block in enumerate(arrived):
        spread_block(block[...], left, index)
    misfit[0] = times_transposed(left[...], own[...]) - observed[...]
    misfit[1] = times_transposed(left[...], mate[...])


def back_kernel(here, there, own, mate, *refs):
    outs, products = refs[:-1], refs[-1]
    for rows, factors in ((0, own), (1, mate)):
        misfit = (here[rows] + there[1 - rows]).astype(BF16)
        products[rows] = jnp.dot(misfit, factors[...], preferred_element_type=F32)
    for index, out in enumerate(outs):
        parts = [adjoint_block(products.at[rows], index).astype(F32) for rows in range(2)]
        out[...] = (parts[0] + parts[1]).astype(BF16)


def pack_kernel(*refs):
    for index, block in enumerate(refs[:-1]):
        refs[-1][index] = block[...]


def gradient_kernel(shifts, own, mate, factors, gradient, left):
    for blocks, chosen in zip((own, mate), both_shifts(shifts)):
        for index, tile in enumerate(chosen):
            spread_block(blocks[index], left, tile)
    gradient[...] = times_transposed(left[...], factors[...]).astype(BF16)


def thin_out(values):
    return values - jnp.clip(values, -LEVEL, LEVEL)


def shrink_kernel(band, *refs):
    tables, starts, gradients, out = refs[: -2 * band - 1], refs[-2 * band - 1 : -band - 1], refs[-band - 1 : -1], refs[-1]
    estimates = [
        start[...] - STEP_SIZE * gradient[...].astype(F32).T for start, gradient in zip(starts, gradients)
    ]
    scale = 1.0 / math.sqrt(band)
    if band == 2:
        here, there = estimates
        out[...] = (thin_out((here + there) * scale) + thin_out((here - there) * scale)) * scale
        return
    (tables,) = tables
    half = out.shape[1] // 2
    lane = lax.broadcasted_iota(jnp.int32, (1, out.shape[1]), 1)
    turn = jnp.where(lane < half, -1.0, 1.0).astype(F32)
    turned = [pltpu.roll(estimate, half, 1) * turn for estimate in estimates]
    total = jnp.zeros_like(estimates[0])
    for time in range(band):
        sample = jnp.zeros_like(estimates[0])
        for index in range(band):
            sample += tables[0, index, time] * estimates[index] + tables[1, index, time] * turned[index]
        thinned = thin_out(sample * scale)
        total += tables[0, 0, time] * thinned - tables[1, 0, time] * (pltpu.roll(thinned, half, 1) * turn)
    out[...] = total * scale


def call(kernel, name, outs, inputs, scratch=(), flops=0, spaces=(), limit=VMEM_LIMIT):
    spaces = (*spaces, *[pltpu.VMEM] * (len(inputs) - len(spaces)))
    moved = sum(x.size * x.dtype.itemsize for x in [*inputs, *outs])
    return pl.pallas_call(
        kernel,
        out_shape=outs,
        in_specs=[pl.BlockSpec(memory_space=space) for space in spaces],
        out_specs=[pl.BlockSpec(memory_space=pltpu.VMEM)] * len(outs),
        scratch_shapes=scratch,
        compiler_params=pltpu.CompilerParams(vmem_limit_bytes=limit),
        cost_estimate=pl.CostEstimate(flops=flops, bytes_accessed=moved, transcendentals=0),
        name=name,
    )(*inputs)


def to_mate(value):
    return lax.ppermute(value, "tile", [(i, i ^ 1) for i in range(lax.axis_size("tile"))])


def after(value, *others):
    return lax.optimization_barrier((value, *others))[0]


def exchange(sends, shifts, beside):
    count = lax.axis_size("tile")
    arrived = []
    for index, send in enumerate(sends):
        arrived.append(lax.ppermute(send, "tile", [(i, i ^ 2 * shifts[i % 2][index]) for i in range(count)]))
    return [after(arrived[0], *beside), *arrived[1:]]


def body(u_factors, v_factors, ranks, observed, start):
    band = lax.axis_size("freq")
    rows, tiles, width = u_factors.shape[1:]
    sources = start.shape[2]
    columns = tiles * width
    left_rows = u_factors.reshape(rows * tiles, width)
    right_rows = v_factors.reshape(rows * tiles, width)
    observed = observed.reshape(rows, sources)
    start = start.reshape(rows, sources)
    shifts = shifts_of(tiles)

    def shape(*dims, dtype=BF16):
        return jax.ShapeDtypeStruct(dims, dtype)

    members = tiles // 2
    wide = pltpu.VMEM((rows * tiles, width), F32)
    block = shape(sources // 2, width)
    blocks = shape(members, sources // 2, width)
    chosen = shape(rows, members * width)
    spread = pltpu.VMEM((sources, columns), BF16)
    flops = 2 * rows * columns * sources

    keep, give = call(
        functools.partial(forward_kernel, shifts),
        "forward",
        [blocks, blocks],
        [start, right_rows],
        [
            pltpu.VMEM(start.shape, F32),
            pltpu.VMEM(right_rows.shape, BF16),
            wide,
            pltpu.VMEM((rows, columns), BF16),
            pltpu.VMEM((sources, columns), F32),
            pltpu.SemaphoreType.DMA((PIECES + 1,)),
        ],
        flops,
        [pltpu.HBM] * 2,
        FIRST_LIMIT,
    )
    sends = call(add_kernel, "add", [block] * members, [keep, to_mate(give)])
    left_rows = after(left_rows, sends[0])
    own_left, mate_left, turned = call(
        functools.partial(rows_kernel, shifts),
        "rows",
        [chosen, chosen, shape(sources, rows, dtype=F32)],
        [ranks, left_rows, to_mate(left_rows), after(observed, give)],
        [wide],
        spaces=[pltpu.SMEM],
    )
    early = after(start, own_left)
    starts = [start]
    for shift in range(1, band):
        starts.append(lax.ppermute(early, "freq", [(f, (f - shift) % band) for f in range(band)]))
    (misfit,) = call(
        image_kernel,
        "image",
        [shape(2, sources, rows, dtype=F32)],
        [*exchange(sends, shifts, [own_left, mate_left, turned]), own_left, mate_left, turned],
        [pltpu.VMEM((sources, members * width), BF16)],
        flops,
    )
    sends = call(
        back_kernel,
        "back",
        [block] * members,
        [misfit, to_mate(misfit), own_left, mate_left],
        [pltpu.VMEM((2, sources, members * width), F32)],
        flops,
    )
    (right,) = call(columns_kernel, "columns", [shape(rows, columns)], [after(right_rows, sends[0])], [wide])
    (own,) = call(pack_kernel, "pack", [blocks], exchange(sends, shifts, [right, *starts[1:]]))
    (gradient,) = call(
        functools.partial(gradient_kernel, shifts),
        "gradient",
        [shape(sources, rows)],
        [own, to_mate(own), right],
        [spread],
        flops,
    )
    gradients = [gradient]
    for shift in range(1, band):
        gradients.append(lax.ppermute(gradient, "freq", [(f, (f - shift) % band) for f in range(band)]))
    inputs, spaces = [*starts, *gradients], []
    if band > 2:
        bands = jnp.arange(band, dtype=jnp.int32)
        phases = (bands[:, None] + lax.axis_index("freq")) * bands[None, :] % band
        phases = (2.0 * math.pi / band) * phases.astype(F32)
        inputs, spaces = [jnp.stack([jnp.cos(phases), jnp.sin(phases)]), *inputs], [pltpu.SMEM]
    (estimate,) = call(
        functools.partial(shrink_kernel, band), "shrink", [shape(rows, sources, dtype=F32)], inputs, spaces=spaces
    )
    return estimate[None]


def solution(mesh):
    in_specs = (
        P("freq", "tile", None, None),
        P("freq", "tile", None, None),
        P("freq", None, None),
        P("freq", "tile", None),
        P("freq", "tile", None),
    )
    out_specs = P("freq", "tile", None)
    return jax.shard_map(body, mesh=mesh, in_specs=in_specs, out_specs=out_specs, check_vma=False)
```

```python
import functools
import math

import jax
import jax.numpy as jnp
from jax import lax
from jax.experimental import pallas as pl
from jax.experimental.pallas import tpu as pltpu
from jax.sharding import PartitionSpec as P

STEP_SIZE = 0.2
LEVEL = 0.5
LANES = 128
VMEM_LIMIT = 32 * 1024 * 1024
FIRST_LIMIT = 55050 * 1024
PIECES = 4
F32 = jnp.float32
BF16 = jnp.bfloat16


def shifts_of(chips):
    far_first = sorted(range(chips), key=lambda shift: (-shift.bit_count(), -shift))
    return [[far_first[at] for at in range(chips) if (at + 1) // 2 % 2 == core] for core in range(2)]


def place():
    position = lax.axis_index("tile")
    return position // 2, position % 2


def columns_of(tile):
    return pl.ds(pl.multiple_of(tile * LANES, LANES), LANES)


def both_shifts(shifts):
    chip, core = place()
    pairs = list(zip(*shifts))
    own = [chip ^ jnp.where(core == 0, first, second) for first, second in pairs]
    mate = [chip ^ jnp.where(core == 0, second, first) for first, second in pairs]
    return own, mate


def signs(rows):
    lane = lax.broadcasted_iota(jnp.int32, (rows, LANES), 1)
    return jnp.where(lane < LANES // 2, 1.0, -1.0).astype(F32)


def separate(source, wide, target, chosen, masks=None):
    rows = target.shape[0]
    tiles = source.shape[0] // rows
    wide[...] = source[...].astype(F32)
    for index, tile in enumerate(chosen):
        part = wide[pl.ds(tile, rows, stride=tiles), :]
        if masks is not None:
            part = jnp.where(masks[index], part, 0.0)
        target[:, index * LANES : (index + 1) * LANES] = part.astype(BF16)


def adjoint_block(product, tile):
    half = product.shape[0] // 2
    real, imaginary = product[:half, columns_of(tile)], product[half:, columns_of(tile)]
    return (real * signs(half) + pltpu.roll(imaginary, LANES // 2, 1)).astype(BF16)


def spread_block(block, left, tile):
    half = block.shape[0]
    block = block.astype(F32)
    left[:half, columns_of(tile)] = (block * signs(half)).astype(BF16)
    left[half:, columns_of(tile)] = pltpu.roll(block, LANES // 2, 1).astype(BF16)


def arrived_block(shifts, index, sent, arrived):
    _, core = place()
    values = arrived[...]
    for side in range(2):
        if shifts[side][index] == 0:
            values = jnp.where(core == side, sent[...], values)
    return values


def times_transposed(left, right):
    return lax.dot_general(left, right, (((1,), (1,)), ((), ())), preferred_element_type=F32)


def forward_kernel(shifts, start, factors, keep, give, start_here, factors_here, wide, separated, product, sems):
    pieces = sems.shape[0] - 1
    rows, columns = separated.shape
    tiles = columns // LANES
    load_start = pltpu.make_async_copy(start, start_here, sems.at[pieces])
    load_start.start()
    loads = []
    for piece in range(pieces):
        at = pl.ds(piece * (rows * tiles // pieces), rows * tiles // pieces)
        loads.append(pltpu.make_async_copy(factors.at[at], factors_here.at[at], sems.at[piece]))
        loads[-1].start()
    load_start.wait()
    values = start_here[...].T.astype(BF16)
    for piece, load in enumerate(loads):
        at = pl.ds(piece * (rows * tiles // pieces), rows * tiles // pieces)
        load.wait()
        separate(
            factors_here.at[at], wide.at[at], separated.at[pl.ds(piece * (rows // pieces), rows // pieces)], range(tiles)
        )
    product[...] = jnp.dot(values, separated[...], preferred_element_type=F32)
    for out, chosen in zip((keep, give), both_shifts(shifts)):
        for index, tile in enumerate(chosen):
            out[index] = adjoint_block(product, tile)


def add_kernel(keep, arrived, *outs):
    for index, out in enumerate(outs):
        out[...] = (keep[index].astype(F32) + arrived[index].astype(F32)).astype(BF16)


def rows_kernel(shifts, ranks, own, mate, observed, own_out, mate_out, turned, wide):
    chip, _ = place()
    chosen, _ = both_shifts(shifts)
    lane = lax.broadcasted_iota(jnp.int32, (1, LANES), 1) % (LANES // 2)
    masks = [lane < ranks[0, chip, tile] for tile in chosen]
    separate(own, wide, own_out, chosen, masks)
    separate(mate, wide, mate_out, chosen, masks)
    turned[...] = observed[...].T


def columns_kernel(factors, separated, wide):
    separate(factors, wide, separated, range(separated.shape[1] // LANES))


def image_kernel(shifts, sent, *refs):
    arrived, (own, mate, observed, misfit, left) = refs[:-5], refs[-5:]
    for index, block in enumerate(arrived):
        spread_block(arrived_block(shifts, index, sent, block), left, index)
    misfit[0] = times_transposed(left[...], own[...]) - observed[...]
    misfit[1] = times_transposed(left[...], mate[...])


def back_kernel(here, there, own, mate, *refs):
    outs, products = refs[:-1], refs[-1]
    for rows, factors in ((0, own), (1, mate)):
        misfit = (here[rows] + there[1 - rows]).astype(BF16)
        products[rows] = jnp.dot(misfit, factors[...], preferred_element_type=F32)
    for index, out in enumerate(outs):
        parts = [adjoint_block(products.at[rows], index).astype(F32) for rows in range(2)]
        out[...] = (parts[0] + parts[1]).astype(BF16)


def pack_kernel(shifts, sent, *refs):
    for index, block in enumerate(refs[:-1]):
        refs[-1][index] = arrived_block(shifts, index, sent, block)


def gradient_kernel(shifts, own, mate, factors, gradient, left):
    for blocks, chosen in zip((own, mate), both_shifts(shifts)):
        for index, tile in enumerate(chosen):
            spread_block(blocks[index], left, tile)
    gradient[...] = times_transposed(factors[...], left[...]).astype(BF16)


def thin_out(values):
    return values - jnp.clip(values, -LEVEL, LEVEL)


def pair_kernel(here, there, gradient, total, difference):
    scale = 1.0 / math.sqrt(2)
    estimate = here[...] - STEP_SIZE * gradient[...].astype(F32)
    total[...] = (estimate + there[...]) * scale
    difference[...] = (estimate - there[...]) * scale


def shrink_pair_kernel(total, difference, gradient, out):
    scale = 1.0 / math.sqrt(2)
    step = (STEP_SIZE * scale) * gradient[...].astype(F32)
    out[...] = (thin_out(total[...] - step) + thin_out(difference[...] + step)) * scale


def shrink_kernel(band, *refs):
    tables, starts, gradients, out = refs[: -2 * band - 1], refs[-2 * band - 1 : -band - 1], refs[-band - 1 : -1], refs[-1]
    estimates = [
        start[...] - STEP_SIZE * gradient[...].astype(F32) for start, gradient in zip(starts, gradients)
    ]
    scale = 1.0 / math.sqrt(band)
    (tables,) = tables
    half = out.shape[1] // 2
    lane = lax.broadcasted_iota(jnp.int32, (1, out.shape[1]), 1)
    turn = jnp.where(lane < half, -1.0, 1.0).astype(F32)
    turned = [pltpu.roll(estimate, half, 1) * turn for estimate in estimates]
    total = jnp.zeros_like(estimates[0])
    for time in range(band):
        sample = jnp.zeros_like(estimates[0])
        for index in range(band):
            sample += tables[0, index, time] * estimates[index] + tables[1, index, time] * turned[index]
        thinned = thin_out(sample * scale)
        total += tables[0, 0, time] * thinned - tables[1, 0, time] * (pltpu.roll(thinned, half, 1) * turn)
    out[...] = total * scale


def call(kernel, name, outs, inputs, scratch=(), flops=0, spaces=(), limit=VMEM_LIMIT):
    spaces = (*spaces, *[pltpu.VMEM] * (len(inputs) - len(spaces)))
    moved = sum(x.size * x.dtype.itemsize for x in [*inputs, *outs])
    return pl.pallas_call(
        kernel,
        out_shape=outs,
        in_specs=[pl.BlockSpec(memory_space=space) for space in spaces],
        out_specs=[pl.BlockSpec(memory_space=pltpu.VMEM)] * len(outs),
        scratch_shapes=scratch,
        compiler_params=pltpu.CompilerParams(vmem_limit_bytes=limit),
        cost_estimate=pl.CostEstimate(flops=flops, bytes_accessed=moved, transcendentals=0),
        name=name,
    )(*inputs)


def to_mate(value):
    return lax.ppermute(value, "tile", [(i, i ^ 1) for i in range(lax.axis_size("tile"))])


def after(value, *others):
    return lax.optimization_barrier((value, *others))[0]


def exchange(sends, shifts, beside):
    count = lax.axis_size("tile")
    arrived = []
    for index, send in enumerate(sends):
        pair = [shifts[core][index] or shifts[1 - core][index] for core in range(2)]
        arrived.append(lax.ppermute(send, "tile", [(i, i ^ 2 * pair[i % 2]) for i in range(count)]))
    arrived[0] = after(arrived[0], *beside)
    (own,) = [send for index, send in enumerate(sends) if 0 in (shifts[0][index], shifts[1][index])]
    return [own, *arrived]


def body(u_factors, v_factors, ranks, observed, start):
    band = lax.axis_size("freq")
    rows, tiles, width = u_factors.shape[1:]
    sources = start.shape[2]
    columns = tiles * width
    left_rows = u_factors.reshape(rows * tiles, width)
    right_rows = v_factors.reshape(rows * tiles, width)
    observed = observed.reshape(rows, sources)
    start = start.reshape(rows, sources)
    shifts = shifts_of(tiles)

    def shape(*dims, dtype=BF16):
        return jax.ShapeDtypeStruct(dims, dtype)

    members = tiles // 2
    wide = pltpu.VMEM((rows * tiles, width), F32)
    block = shape(sources // 2, width)
    blocks = shape(members, sources // 2, width)
    chosen = shape(rows, members * width)
    spread = pltpu.VMEM((sources, columns), BF16)
    flops = 2 * rows * columns * sources

    keep, give = call(
        functools.partial(forward_kernel, shifts),
        "forward",
        [blocks, blocks],
        [start, right_rows],
        [
            pltpu.VMEM(start.shape, F32),
            pltpu.VMEM(right_rows.shape, BF16),
            wide,
            pltpu.VMEM((rows, columns), BF16),
            pltpu.VMEM((sources, columns), F32),
            pltpu.SemaphoreType.DMA((PIECES + 1,)),
        ],
        flops,
        [pltpu.HBM] * 2,
        FIRST_LIMIT,
    )
    sends = call(add_kernel, "add", [block] * members, [keep, to_mate(give)])
    left_rows = after(left_rows, sends[0])
    own_left, mate_left, turned = call(
        functools.partial(rows_kernel, shifts),
        "rows",
        [chosen, chosen, shape(sources, rows, dtype=F32)],
        [ranks, left_rows, to_mate(left_rows), after(observed, give)],
        [wide],
        spaces=[pltpu.SMEM],
    )
    early = after(start, own_left)
    starts = [start]
    for shift in range(1, band):
        starts.append(lax.ppermute(early, "freq", [(f, (f - shift) % band) for f in range(band)]))
    (misfit,) = call(
        functools.partial(image_kernel, shifts),
        "image",
        [shape(2, sources, rows, dtype=F32)],
        [*exchange(sends, shifts, [own_left, mate_left, turned]), own_left, mate_left, turned],
        [pltpu.VMEM((sources, members * width), BF16)],
        flops,
    )
    sends = call(
        back_kernel,
        "back",
        [block] * members,
        [misfit, to_mate(misfit), own_left, mate_left],
        [pltpu.VMEM((2, sources, members * width), F32)],
        flops,
    )
    (right,) = call(columns_kernel, "columns", [shape(rows, columns)], [after(right_rows, sends[0])], [wide])
    (own,) = call(functools.partial(pack_kernel, shifts), "pack", [blocks], exchange(sends, shifts, [right, *starts[1:]]))
    (gradient,) = call(
        functools.partial(gradient_kernel, shifts),
        "gradient",
        [shape(rows, sources)],
        [own, to_mate(own), right],
        [spread],
        flops,
    )
    gradients = [gradient]
    for shift in range(1, band):
        gradients.append(lax.ppermute(gradient, "freq", [(f, (f - shift) % band) for f in range(band)]))
    result = shape(rows, sources, dtype=F32)
    if band == 2:
        halves = call(pair_kernel, "pair", [result] * 2, [*starts, gradient])
        (estimate,) = call(shrink_pair_kernel, "shrink", [result], [*halves, gradients[1]])
        return estimate[None]
    bands = jnp.arange(band, dtype=jnp.int32)
    phases = (bands[:, None] + lax.axis_index("freq")) * bands[None, :] % band
    phases = (2.0 * math.pi / band) * phases.astype(F32)
    tables = jnp.stack([jnp.cos(phases), jnp.sin(phases)])
    (estimate,) = call(
        functools.partial(shrink_kernel, band), "shrink", [result], [tables, *starts, *gradients], spaces=[pltpu.SMEM]
    )
    return estimate[None]


def solution(mesh):
    in_specs = (
        P("freq", "tile", None, None),
        P("freq", "tile", None, None),
        P("freq", None, None),
        P("freq", "tile", None),
        P("freq", "tile", None),
    )
    out_specs = P("freq", "tile", None)
    return jax.shard_map(body, mesh=mesh, in_specs=in_specs, out_specs=out_specs, check_vma=False)
```

```python
import functools
import math

import jax
import jax.numpy as jnp
from jax import lax
from jax.experimental import pallas as pl
from jax.experimental.pallas import tpu as pltpu
from jax.sharding import PartitionSpec as P

STEP_SIZE = 0.2
LEVEL = 0.5
LANES = 128
VMEM_LIMIT = 32 * 1024 * 1024
FIRST_LIMIT = 55050 * 1024
PIECES = 4
F32 = jnp.float32
BF16 = jnp.bfloat16


def shifts_of(chips):
    far_first = sorted(range(chips), key=lambda shift: (-shift.bit_count(), -shift))
    return [[far_first[at] for at in range(chips) if (at + 1) // 2 % 2 == core] for core in range(2)]


def own_index(shifts):
    (index,) = [index for index, pair in enumerate(zip(*shifts)) if 0 in pair]
    return index


def place():
    position = lax.axis_index("tile")
    return position // 2, position % 2


def columns_of(tile):
    return pl.ds(pl.multiple_of(tile * LANES, LANES), LANES)


def both_shifts(shifts):
    chip, core = place()
    pairs = list(zip(*shifts))
    own = [chip ^ jnp.where(core == 0, first, second) for first, second in pairs]
    mate = [chip ^ jnp.where(core == 0, second, first) for first, second in pairs]
    return own, mate


def signs(rows):
    lane = lax.broadcasted_iota(jnp.int32, (rows, LANES), 1)
    return jnp.where(lane < LANES // 2, 1.0, -1.0).astype(F32)


def separate(source, wide, target, chosen, masks=None):
    rows = target.shape[0]
    tiles = source.shape[0] // rows
    wide[...] = source[...].astype(F32)
    for index, tile in enumerate(chosen):
        part = wide[pl.ds(tile, rows, stride=tiles), :]
        if masks is not None:
            part = jnp.where(masks[index], part, 0.0)
        target[:, index * LANES : (index + 1) * LANES] = part.astype(BF16)


def adjoint_block(product, tile):
    half = product.shape[0] // 2
    real, imaginary = product[:half, columns_of(tile)], product[half:, columns_of(tile)]
    return (real * signs(half) + pltpu.roll(imaginary, LANES // 2, 1)).astype(BF16)


def spread_block(block, left, tile):
    half = block.shape[0]
    block = block.astype(F32)
    left[:half, columns_of(tile)] = (block * signs(half)).astype(BF16)
    left[half:, columns_of(tile)] = pltpu.roll(block, LANES // 2, 1).astype(BF16)


def arrived_block(shifts, index, sent, arrived):
    _, core = place()
    values = arrived[...]
    for side in range(2):
        if shifts[side][index] == 0:
            values = jnp.where(core == side, sent[...], values)
    return values


def times_transposed(left, right):
    return lax.dot_general(left, right, (((1,), (1,)), ((), ())), preferred_element_type=F32)


def forward_kernel(shifts, start, factors, keep, give, start_here, factors_here, wide, separated, product, sems):
    pieces = sems.shape[0] - 1
    rows, columns = separated.shape
    tiles = columns // LANES
    load_start = pltpu.make_async_copy(start, start_here, sems.at[pieces])
    load_start.start()
    loads = []
    for piece in range(pieces):
        at = pl.ds(piece * (rows * tiles // pieces), rows * tiles // pieces)
        loads.append(pltpu.make_async_copy(factors.at[at], factors_here.at[at], sems.at[piece]))
        loads[-1].start()
    load_start.wait()
    values = start_here[...].T.astype(BF16)
    for piece, load in enumerate(loads):
        at = pl.ds(piece * (rows * tiles // pieces), rows * tiles // pieces)
        load.wait()
        separate(
            factors_here.at[at], wide.at[at], separated.at[pl.ds(piece * (rows // pieces), rows // pieces)], range(tiles)
        )
    product[...] = jnp.dot(values, separated[...], preferred_element_type=F32)
    for out, chosen in zip((keep, give), both_shifts(shifts)):
        for index, tile in enumerate(chosen):
            out[index] = adjoint_block(product, tile)


def add_kernel(shifts, keep, arrived, *outs):
    outs, own = outs[:-1], outs[-1]
    for index, out in enumerate(outs):
        out[...] = (keep[index].astype(F32) + arrived[index].astype(F32)).astype(BF16)
    own[...] = outs[own_index(shifts)][...]


def rows_kernel(shifts, ranks, own, mate, observed, own_out, mate_out, turned, wide):
    chip, _ = place()
    chosen, _ = both_shifts(shifts)
    lane = lax.broadcasted_iota(jnp.int32, (1, LANES), 1) % (LANES // 2)
    masks = [lane < ranks[0, chip, tile] for tile in chosen]
    separate(own, wide, own_out, chosen, masks)
    separate(mate, wide, mate_out, chosen, masks)
    turned[...] = observed[...].T


def columns_kernel(factors, separated, wide):
    separate(factors, wide, separated, range(separated.shape[1] // LANES))


def image_kernel(shifts, sent, *refs):
    arrived, (own, mate, observed, misfit, left) = refs[:-5], refs[-5:]
    for index, block in enumerate(arrived):
        spread_block(arrived_block(shifts, index, sent, block), left, index)
    misfit[0] = times_transposed(left[...], own[...]) - observed[...]
    misfit[1] = times_transposed(left[...], mate[...])


def back_kernel(shifts, here, there, own, mate, *refs):
    outs, kept, products = refs[:-2], refs[-2], refs[-1]
    for rows, factors in ((0, own), (1, mate)):
        misfit = (here[rows] + there[1 - rows]).astype(BF16)
        products[rows] = jnp.dot(misfit, factors[...], preferred_element_type=F32)
    for index, out in enumerate(outs):
        parts = [adjoint_block(products.at[rows], index).astype(F32) for rows in range(2)]
        out[...] = (parts[0] + parts[1]).astype(BF16)
    kept[...] = outs[own_index(shifts)][...]


def pack_kernel(shifts, sent, *refs):
    for index, block in enumerate(refs[:-1]):
        refs[-1][index] = arrived_block(shifts, index, sent, block)


def gradient_kernel(shifts, own, mate, factors, gradient, left):
    for blocks, chosen in zip((own, mate), both_shifts(shifts)):
        for index, tile in enumerate(chosen):
            spread_block(blocks[index], left, tile)
    gradient[...] = times_transposed(factors[...], left[...]).astype(BF16)


def thin_out(values):
    return values - jnp.clip(values, -LEVEL, LEVEL)


def pair_kernel(here, there, gradient, total, difference):
    scale = 1.0 / math.sqrt(2)
    estimate = here[...] - STEP_SIZE * gradient[...].astype(F32)
    total[...] = (estimate + there[...]) * scale
    difference[...] = (estimate - there[...]) * scale


def shrink_pair_kernel(total, difference, gradient, out):
    scale = 1.0 / math.sqrt(2)
    step = (STEP_SIZE * scale) * gradient[...].astype(F32)
    out[...] = (thin_out(total[...] - step) + thin_out(difference[...] + step)) * scale


def shrink_kernel(band, *refs):
    tables, starts, gradients, out = refs[: -2 * band - 1], refs[-2 * band - 1 : -band - 1], refs[-band - 1 : -1], refs[-1]
    estimates = [
        start[...] - STEP_SIZE * gradient[...].astype(F32) for start, gradient in zip(starts, gradients)
    ]
    scale = 1.0 / math.sqrt(band)
    (tables,) = tables
    half = out.shape[1] // 2
    lane = lax.broadcasted_iota(jnp.int32, (1, out.shape[1]), 1)
    turn = jnp.where(lane < half, -1.0, 1.0).astype(F32)
    turned = [pltpu.roll(estimate, half, 1) * turn for estimate in estimates]
    total = jnp.zeros_like(estimates[0])
    for time in range(band):
        sample = jnp.zeros_like(estimates[0])
        for index in range(band):
            sample += tables[0, index, time] * estimates[index] + tables[1, index, time] * turned[index]
        thinned = thin_out(sample * scale)
        total += tables[0, 0, time] * thinned - tables[1, 0, time] * (pltpu.roll(thinned, half, 1) * turn)
    out[...] = total * scale


def call(kernel, name, outs, inputs, scratch=(), flops=0, spaces=(), limit=VMEM_LIMIT):
    spaces = (*spaces, *[pltpu.VMEM] * (len(inputs) - len(spaces)))
    moved = sum(x.size * x.dtype.itemsize for x in [*inputs, *outs])
    return pl.pallas_call(
        kernel,
        out_shape=outs,
        in_specs=[pl.BlockSpec(memory_space=space) for space in spaces],
        out_specs=[pl.BlockSpec(memory_space=pltpu.VMEM)] * len(outs),
        scratch_shapes=scratch,
        compiler_params=pltpu.CompilerParams(vmem_limit_bytes=limit),
        cost_estimate=pl.CostEstimate(flops=flops, bytes_accessed=moved, transcendentals=0),
        name=name,
    )(*inputs)


def to_mate(value):
    return lax.ppermute(value, "tile", [(i, i ^ 1) for i in range(lax.axis_size("tile"))])


def after(value, *others):
    return lax.optimization_barrier((value, *others))[0]


def exchange(sends, shifts, beside):
    count = lax.axis_size("tile")
    arrived = []
    for index, send in enumerate(sends[:-1]):
        pair = [shifts[core][index] or shifts[1 - core][index] for core in range(2)]
        arrived.append(lax.ppermute(send, "tile", [(i, i ^ 2 * pair[i % 2]) for i in range(count)]))
    arrived[0] = after(arrived[0], *beside)
    return [sends[-1], *arrived]


def body(u_factors, v_factors, ranks, observed, start):
    band = lax.axis_size("freq")
    rows, tiles, width = u_factors.shape[1:]
    sources = start.shape[2]
    columns = tiles * width
    left_rows = u_factors.reshape(rows * tiles, width)
    right_rows = v_factors.reshape(rows * tiles, width)
    observed = observed.reshape(rows, sources)
    start = start.reshape(rows, sources)
    shifts = shifts_of(tiles)

    def shape(*dims, dtype=BF16):
        return jax.ShapeDtypeStruct(dims, dtype)

    members = tiles // 2
    wide = pltpu.VMEM((rows * tiles, width), F32)
    block = shape(sources // 2, width)
    blocks = shape(members, sources // 2, width)
    chosen = shape(rows, members * width)
    spread = pltpu.VMEM((sources, columns), BF16)
    flops = 2 * rows * columns * sources

    keep, give = call(
        functools.partial(forward_kernel, shifts),
        "forward",
        [blocks, blocks],
        [start, right_rows],
        [
            pltpu.VMEM(start.shape, F32),
            pltpu.VMEM(right_rows.shape, BF16),
            wide,
            pltpu.VMEM((rows, columns), BF16),
            pltpu.VMEM((sources, columns), F32),
            pltpu.SemaphoreType.DMA((PIECES + 1,)),
        ],
        flops,
        [pltpu.HBM] * 2,
        FIRST_LIMIT,
    )
    sends = call(functools.partial(add_kernel, shifts), "add", [block] * (members + 1), [keep, to_mate(give)])
    left_rows = after(left_rows, sends[0])
    own_left, mate_left, turned = call(
        functools.partial(rows_kernel, shifts),
        "rows",
        [chosen, chosen, shape(sources, rows, dtype=F32)],
        [ranks, left_rows, to_mate(left_rows), after(observed, give)],
        [wide],
        spaces=[pltpu.SMEM],
    )
    early = after(start, own_left)
    starts = [start]
    for shift in range(1, band):
        starts.append(lax.ppermute(early, "freq", [(f, (f - shift) % band) for f in range(band)]))
    (misfit,) = call(
        functools.partial(image_kernel, shifts),
        "image",
        [shape(2, sources, rows, dtype=F32)],
        [*exchange(sends, shifts, [own_left, mate_left, turned]), own_left, mate_left, turned],
        [pltpu.VMEM((sources, members * width), BF16)],
        flops,
    )
    sends = call(
        functools.partial(back_kernel, shifts),
        "back",
        [block] * (members + 1),
        [misfit, to_mate(misfit), own_left, mate_left],
        [pltpu.VMEM((2, sources, members * width), F32)],
        flops,
    )
    (right,) = call(columns_kernel, "columns", [shape(rows, columns)], [after(right_rows, sends[0])], [wide])
    (own,) = call(functools.partial(pack_kernel, shifts), "pack", [blocks], exchange(sends, shifts, [right, *starts[1:]]))
    (gradient,) = call(
        functools.partial(gradient_kernel, shifts),
        "gradient",
        [shape(rows, sources)],
        [own, to_mate(own), right],
        [spread],
        flops,
    )
    gradients = [gradient]
    for shift in range(1, band):
        gradients.append(lax.ppermute(gradient, "freq", [(f, (f - shift) % band) for f in range(band)]))
    result = shape(rows, sources, dtype=F32)
    if band == 2:
        halves = call(pair_kernel, "pair", [result] * 2, [*starts, gradient])
        (estimate,) = call(shrink_pair_kernel, "shrink", [result], [*halves, gradients[1]])
        return estimate[None]
    bands = jnp.arange(band, dtype=jnp.int32)
    phases = (bands[:, None] + lax.axis_index("freq")) * bands[None, :] % band
    phases = (2.0 * math.pi / band) * phases.astype(F32)
    tables = jnp.stack([jnp.cos(phases), jnp.sin(phases)])
    (estimate,) = call(
        functools.partial(shrink_kernel, band), "shrink", [result], [tables, *starts, *gradients], spaces=[pltpu.SMEM]
    )
    return estimate[None]


def solution(mesh):
    in_specs = (
        P("freq", "tile", None, None),
        P("freq", "tile", None, None),
        P("freq", None, None),
        P("freq", "tile", None),
        P("freq", "tile", None),
    )
    out_specs = P("freq", "tile", None)
    return jax.shard_map(body, mesh=mesh, in_specs=in_specs, out_specs=out_specs, check_vma=False)
```

```python
import functools
import math

import jax
import jax.numpy as jnp
from jax import lax
from jax.experimental import pallas as pl
from jax.experimental.pallas import tpu as pltpu
from jax.sharding import PartitionSpec as P

STEP_SIZE = 0.2
LEVEL = 0.5
LANES = 128
VMEM_LIMIT = 32 * 1024 * 1024
FIRST_LIMIT = 55050 * 1024
PIECES = 4
F32 = jnp.float32
BF16 = jnp.bfloat16


def shifts_of(chips):
    upper = sorted(range(chips // 2, chips - 1), key=lambda shift: (shift % 2, shift))
    lower = sorted(range(1, chips // 2), key=lambda shift: (-shift.bit_count(), shift))
    return [[*upper, 0], [chips - 1, *lower]]


def own_index(shifts):
    (index,) = [index for index, pair in enumerate(zip(*shifts)) if 0 in pair]
    return index


def place():
    position = lax.axis_index("tile")
    return position // 2, position % 2


def columns_of(tile):
    return pl.ds(pl.multiple_of(tile * LANES, LANES), LANES)


def both_shifts(shifts):
    chip, core = place()
    pairs = list(zip(*shifts))
    own = [chip ^ jnp.where(core == 0, first, second) for first, second in pairs]
    mate = [chip ^ jnp.where(core == 0, second, first) for first, second in pairs]
    return own, mate


def signs(rows):
    lane = lax.broadcasted_iota(jnp.int32, (rows, LANES), 1)
    return jnp.where(lane < LANES // 2, 1.0, -1.0).astype(F32)


def separate(source, wide, target, chosen, masks=None):
    rows = target.shape[0]
    tiles = source.shape[0] // rows
    wide[...] = source[...].astype(F32)
    for index, tile in enumerate(chosen):
        part = wide[pl.ds(tile, rows, stride=tiles), :]
        if masks is not None:
            part = jnp.where(masks[index], part, 0.0)
        target[:, index * LANES : (index + 1) * LANES] = part.astype(BF16)


def adjoint_block(product, tile):
    half = product.shape[0] // 2
    real, imaginary = product[:half, columns_of(tile)], product[half:, columns_of(tile)]
    return (real * signs(half) + pltpu.roll(imaginary, LANES // 2, 1)).astype(BF16)


def spread_block(block, left, tile):
    half = block.shape[0]
    block = block.astype(F32)
    left[:half, columns_of(tile)] = (block * signs(half)).astype(BF16)
    left[half:, columns_of(tile)] = pltpu.roll(block, LANES // 2, 1).astype(BF16)


def arrived_block(shifts, index, sent, arrived):
    _, core = place()
    values = arrived[...]
    for side in range(2):
        if shifts[side][index] == 0:
            values = jnp.where(core == side, sent[...], values)
    return values


def times_transposed(left, right):
    return lax.dot_general(left, right, (((1,), (1,)), ((), ())), preferred_element_type=F32)


def forward_kernel(shifts, start, factors, keep, give, start_here, factors_here, wide, separated, product, sems):
    pieces = sems.shape[0] - 1
    rows, columns = separated.shape
    tiles = columns // LANES
    load_start = pltpu.make_async_copy(start, start_here, sems.at[pieces])
    load_start.start()
    loads = []
    for piece in range(pieces):
        at = pl.ds(piece * (rows * tiles // pieces), rows * tiles // pieces)
        loads.append(pltpu.make_async_copy(factors.at[at], factors_here.at[at], sems.at[piece]))
        loads[-1].start()
    load_start.wait()
    values = start_here[...].T.astype(BF16)
    for piece, load in enumerate(loads):
        at = pl.ds(piece * (rows * tiles // pieces), rows * tiles // pieces)
        load.wait()
        separate(
            factors_here.at[at], wide.at[at], separated.at[pl.ds(piece * (rows // pieces), rows // pieces)], range(tiles)
        )
    product[...] = jnp.dot(values, separated[...], preferred_element_type=F32)
    for out, chosen in zip((keep, give), both_shifts(shifts)):
        for index, tile in enumerate(chosen):
            out[index] = adjoint_block(product, tile)


def add_kernel(shifts, keep, arrived, *outs):
    outs, own = outs[:-1], outs[-1]
    for index, out in enumerate(outs):
        out[...] = (keep[index].astype(F32) + arrived[index].astype(F32)).astype(BF16)
    own[...] = outs[own_index(shifts)][...]


def rows_kernel(shifts, ranks, own, mate, observed, start, own_out, mate_out, turned, start_out, wide):
    chip, _ = place()
    chosen, _ = both_shifts(shifts)
    lane = lax.broadcasted_iota(jnp.int32, (1, LANES), 1) % (LANES // 2)
    masks = [lane < ranks[0, chip, tile] for tile in chosen]
    separate(own, wide, own_out, chosen, masks)
    separate(mate, wide, mate_out, chosen, masks)
    turned[...] = observed[...].T
    start_out[...] = start[...]


def columns_kernel(factors, separated, wide):
    separate(factors, wide, separated, range(separated.shape[1] // LANES))


def image_kernel(shifts, sent, *refs):
    arrived, (own, mate, observed, misfit, left) = refs[:-5], refs[-5:]
    for index, block in enumerate(arrived):
        spread_block(arrived_block(shifts, index, sent, block), left, index)
    misfit[0] = times_transposed(left[...], own[...]) - observed[...]
    misfit[1] = times_transposed(left[...], mate[...])


def back_kernel(shifts, here, there, own, mate, *refs):
    outs, kept, products = refs[:-2], refs[-2], refs[-1]
    for rows, factors in ((0, own), (1, mate)):
        misfit = (here[rows] + there[1 - rows]).astype(BF16)
        products[rows] = jnp.dot(misfit, factors[...], preferred_element_type=F32)
    for index, out in enumerate(outs):
        parts = [adjoint_block(products.at[rows], index).astype(F32) for rows in range(2)]
        out[...] = (parts[0] + parts[1]).astype(BF16)
    kept[...] = outs[own_index(shifts)][...]


def pack_kernel(shifts, sent, *refs):
    for index, block in enumerate(refs[:-1]):
        refs[-1][index] = arrived_block(shifts, index, sent, block)


def gradient_kernel(shifts, own, mate, factors, gradient, left):
    for blocks, chosen in zip((own, mate), both_shifts(shifts)):
        for index, tile in enumerate(chosen):
            spread_block(blocks[index], left, tile)
    gradient[...] = times_transposed(factors[...], left[...]).astype(BF16)


def thin_out(values):
    return values - jnp.clip(values, -LEVEL, LEVEL)


def pair_kernel(here, there, gradient, total, difference):
    scale = 1.0 / math.sqrt(2)
    estimate = here[...] - STEP_SIZE * gradient[...].astype(F32)
    total[...] = (estimate + there[...]) * scale
    difference[...] = (estimate - there[...]) * scale


def shrink_pair_kernel(total, difference, gradient, out):
    scale = 1.0 / math.sqrt(2)
    step = (STEP_SIZE * scale) * gradient[...].astype(F32)
    out[...] = (thin_out(total[...] - step) + thin_out(difference[...] + step)) * scale


def shrink_kernel(band, *refs):
    tables, starts, gradients, out = refs[: -2 * band - 1], refs[-2 * band - 1 : -band - 1], refs[-band - 1 : -1], refs[-1]
    estimates = [
        start[...] - STEP_SIZE * gradient[...].astype(F32) for start, gradient in zip(starts, gradients)
    ]
    scale = 1.0 / math.sqrt(band)
    (tables,) = tables
    half = out.shape[1] // 2
    lane = lax.broadcasted_iota(jnp.int32, (1, out.shape[1]), 1)
    turn = jnp.where(lane < half, -1.0, 1.0).astype(F32)
    turned = [pltpu.roll(estimate, half, 1) * turn for estimate in estimates]
    total = jnp.zeros_like(estimates[0])
    for time in range(band):
        sample = jnp.zeros_like(estimates[0])
        for index in range(band):
            sample += tables[0, index, time] * estimates[index] + tables[1, index, time] * turned[index]
        thinned = thin_out(sample * scale)
        total += tables[0, 0, time] * thinned - tables[1, 0, time] * (pltpu.roll(thinned, half, 1) * turn)
    out[...] = total * scale


def call(kernel, name, outs, inputs, scratch=(), flops=0, spaces=(), limit=VMEM_LIMIT):
    spaces = (*spaces, *[pltpu.VMEM] * (len(inputs) - len(spaces)))
    moved = sum(x.size * x.dtype.itemsize for x in [*inputs, *outs])
    return pl.pallas_call(
        kernel,
        out_shape=outs,
        in_specs=[pl.BlockSpec(memory_space=space) for space in spaces],
        out_specs=[pl.BlockSpec(memory_space=pltpu.VMEM)] * len(outs),
        scratch_shapes=scratch,
        compiler_params=pltpu.CompilerParams(vmem_limit_bytes=limit),
        cost_estimate=pl.CostEstimate(flops=flops, bytes_accessed=moved, transcendentals=0),
        name=name,
    )(*inputs)


def to_mate(value):
    return lax.ppermute(value, "tile", [(i, i ^ 1) for i in range(lax.axis_size("tile"))])


def after(value, *others):
    return lax.optimization_barrier((value, *others))[0]


def exchange(sends, shifts, beside):
    count = lax.axis_size("tile")
    arrived = []
    for index, send in enumerate(sends[:-1]):
        pair = [shifts[core][index] or shifts[1 - core][index] for core in range(2)]
        arrived.append(lax.ppermute(send, "tile", [(i, i ^ 2 * pair[i % 2]) for i in range(count)]))
    arrived[0] = after(arrived[0], *beside)
    return [sends[-1], *arrived]


def body(u_factors, v_factors, ranks, observed, start):
    band = lax.axis_size("freq")
    rows, tiles, width = u_factors.shape[1:]
    sources = start.shape[2]
    columns = tiles * width
    left_rows = u_factors.reshape(rows * tiles, width)
    right_rows = v_factors.reshape(rows * tiles, width)
    observed = observed.reshape(rows, sources)
    start = start.reshape(rows, sources)
    shifts = shifts_of(tiles)

    def shape(*dims, dtype=BF16):
        return jax.ShapeDtypeStruct(dims, dtype)

    members = tiles // 2
    wide = pltpu.VMEM((rows * tiles, width), F32)
    block = shape(sources // 2, width)
    blocks = shape(members, sources // 2, width)
    chosen = shape(rows, members * width)
    spread = pltpu.VMEM((sources, columns), BF16)
    flops = 2 * rows * columns * sources

    keep, give = call(
        functools.partial(forward_kernel, shifts),
        "forward",
        [blocks, blocks],
        [start, right_rows],
        [
            pltpu.VMEM(start.shape, F32),
            pltpu.VMEM(right_rows.shape, BF16),
            wide,
            pltpu.VMEM((rows, columns), BF16),
            pltpu.VMEM((sources, columns), F32),
            pltpu.SemaphoreType.DMA((PIECES + 1,)),
        ],
        flops,
        [pltpu.HBM] * 2,
        FIRST_LIMIT,
    )
    sends = call(functools.partial(add_kernel, shifts), "add", [block] * (members + 1), [keep, to_mate(give)])
    left_rows = after(left_rows, sends[0])
    own_left, mate_left, turned, start = call(
        functools.partial(rows_kernel, shifts),
        "rows",
        [chosen, chosen, shape(sources, rows, dtype=F32), shape(rows, sources, dtype=F32)],
        [ranks, left_rows, to_mate(left_rows), after(observed, give), after(start, give)],
        [wide],
        spaces=[pltpu.SMEM],
    )
    starts = [start]
    for shift in range(1, band):
        starts.append(lax.ppermute(start, "freq", [(f, (f - shift) % band) for f in range(band)]))
    (misfit,) = call(
        functools.partial(image_kernel, shifts),
        "image",
        [shape(2, sources, rows, dtype=F32)],
        [*exchange(sends, shifts, [own_left, mate_left, turned]), own_left, mate_left, turned],
        [pltpu.VMEM((sources, members * width), BF16)],
        flops,
    )
    sends = call(
        functools.partial(back_kernel, shifts),
        "back",
        [block] * (members + 1),
        [misfit, to_mate(misfit), own_left, mate_left],
        [pltpu.VMEM((2, sources, members * width), F32)],
        flops,
    )
    (right,) = call(columns_kernel, "columns", [shape(rows, columns)], [after(right_rows, sends[0])], [wide])
    (own,) = call(functools.partial(pack_kernel, shifts), "pack", [blocks], exchange(sends, shifts, [right, *starts[1:]]))
    (gradient,) = call(
        functools.partial(gradient_kernel, shifts),
        "gradient",
        [shape(rows, sources)],
        [own, to_mate(own), right],
        [spread],
        flops,
    )
    gradients = [gradient]
    for shift in range(1, band):
        gradients.append(lax.ppermute(gradient, "freq", [(f, (f - shift) % band) for f in range(band)]))
    result = shape(rows, sources, dtype=F32)
    if band == 2:
        halves = call(pair_kernel, "pair", [result] * 2, [*starts, gradient])
        (estimate,) = call(shrink_pair_kernel, "shrink", [result], [*halves, gradients[1]])
        return estimate[None]
    bands = jnp.arange(band, dtype=jnp.int32)
    phases = (bands[:, None] + lax.axis_index("freq")) * bands[None, :] % band
    phases = (2.0 * math.pi / band) * phases.astype(F32)
    tables = jnp.stack([jnp.cos(phases), jnp.sin(phases)])
    (estimate,) = call(
        functools.partial(shrink_kernel, band), "shrink", [result], [tables, *starts, *gradients], spaces=[pltpu.SMEM]
    )
    return estimate[None]


def solution(mesh):
    in_specs = (
        P("freq", "tile", None, None),
        P("freq", "tile", None, None),
        P("freq", None, None),
        P("freq", "tile", None),
        P("freq", "tile", None),
    )
    out_specs = P("freq", "tile", None)
    return jax.shard_map(body, mesh=mesh, in_specs=in_specs, out_specs=out_specs, check_vma=False)
```

```python
import functools
import math

import jax
import jax.numpy as jnp
from jax import lax
from jax.experimental import pallas as pl
from jax.experimental.pallas import tpu as pltpu
from jax.sharding import PartitionSpec as P

STEP_SIZE = 0.2
LEVEL = 0.5
LANES = 128
VMEM_LIMIT = 32 * 1024 * 1024
FIRST_LIMIT = 55050 * 1024
PIECES = 4
F32 = jnp.float32
BF16 = jnp.bfloat16


def shifts_of(chips):
    same_side_first = lambda shift: (shift % 2, shift)
    upper = sorted(range(chips // 2, chips - 1), key=same_side_first)
    lower = sorted(range(2, chips // 2), key=same_side_first)
    return [[*upper, 1], [*lower[:1], chips - 1, *lower[1:], 0]]


def own_index(shifts):
    (index,) = [index for index, pair in enumerate(zip(*shifts)) if 0 in pair]
    return index


def place():
    position = lax.axis_index("tile")
    return position // 2, position % 2


def columns_of(tile):
    return pl.ds(pl.multiple_of(tile * LANES, LANES), LANES)


def both_shifts(shifts):
    chip, core = place()
    pairs = list(zip(*shifts))
    own = [chip ^ jnp.where(core == 0, first, second) for first, second in pairs]
    mate = [chip ^ jnp.where(core == 0, second, first) for first, second in pairs]
    return own, mate


def signs(rows):
    lane = lax.broadcasted_iota(jnp.int32, (rows, LANES), 1)
    return jnp.where(lane < LANES // 2, 1.0, -1.0).astype(F32)


def separate(source, wide, target, chosen, masks=None):
    rows = target.shape[0]
    tiles = source.shape[0] // rows
    wide[...] = source[...].astype(F32)
    for index, tile in enumerate(chosen):
        part = wide[pl.ds(tile, rows, stride=tiles), :]
        if masks is not None:
            part = jnp.where(masks[index], part, 0.0)
        target[:, index * LANES : (index + 1) * LANES] = part.astype(BF16)


def adjoint_block(product, tile):
    half = product.shape[0] // 2
    real, imaginary = product[:half, columns_of(tile)], product[half:, columns_of(tile)]
    return (real * signs(half) + pltpu.roll(imaginary, LANES // 2, 1)).astype(BF16)


def spread_block(block, left, tile):
    half = block.shape[0]
    block = block.astype(F32)
    left[:half, columns_of(tile)] = (block * signs(half)).astype(BF16)
    left[half:, columns_of(tile)] = pltpu.roll(block, LANES // 2, 1).astype(BF16)


def arrived_block(shifts, index, sent, arrived):
    _, core = place()
    values = arrived[...]
    for side in range(2):
        if shifts[side][index] == 0:
            values = jnp.where(core == side, sent[...], values)
    return values


def times_transposed(left, right):
    return lax.dot_general(left, right, (((1,), (1,)), ((), ())), preferred_element_type=F32)


def forward_kernel(shifts, start, factors, keep, give, start_here, factors_here, wide, separated, product, sems):
    pieces = sems.shape[0] - 1
    rows, columns = separated.shape
    tiles = columns // LANES
    load_start = pltpu.make_async_copy(start, start_here, sems.at[pieces])
    load_start.start()
    loads = []
    for piece in range(pieces):
        at = pl.ds(piece * (rows * tiles // pieces), rows * tiles // pieces)
        loads.append(pltpu.make_async_copy(factors.at[at], factors_here.at[at], sems.at[piece]))
        loads[-1].start()
    load_start.wait()
    values = start_here[...].T.astype(BF16)
    for piece, load in enumerate(loads):
        at = pl.ds(piece * (rows * tiles // pieces), rows * tiles // pieces)
        load.wait()
        separate(
            factors_here.at[at], wide.at[at], separated.at[pl.ds(piece * (rows // pieces), rows // pieces)], range(tiles)
        )
    product[...] = jnp.dot(values, separated[...], preferred_element_type=F32)
    for out, chosen in zip((keep, give), both_shifts(shifts)):
        for index, tile in enumerate(chosen):
            out[index] = adjoint_block(product, tile)


def add_kernel(shifts, keep, arrived, *outs):
    outs, own = outs[:-1], outs[-1]
    for index, out in enumerate(outs):
        out[...] = (keep[index].astype(F32) + arrived[index].astype(F32)).astype(BF16)
    own[...] = outs[own_index(shifts)][...]


def rows_kernel(shifts, ranks, own, mate, observed, start, own_out, mate_out, turned, start_out, wide):
    chip, _ = place()
    chosen, _ = both_shifts(shifts)
    lane = lax.broadcasted_iota(jnp.int32, (1, LANES), 1) % (LANES // 2)
    masks = [lane < ranks[0, chip, tile] for tile in chosen]
    separate(own, wide, own_out, chosen, masks)
    separate(mate, wide, mate_out, chosen, masks)
    turned[...] = observed[...].T
    start_out[...] = start[...]


def columns_kernel(factors, separated, wide):
    separate(factors, wide, separated, range(separated.shape[1] // LANES))


def image_kernel(shifts, sent, *refs):
    arrived, (own, mate, observed, misfit, left) = refs[:-5], refs[-5:]
    for index, block in enumerate(arrived):
        spread_block(arrived_block(shifts, index, sent, block), left, index)
    misfit[0] = times_transposed(left[...], own[...]) - observed[...]
    misfit[1] = times_transposed(left[...], mate[...])


def back_kernel(shifts, here, there, own, mate, *refs):
    outs, kept, products = refs[:-2], refs[-2], refs[-1]
    for rows, factors in ((0, own), (1, mate)):
        misfit = (here[rows] + there[1 - rows]).astype(BF16)
        products[rows] = jnp.dot(misfit, factors[...], preferred_element_type=F32)
    for index, out in enumerate(outs):
        parts = [adjoint_block(products.at[rows], index).astype(F32) for rows in range(2)]
        out[...] = (parts[0] + parts[1]).astype(BF16)
    kept[...] = outs[own_index(shifts)][...]


def pack_kernel(shifts, sent, *refs):
    for index, block in enumerate(refs[:-1]):
        refs[-1][index] = arrived_block(shifts, index, sent, block)


def gradient_kernel(shifts, own, mate, factors, gradient, left):
    for blocks, chosen in zip((own, mate), both_shifts(shifts)):
        for index, tile in enumerate(chosen):
            spread_block(blocks[index], left, tile)
    gradient[...] = times_transposed(factors[...], left[...]).astype(BF16)


def thin_out(values):
    return values - jnp.clip(values, -LEVEL, LEVEL)


def pair_kernel(here, there, gradient, total, difference):
    scale = 1.0 / math.sqrt(2)
    estimate = here[...] - STEP_SIZE * gradient[...].astype(F32)
    total[...] = (estimate + there[...]) * scale
    difference[...] = (estimate - there[...]) * scale


def shrink_pair_kernel(total, difference, gradient, out):
    scale = 1.0 / math.sqrt(2)
    step = (STEP_SIZE * scale) * gradient[...].astype(F32)
    out[...] = (thin_out(total[...] - step) + thin_out(difference[...] + step)) * scale


def shrink_kernel(band, *refs):
    tables, starts, gradients, out = refs[: -2 * band - 1], refs[-2 * band - 1 : -band - 1], refs[-band - 1 : -1], refs[-1]
    estimates = [
        start[...] - STEP_SIZE * gradient[...].astype(F32) for start, gradient in zip(starts, gradients)
    ]
    scale = 1.0 / math.sqrt(band)
    (tables,) = tables
    half = out.shape[1] // 2
    lane = lax.broadcasted_iota(jnp.int32, (1, out.shape[1]), 1)
    turn = jnp.where(lane < half, -1.0, 1.0).astype(F32)
    turned = [pltpu.roll(estimate, half, 1) * turn for estimate in estimates]
    total = jnp.zeros_like(estimates[0])
    for time in range(band):
        sample = jnp.zeros_like(estimates[0])
        for index in range(band):
            sample += tables[0, index, time] * estimates[index] + tables[1, index, time] * turned[index]
        thinned = thin_out(sample * scale)
        total += tables[0, 0, time] * thinned - tables[1, 0, time] * (pltpu.roll(thinned, half, 1) * turn)
    out[...] = total * scale


def call(kernel, name, outs, inputs, scratch=(), flops=0, spaces=(), limit=VMEM_LIMIT):
    spaces = (*spaces, *[pltpu.VMEM] * (len(inputs) - len(spaces)))
    moved = sum(x.size * x.dtype.itemsize for x in [*inputs, *outs])
    return pl.pallas_call(
        kernel,
        out_shape=outs,
        in_specs=[pl.BlockSpec(memory_space=space) for space in spaces],
        out_specs=[pl.BlockSpec(memory_space=pltpu.VMEM)] * len(outs),
        scratch_shapes=scratch,
        compiler_params=pltpu.CompilerParams(vmem_limit_bytes=limit),
        cost_estimate=pl.CostEstimate(flops=flops, bytes_accessed=moved, transcendentals=0),
        name=name,
    )(*inputs)


def to_mate(value):
    return lax.ppermute(value, "tile", [(i, i ^ 1) for i in range(lax.axis_size("tile"))])


def after(value, *others):
    return lax.optimization_barrier((value, *others))[0]


def exchange(sends, shifts, beside):
    count = lax.axis_size("tile")
    arrived = []
    for index, send in enumerate(sends[:-1]):
        pair = [shifts[core][index] or shifts[1 - core][index] for core in range(2)]
        arrived.append(lax.ppermute(send, "tile", [(i, i ^ 2 * pair[i % 2]) for i in range(count)]))
    arrived[0] = after(arrived[0], *beside)
    return [sends[-1], *arrived]


def body(u_factors, v_factors, ranks, observed, start):
    band = lax.axis_size("freq")
    rows, tiles, width = u_factors.shape[1:]
    sources = start.shape[2]
    columns = tiles * width
    left_rows = u_factors.reshape(rows * tiles, width)
    right_rows = v_factors.reshape(rows * tiles, width)
    observed = observed.reshape(rows, sources)
    start = start.reshape(rows, sources)
    shifts = shifts_of(tiles)

    def shape(*dims, dtype=BF16):
        return jax.ShapeDtypeStruct(dims, dtype)

    members = tiles // 2
    wide = pltpu.VMEM((rows * tiles, width), F32)
    block = shape(sources // 2, width)
    blocks = shape(members, sources // 2, width)
    chosen = shape(rows, members * width)
    spread = pltpu.VMEM((sources, columns), BF16)
    flops = 2 * rows * columns * sources

    keep, give = call(
        functools.partial(forward_kernel, shifts),
        "forward",
        [blocks, blocks],
        [start, right_rows],
        [
            pltpu.VMEM(start.shape, F32),
            pltpu.VMEM(right_rows.shape, BF16),
            wide,
            pltpu.VMEM((rows, columns), BF16),
            pltpu.VMEM((sources, columns), F32),
            pltpu.SemaphoreType.DMA((PIECES + 1,)),
        ],
        flops,
        [pltpu.HBM] * 2,
        FIRST_LIMIT,
    )
    sends = call(functools.partial(add_kernel, shifts), "add", [block] * (members + 1), [keep, to_mate(give)])
    left_rows = after(left_rows, sends[0])
    own_left, mate_left, turned, start = call(
        functools.partial(rows_kernel, shifts),
        "rows",
        [chosen, chosen, shape(sources, rows, dtype=F32), shape(rows, sources, dtype=F32)],
        [ranks, left_rows, to_mate(left_rows), after(observed, give), after(start, give)],
        [wide],
        spaces=[pltpu.SMEM],
    )
    starts = [start]
    for shift in range(1, band):
        starts.append(lax.ppermute(start, "freq", [(f, (f - shift) % band) for f in range(band)]))
    (misfit,) = call(
        functools.partial(image_kernel, shifts),
        "image",
        [shape(2, sources, rows, dtype=F32)],
        [*exchange(sends, shifts, [own_left, mate_left, turned]), own_left, mate_left, turned],
        [pltpu.VMEM((sources, members * width), BF16)],
        flops,
    )
    sends = call(
        functools.partial(back_kernel, shifts),
        "back",
        [block] * (members + 1),
        [misfit, to_mate(misfit), own_left, mate_left],
        [pltpu.VMEM((2, sources, members * width), F32)],
        flops,
    )
    (right,) = call(columns_kernel, "columns", [shape(rows, columns)], [after(right_rows, sends[0])], [wide])
    (own,) = call(functools.partial(pack_kernel, shifts), "pack", [blocks], exchange(sends, shifts, [right, *starts[1:]]))
    (gradient,) = call(
        functools.partial(gradient_kernel, shifts),
        "gradient",
        [shape(rows, sources)],
        [own, to_mate(own), right],
        [spread],
        flops,
    )
    gradients = [gradient]
    for shift in range(1, band):
        gradients.append(lax.ppermute(gradient, "freq", [(f, (f - shift) % band) for f in range(band)]))
    result = shape(rows, sources, dtype=F32)
    if band == 2:
        halves = call(pair_kernel, "pair", [result] * 2, [*starts, gradient])
        (estimate,) = call(shrink_pair_kernel, "shrink", [result], [*halves, gradients[1]])
        return estimate[None]
    bands = jnp.arange(band, dtype=jnp.int32)
    phases = (bands[:, None] + lax.axis_index("freq")) * bands[None, :] % band
    phases = (2.0 * math.pi / band) * phases.astype(F32)
    tables = jnp.stack([jnp.cos(phases), jnp.sin(phases)])
    (estimate,) = call(
        functools.partial(shrink_kernel, band), "shrink", [result], [tables, *starts, *gradients], spaces=[pltpu.SMEM]
    )
    return estimate[None]


def solution(mesh):
    in_specs = (
        P("freq", "tile", None, None),
        P("freq", "tile", None, None),
        P("freq", None, None),
        P("freq", "tile", None),
        P("freq", "tile", None),
    )
    out_specs = P("freq", "tile", None)
    return jax.shard_map(body, mesh=mesh, in_specs=in_specs, out_specs=out_specs, check_vma=False)
```

```python
import functools
import math

import jax
import jax.numpy as jnp
from jax import lax
from jax.experimental import pallas as pl
from jax.experimental.pallas import tpu as pltpu
from jax.sharding import PartitionSpec as P

STEP_SIZE = 0.2
LEVEL = 0.5
LANES = 128
VMEM_LIMIT = 32 * 1024 * 1024
FIRST_LIMIT = 55050 * 1024
PIECES = 4
F32 = jnp.float32
BF16 = jnp.bfloat16


def shifts_of(chips):
    order = sorted(range(0, chips, 2), key=lambda shift: -(shift ^ shift >> 1))
    return [order, [shift + 1 for shift in order]]


def own_index(shifts):
    (index,) = [index for index, pair in enumerate(zip(*shifts)) if 0 in pair]
    return index


def place():
    position = lax.axis_index("tile")
    return position // 2, position % 2


def columns_of(tile):
    return pl.ds(pl.multiple_of(tile * LANES, LANES), LANES)


def both_shifts(shifts):
    chip, core = place()
    pairs = list(zip(*shifts))
    own = [chip ^ jnp.where(core == 0, first, second) for first, second in pairs]
    mate = [chip ^ jnp.where(core == 0, second, first) for first, second in pairs]
    return own, mate


def signs(rows):
    lane = lax.broadcasted_iota(jnp.int32, (rows, LANES), 1)
    return jnp.where(lane < LANES // 2, 1.0, -1.0).astype(F32)


def separate(source, wide, target, chosen, masks=None):
    rows = target.shape[0]
    tiles = source.shape[0] // rows
    wide[...] = source[...].astype(F32)
    for index, tile in enumerate(chosen):
        part = wide[pl.ds(tile, rows, stride=tiles), :]
        if masks is not None:
            part = jnp.where(masks[index], part, 0.0)
        target[:, index * LANES : (index + 1) * LANES] = part.astype(BF16)


def adjoint_block(product, tile):
    half = product.shape[0] // 2
    real, imaginary = product[:half, columns_of(tile)], product[half:, columns_of(tile)]
    return (real * signs(half) + pltpu.roll(imaginary, LANES // 2, 1)).astype(BF16)


def spread_block(block, left, tile):
    half = block.shape[0]
    block = block.astype(F32)
    left[:half, columns_of(tile)] = (block * signs(half)).astype(BF16)
    left[half:, columns_of(tile)] = pltpu.roll(block, LANES // 2, 1).astype(BF16)


def arrived_block(shifts, index, sent, arrived):
    _, core = place()
    values = arrived[...]
    for side in range(2):
        if shifts[side][index] == 0:
            values = jnp.where(core == side, sent[...], values)
    return values


def times_transposed(left, right):
    return lax.dot_general(left, right, (((1,), (1,)), ((), ())), preferred_element_type=F32)


def forward_kernel(shifts, start, factors, keep, give, start_here, factors_here, wide, separated, product, sems):
    pieces = sems.shape[0] - 1
    rows, columns = separated.shape
    tiles = columns // LANES
    load_start = pltpu.make_async_copy(start, start_here, sems.at[pieces])
    load_start.start()
    loads = []
    for piece in range(pieces):
        at = pl.ds(piece * (rows * tiles // pieces), rows * tiles // pieces)
        loads.append(pltpu.make_async_copy(factors.at[at], factors_here.at[at], sems.at[piece]))
        loads[-1].start()
    load_start.wait()
    values = start_here[...].T.astype(BF16)
    for piece, load in enumerate(loads):
        at = pl.ds(piece * (rows * tiles // pieces), rows * tiles // pieces)
        load.wait()
        separate(
            factors_here.at[at], wide.at[at], separated.at[pl.ds(piece * (rows // pieces), rows // pieces)], range(tiles)
        )
    product[...] = jnp.dot(values, separated[...], preferred_element_type=F32)
    for out, chosen in zip((keep, give), both_shifts(shifts)):
        for index, tile in enumerate(chosen):
            out[index] = adjoint_block(product, tile)


def add_kernel(shifts, keep, arrived, *outs):
    outs, own = outs[:-1], outs[-1]
    for index, out in enumerate(outs):
        out[...] = (keep[index].astype(F32) + arrived[index].astype(F32)).astype(BF16)
    own[...] = outs[own_index(shifts)][...]


def rows_kernel(shifts, ranks, own, mate, observed, start, own_out, mate_out, turned, start_out, wide):
    chip, _ = place()
    chosen, _ = both_shifts(shifts)
    lane = lax.broadcasted_iota(jnp.int32, (1, LANES), 1) % (LANES // 2)
    masks = [lane < ranks[0, chip, tile] for tile in chosen]
    separate(own, wide, own_out, chosen, masks)
    separate(mate, wide, mate_out, chosen, masks)
    turned[...] = observed[...].T
    start_out[...] = start[...]


def columns_kernel(factors, separated, wide):
    separate(factors, wide, separated, range(separated.shape[1] // LANES))


def image_kernel(shifts, sent, *refs):
    arrived, (own, mate, observed, misfit, left) = refs[:-5], refs[-5:]
    for index, block in enumerate(arrived):
        spread_block(arrived_block(shifts, index, sent, block), left, index)
    misfit[0] = times_transposed(left[...], own[...]) - observed[...]
    misfit[1] = times_transposed(left[...], mate[...])


def back_kernel(shifts, here, there, own, mate, *refs):
    outs, kept, products = refs[:-2], refs[-2], refs[-1]
    for rows, factors in ((0, own), (1, mate)):
        misfit = (here[rows] + there[1 - rows]).astype(BF16)
        products[rows] = jnp.dot(misfit, factors[...], preferred_element_type=F32)
    for index, out in enumerate(outs):
        parts = [adjoint_block(products.at[rows], index).astype(F32) for rows in range(2)]
        out[...] = (parts[0] + parts[1]).astype(BF16)
    kept[...] = outs[own_index(shifts)][...]


def pack_kernel(shifts, sent, *refs):
    for index, block in enumerate(refs[:-1]):
        refs[-1][index] = arrived_block(shifts, index, sent, block)


def gradient_kernel(shifts, own, mate, factors, gradient, left):
    for blocks, chosen in zip((own, mate), both_shifts(shifts)):
        for index, tile in enumerate(chosen):
            spread_block(blocks[index], left, tile)
    gradient[...] = times_transposed(factors[...], left[...]).astype(BF16)


def thin_out(values):
    return values - jnp.clip(values, -LEVEL, LEVEL)


def pair_kernel(here, there, gradient, total, difference):
    scale = 1.0 / math.sqrt(2)
    estimate = here[...] - STEP_SIZE * gradient[...].astype(F32)
    total[...] = (estimate + there[...]) * scale
    difference[...] = (estimate - there[...]) * scale


def shrink_pair_kernel(total, difference, gradient, out):
    scale = 1.0 / math.sqrt(2)
    step = (STEP_SIZE * scale) * gradient[...].astype(F32)
    out[...] = (thin_out(total[...] - step) + thin_out(difference[...] + step)) * scale


def shrink_kernel(band, *refs):
    tables, starts, gradients, out = refs[: -2 * band - 1], refs[-2 * band - 1 : -band - 1], refs[-band - 1 : -1], refs[-1]
    estimates = [
        start[...] - STEP_SIZE * gradient[...].astype(F32) for start, gradient in zip(starts, gradients)
    ]
    scale = 1.0 / math.sqrt(band)
    (tables,) = tables
    half = out.shape[1] // 2
    lane = lax.broadcasted_iota(jnp.int32, (1, out.shape[1]), 1)
    turn = jnp.where(lane < half, -1.0, 1.0).astype(F32)
    turned = [pltpu.roll(estimate, half, 1) * turn for estimate in estimates]
    total = jnp.zeros_like(estimates[0])
    for time in range(band):
        sample = jnp.zeros_like(estimates[0])
        for index in range(band):
            sample += tables[0, index, time] * estimates[index] + tables[1, index, time] * turned[index]
        thinned = thin_out(sample * scale)
        total += tables[0, 0, time] * thinned - tables[1, 0, time] * (pltpu.roll(thinned, half, 1) * turn)
    out[...] = total * scale


def call(kernel, name, outs, inputs, scratch=(), flops=0, spaces=(), limit=VMEM_LIMIT):
    spaces = (*spaces, *[pltpu.VMEM] * (len(inputs) - len(spaces)))
    moved = sum(x.size * x.dtype.itemsize for x in [*inputs, *outs])
    return pl.pallas_call(
        kernel,
        out_shape=outs,
        in_specs=[pl.BlockSpec(memory_space=space) for space in spaces],
        out_specs=[pl.BlockSpec(memory_space=pltpu.VMEM)] * len(outs),
        scratch_shapes=scratch,
        compiler_params=pltpu.CompilerParams(vmem_limit_bytes=limit),
        cost_estimate=pl.CostEstimate(flops=flops, bytes_accessed=moved, transcendentals=0),
        name=name,
    )(*inputs)


def to_mate(value):
    return lax.ppermute(value, "tile", [(i, i ^ 1) for i in range(lax.axis_size("tile"))])


def after(value, *others):
    return lax.optimization_barrier((value, *others))[0]


def exchange(sends, shifts, beside):
    count = lax.axis_size("tile")
    arrived = []
    for index, send in enumerate(sends[:-1]):
        pair = [shifts[core][index] or shifts[1 - core][index] for core in range(2)]
        arrived.append(lax.ppermute(send, "tile", [(i, i ^ 2 * pair[i % 2]) for i in range(count)]))
    arrived[0] = after(arrived[0], *beside)
    return [sends[-1], *arrived]


def body(u_factors, v_factors, ranks, observed, start):
    band = lax.axis_size("freq")
    rows, tiles, width = u_factors.shape[1:]
    sources = start.shape[2]
    columns = tiles * width
    left_rows = u_factors.reshape(rows * tiles, width)
    right_rows = v_factors.reshape(rows * tiles, width)
    observed = observed.reshape(rows, sources)
    start = start.reshape(rows, sources)
    shifts = shifts_of(tiles)

    def shape(*dims, dtype=BF16):
        return jax.ShapeDtypeStruct(dims, dtype)

    members = tiles // 2
    wide = pltpu.VMEM((rows * tiles, width), F32)
    block = shape(sources // 2, width)
    blocks = shape(members, sources // 2, width)
    chosen = shape(rows, members * width)
    spread = pltpu.VMEM((sources, columns), BF16)
    flops = 2 * rows * columns * sources

    keep, give = call(
        functools.partial(forward_kernel, shifts),
        "forward",
        [blocks, blocks],
        [start, right_rows],
        [
            pltpu.VMEM(start.shape, F32),
            pltpu.VMEM(right_rows.shape, BF16),
            wide,
            pltpu.VMEM((rows, columns), BF16),
            pltpu.VMEM((sources, columns), F32),
            pltpu.SemaphoreType.DMA((PIECES + 1,)),
        ],
        flops,
        [pltpu.HBM] * 2,
        FIRST_LIMIT,
    )
    sends = call(functools.partial(add_kernel, shifts), "add", [block] * (members + 1), [keep, to_mate(give)])
    left_rows = after(left_rows, sends[0])
    own_left, mate_left, turned, start = call(
        functools.partial(rows_kernel, shifts),
        "rows",
        [chosen, chosen, shape(sources, rows, dtype=F32), shape(rows, sources, dtype=F32)],
        [ranks, left_rows, to_mate(left_rows), after(observed, give), after(start, give)],
        [wide],
        spaces=[pltpu.SMEM],
    )
    starts = [start]
    for shift in range(1, band):
        starts.append(lax.ppermute(start, "freq", [(f, (f - shift) % band) for f in range(band)]))
    (misfit,) = call(
        functools.partial(image_kernel, shifts),
        "image",
        [shape(2, sources, rows, dtype=F32)],
        [*exchange(sends, shifts, [own_left, mate_left, turned]), own_left, mate_left, turned],
        [pltpu.VMEM((sources, members * width), BF16)],
        flops,
    )
    sends = call(
        functools.partial(back_kernel, shifts),
        "back",
        [block] * (members + 1),
        [misfit, to_mate(misfit), own_left, mate_left],
        [pltpu.VMEM((2, sources, members * width), F32)],
        flops,
    )
    (right,) = call(columns_kernel, "columns", [shape(rows, columns)], [after(right_rows, sends[0])], [wide])
    (own,) = call(functools.partial(pack_kernel, shifts), "pack", [blocks], exchange(sends, shifts, [right, *starts[1:]]))
    (gradient,) = call(
        functools.partial(gradient_kernel, shifts),
        "gradient",
        [shape(rows, sources)],
        [own, to_mate(own), right],
        [spread],
        flops,
    )
    gradients = [gradient]
    for shift in range(1, band):
        gradients.append(lax.ppermute(gradient, "freq", [(f, (f - shift) % band) for f in range(band)]))
    result = shape(rows, sources, dtype=F32)
    if band == 2:
        halves = call(pair_kernel, "pair", [result] * 2, [*starts, gradient])
        (estimate,) = call(shrink_pair_kernel, "shrink", [result], [*halves, gradients[1]])
        return estimate[None]
    bands = jnp.arange(band, dtype=jnp.int32)
    phases = (bands[:, None] + lax.axis_index("freq")) * bands[None, :] % band
    phases = (2.0 * math.pi / band) * phases.astype(F32)
    tables = jnp.stack([jnp.cos(phases), jnp.sin(phases)])
    (estimate,) = call(
        functools.partial(shrink_kernel, band), "shrink", [result], [tables, *starts, *gradients], spaces=[pltpu.SMEM]
    )
    return estimate[None]


def solution(mesh):
    in_specs = (
        P("freq", "tile", None, None),
        P("freq", "tile", None, None),
        P("freq", None, None),
        P("freq", "tile", None),
        P("freq", "tile", None),
    )
    out_specs = P("freq", "tile", None)
    return jax.shard_map(body, mesh=mesh, in_specs=in_specs, out_specs=out_specs, check_vma=False)
```

```python
import functools
import math

import jax
import jax.numpy as jnp
from jax import lax
from jax.experimental import pallas as pl
from jax.experimental.pallas import tpu as pltpu
from jax.sharding import PartitionSpec as P

STEP_SIZE = 0.2
LEVEL = 0.5
LANES = 128
VMEM_LIMIT = 32 * 1024 * 1024
FIRST_LIMIT = 55050 * 1024
PIECES = 4
F32 = jnp.float32
BF16 = jnp.bfloat16


def shifts_of(chips):
    even = list(range(chips - 2, -1, -2))
    odd = [shift + 1 for shift in even]
    even[-2], odd[-1] = odd[-1], even[-2]
    return [even, odd]


def place():
    position = lax.axis_index("tile")
    return position // 2, position % 2


def columns_of(tile):
    return pl.ds(pl.multiple_of(tile * LANES, LANES), LANES)


def both_shifts(shifts):
    chip, core = place()
    pairs = list(zip(*shifts))
    own = [chip ^ jnp.where(core == 0, first, second) for first, second in pairs]
    mate = [chip ^ jnp.where(core == 0, second, first) for first, second in pairs]
    return own, mate


def signs(rows):
    lane = lax.broadcasted_iota(jnp.int32, (rows, LANES), 1)
    return jnp.where(lane < LANES // 2, 1.0, -1.0).astype(F32)


def separate(source, wide, target, chosen, masks=None):
    rows = target.shape[0]
    tiles = source.shape[0] // rows
    wide[...] = source[...].astype(F32)
    for index, tile in enumerate(chosen):
        part = wide[pl.ds(tile, rows, stride=tiles), :]
        if masks is not None:
            part = jnp.where(masks[index], part, 0.0)
        target[:, index * LANES : (index + 1) * LANES] = part.astype(BF16)


def adjoint_block(product, tile):
    half = product.shape[0] // 2
    real, imaginary = product[:half, columns_of(tile)], product[half:, columns_of(tile)]
    return (real * signs(half) + pltpu.roll(imaginary, LANES // 2, 1)).astype(BF16)


def spread_block(block, left, tile):
    half = block.shape[0]
    block = block.astype(F32)
    left[:half, columns_of(tile)] = (block * signs(half)).astype(BF16)
    left[half:, columns_of(tile)] = pltpu.roll(block, LANES // 2, 1).astype(BF16)


def times_transposed(left, right):
    return lax.dot_general(left, right, (((1,), (1,)), ((), ())), preferred_element_type=F32)


def forward_kernel(shifts, start, factors, keep, give, start_here, factors_here, wide, separated, product, sems):
    pieces = sems.shape[0] - 1
    rows, columns = separated.shape
    tiles = columns // LANES
    load_start = pltpu.make_async_copy(start, start_here, sems.at[pieces])
    load_start.start()
    loads = []
    for piece in range(pieces):
        at = pl.ds(piece * (rows * tiles // pieces), rows * tiles // pieces)
        loads.append(pltpu.make_async_copy(factors.at[at], factors_here.at[at], sems.at[piece]))
        loads[-1].start()
    load_start.wait()
    values = start_here[...].T.astype(BF16)
    for piece, load in enumerate(loads):
        at = pl.ds(piece * (rows * tiles // pieces), rows * tiles // pieces)
        load.wait()
        separate(
            factors_here.at[at], wide.at[at], separated.at[pl.ds(piece * (rows // pieces), rows // pieces)], range(tiles)
        )
    product[...] = jnp.dot(values, separated[...], preferred_element_type=F32)
    for out, chosen in zip((keep, give), both_shifts(shifts)):
        for index, tile in enumerate(chosen):
            out[index] = adjoint_block(product, tile)


def add_kernel(keep, arrived, *outs):
    for index, out in enumerate(outs):
        out[...] = (keep[index].astype(F32) + arrived[index].astype(F32)).astype(BF16)


def rows_kernel(shifts, ranks, own, mate, observed, start, own_out, mate_out, turned, start_out, wide):
    chip, _ = place()
    _, chosen = both_shifts(shifts)
    lane = lax.broadcasted_iota(jnp.int32, (1, LANES), 1) % (LANES // 2)
    masks = [lane < ranks[0, chip, tile] for tile in chosen]
    separate(own, wide, own_out, chosen, masks)
    separate(mate, wide, mate_out, chosen, masks)
    turned[...] = observed[...].T
    start_out[...] = start[...]


def columns_kernel(factors, separated, wide):
    separate(factors, wide, separated, range(separated.shape[1] // LANES))


def image_kernel(*refs):
    arrived, (own, mate, observed, misfit, left) = refs[:-5], refs[-5:]
    for index, block in enumerate(arrived):
        spread_block(block[...], left, index)
    misfit[0] = times_transposed(left[...], own[...]) - observed[...]
    misfit[1] = times_transposed(left[...], mate[...])


def back_kernel(here, there, own, mate, *refs):
    outs, products = refs[:-1], refs[-1]
    for rows, factors in ((0, own), (1, mate)):
        misfit = (here[rows] + there[1 - rows]).astype(BF16)
        products[rows] = jnp.dot(misfit, factors[...], preferred_element_type=F32)
    for index, out in enumerate(outs):
        parts = [adjoint_block(products.at[rows], index).astype(F32) for rows in range(2)]
        out[...] = (parts[0] + parts[1]).astype(BF16)


def pack_kernel(*refs):
    for index, block in enumerate(refs[:-1]):
        refs[-1][index] = block[...]


def gradient_kernel(shifts, own, mate, factors, gradient, left):
    for blocks, chosen in zip((own, mate), both_shifts(shifts)):
        for index, tile in enumerate(chosen):
            spread_block(blocks[index], left, tile)
    gradient[...] = times_transposed(factors[...], left[...]).astype(BF16)


def thin_out(values):
    return values - jnp.clip(values, -LEVEL, LEVEL)


def pair_kernel(here, there, gradient, total, difference):
    scale = 1.0 / math.sqrt(2)
    estimate = here[...] - STEP_SIZE * gradient[...].astype(F32)
    total[...] = (estimate + there[...]) * scale
    difference[...] = (estimate - there[...]) * scale


def shrink_pair_kernel(total, difference, gradient, out):
    scale = 1.0 / math.sqrt(2)
    step = (STEP_SIZE * scale) * gradient[...].astype(F32)
    out[...] = (thin_out(total[...] - step) + thin_out(difference[...] + step)) * scale


def shrink_kernel(band, *refs):
    tables, starts, gradients, out = refs[: -2 * band - 1], refs[-2 * band - 1 : -band - 1], refs[-band - 1 : -1], refs[-1]
    estimates = [
        start[...] - STEP_SIZE * gradient[...].astype(F32) for start, gradient in zip(starts, gradients)
    ]
    scale = 1.0 / math.sqrt(band)
    (tables,) = tables
    half = out.shape[1] // 2
    lane = lax.broadcasted_iota(jnp.int32, (1, out.shape[1]), 1)
    turn = jnp.where(lane < half, -1.0, 1.0).astype(F32)
    turned = [pltpu.roll(estimate, half, 1) * turn for estimate in estimates]
    total = jnp.zeros_like(estimates[0])
    for time in range(band):
        sample = jnp.zeros_like(estimates[0])
        for index in range(band):
            sample += tables[0, index, time] * estimates[index] + tables[1, index, time] * turned[index]
        thinned = thin_out(sample * scale)
        total += tables[0, 0, time] * thinned - tables[1, 0, time] * (pltpu.roll(thinned, half, 1) * turn)
    out[...] = total * scale


def call(kernel, name, outs, inputs, scratch=(), flops=0, spaces=(), limit=VMEM_LIMIT):
    spaces = (*spaces, *[pltpu.VMEM] * (len(inputs) - len(spaces)))
    moved = sum(x.size * x.dtype.itemsize for x in [*inputs, *outs])
    return pl.pallas_call(
        kernel,
        out_shape=outs,
        in_specs=[pl.BlockSpec(memory_space=space) for space in spaces],
        out_specs=[pl.BlockSpec(memory_space=pltpu.VMEM)] * len(outs),
        scratch_shapes=scratch,
        compiler_params=pltpu.CompilerParams(vmem_limit_bytes=limit),
        cost_estimate=pl.CostEstimate(flops=flops, bytes_accessed=moved, transcendentals=0),
        name=name,
    )(*inputs)


def to_mate(value):
    return lax.ppermute(value, "tile", [(i, i ^ 1) for i in range(lax.axis_size("tile"))])


def after(value, *others):
    return lax.optimization_barrier((value, *others))[0]


def exchange(sends, shifts, beside):
    count = lax.axis_size("tile")
    arrived = []
    for index, send in enumerate(sends):
        pairs = [(i, i ^ 2 * shifts[i % 2][index] ^ 1) for i in range(count)]
        arrived.append(lax.ppermute(send, "tile", pairs))
    return [after(arrived[0], *beside), *arrived[1:]]


def body(u_factors, v_factors, ranks, observed, start):
    band = lax.axis_size("freq")
    rows, tiles, width = u_factors.shape[1:]
    sources = start.shape[2]
    columns = tiles * width
    left_rows = u_factors.reshape(rows * tiles, width)
    right_rows = v_factors.reshape(rows * tiles, width)
    observed = observed.reshape(rows, sources)
    start = start.reshape(rows, sources)
    shifts = shifts_of(tiles)

    def shape(*dims, dtype=BF16):
        return jax.ShapeDtypeStruct(dims, dtype)

    members = tiles // 2
    wide = pltpu.VMEM((rows * tiles, width), F32)
    block = shape(sources // 2, width)
    blocks = shape(members, sources // 2, width)
    chosen = shape(rows, members * width)
    spread = pltpu.VMEM((sources, columns), BF16)
    flops = 2 * rows * columns * sources

    keep, give = call(
        functools.partial(forward_kernel, shifts),
        "forward",
        [blocks, blocks],
        [start, right_rows],
        [
            pltpu.VMEM(start.shape, F32),
            pltpu.VMEM(right_rows.shape, BF16),
            wide,
            pltpu.VMEM((rows, columns), BF16),
            pltpu.VMEM((sources, columns), F32),
            pltpu.SemaphoreType.DMA((PIECES + 1,)),
        ],
        flops,
        [pltpu.HBM] * 2,
        FIRST_LIMIT,
    )
    sends = call(add_kernel, "add", [block] * members, [keep, to_mate(give)])
    left_rows = after(left_rows, sends[0])
    own_left, mate_left, turned, start = call(
        functools.partial(rows_kernel, shifts),
        "rows",
        [chosen, chosen, shape(sources, rows, dtype=F32), shape(rows, sources, dtype=F32)],
        [ranks, left_rows, to_mate(left_rows), after(observed, give), after(start, give)],
        [wide],
        spaces=[pltpu.SMEM],
    )
    starts = [start]
    for shift in range(1, band):
        starts.append(lax.ppermute(start, "freq", [(f, (f - shift) % band) for f in range(band)]))
    (misfit,) = call(
        image_kernel,
        "image",
        [shape(2, sources, rows, dtype=F32)],
        [*exchange(sends, shifts, [own_left, mate_left, turned]), own_left, mate_left, turned],
        [pltpu.VMEM((sources, members * width), BF16)],
        flops,
    )
    sends = call(
        back_kernel,
        "back",
        [block] * members,
        [misfit, to_mate(misfit), own_left, mate_left],
        [pltpu.VMEM((2, sources, members * width), F32)],
        flops,
    )
    (right,) = call(columns_kernel, "columns", [shape(rows, columns)], [after(right_rows, sends[0])], [wide])
    (own,) = call(pack_kernel, "pack", [blocks], exchange(sends, shifts[::-1], [right, *starts[1:]]))
    (gradient,) = call(
        functools.partial(gradient_kernel, shifts),
        "gradient",
        [shape(rows, sources)],
        [own, to_mate(own), right],
        [spread],
        flops,
    )
    gradients = [gradient]
    for shift in range(1, band):
        gradients.append(lax.ppermute(gradient, "freq", [(f, (f - shift) % band) for f in range(band)]))
    result = shape(rows, sources, dtype=F32)
    if band == 2:
        halves = call(pair_kernel, "pair", [result] * 2, [*starts, gradient])
        (estimate,) = call(shrink_pair_kernel, "shrink", [result], [*halves, gradients[1]])
        return estimate[None]
    bands = jnp.arange(band, dtype=jnp.int32)
    phases = (bands[:, None] + lax.axis_index("freq")) * bands[None, :] % band
    phases = (2.0 * math.pi / band) * phases.astype(F32)
    tables = jnp.stack([jnp.cos(phases), jnp.sin(phases)])
    (estimate,) = call(
        functools.partial(shrink_kernel, band), "shrink", [result], [tables, *starts, *gradients], spaces=[pltpu.SMEM]
    )
    return estimate[None]


def solution(mesh):
    in_specs = (
        P("freq", "tile", None, None),
        P("freq", "tile", None, None),
        P("freq", None, None),
        P("freq", "tile", None),
        P("freq", "tile", None),
    )
    out_specs = P("freq", "tile", None)
    return jax.shard_map(body, mesh=mesh, in_specs=in_specs, out_specs=out_specs, check_vma=False)
```

```python
import functools
import math

import jax
import jax.numpy as jnp
from jax import lax
from jax.experimental import pallas as pl
from jax.experimental.pallas import tpu as pltpu
from jax.sharding import PartitionSpec as P

STEP_SIZE = 0.2
LEVEL = 0.5
LANES = 128
VMEM_LIMIT = 32 * 1024 * 1024
FIRST_LIMIT = 55050 * 1024
PIECES = 4
F32 = jnp.float32
BF16 = jnp.bfloat16


def shifts_of(chips):
    even = list(range(chips - 2, -1, -2))
    odd = [shift + 1 for shift in even]
    even[-2], odd[-1] = odd[-1], even[-2]
    return [even, odd]


def place():
    position = lax.axis_index("tile")
    return position // 2, position % 2


def columns_of(tile):
    return pl.ds(pl.multiple_of(tile * LANES, LANES), LANES)


def both_shifts(shifts):
    chip, core = place()
    pairs = list(zip(*shifts))
    own = [chip ^ jnp.where(core == 0, first, second) for first, second in pairs]
    mate = [chip ^ jnp.where(core == 0, second, first) for first, second in pairs]
    return own, mate


def signs(rows):
    lane = lax.broadcasted_iota(jnp.int32, (rows, LANES), 1)
    return jnp.where(lane < LANES // 2, 1.0, -1.0).astype(F32)


def separate(source, wide, target, chosen, masks=None):
    rows = target.shape[0]
    tiles = source.shape[0] // rows
    wide[...] = source[...].astype(F32)
    for index, tile in enumerate(chosen):
        part = wide[pl.ds(tile, rows, stride=tiles), :]
        if masks is not None:
            part = jnp.where(masks[index], part, 0.0)
        target[:, index * LANES : (index + 1) * LANES] = part.astype(BF16)


def adjoint_block(product, tile):
    half = product.shape[0] // 2
    real, imaginary = product[:half, columns_of(tile)], product[half:, columns_of(tile)]
    return (real * signs(half) + pltpu.roll(imaginary, LANES // 2, 1)).astype(BF16)


def spread_block(block, left, tile):
    half = block.shape[0]
    block = block.astype(F32)
    left[:half, columns_of(tile)] = (block * signs(half)).astype(BF16)
    left[half:, columns_of(tile)] = pltpu.roll(block, LANES // 2, 1).astype(BF16)


def times_transposed(left, right):
    return lax.dot_general(left, right, (((1,), (1,)), ((), ())), preferred_element_type=F32)


def block_parts(shifts, start, separated, product):
    product[...] = jnp.dot(start[...].T.astype(BF16), separated[...], preferred_element_type=F32)
    return [adjoint_block(product, index) for index in range(len(shifts[0]))]


def forward_kernel(shifts, start, factors, parts, start_here, factors_here, sems, wide, separated, product):
    pieces = sems.shape[0] - 1
    rows = start.shape[0]
    tiles = factors.shape[0] // rows
    chosen, _ = both_shifts(shifts)
    load_start = pltpu.make_async_copy(start, start_here, sems.at[pieces])
    load_start.start()
    loads = []
    for piece in range(pieces):
        at = pl.ds(piece * (rows * tiles // pieces), rows * tiles // pieces)
        loads.append(pltpu.make_async_copy(factors.at[at], factors_here.at[at], sems.at[piece]))
        loads[-1].start()
    load_start.wait()
    for piece, load in enumerate(loads):
        at = pl.ds(piece * (rows * tiles // pieces), rows * tiles // pieces)
        load.wait()
        separate(
            factors_here.at[at], wide.at[at], separated.at[pl.ds(piece * (rows // pieces), rows // pieces)], chosen
        )
    for index, block in enumerate(block_parts(shifts, start_here, separated, product)):
        parts[index] = block


def join_kernel(shifts, parts, start, factors, *refs):
    outs, (wide, separated, product) = refs[:-3], refs[-3:]
    chosen, _ = both_shifts(shifts)
    separate(factors, wide, separated, chosen)
    for index, block in enumerate(block_parts(shifts, start, separated, product)):
        outs[index][...] = (parts[index].astype(F32) + block.astype(F32)).astype(BF16)


def rows_kernel(shifts, ranks, own, mate, observed, start, own_out, mate_out, turned, start_out, wide):
    chip, _ = place()
    _, chosen = both_shifts(shifts)
    lane = lax.broadcasted_iota(jnp.int32, (1, LANES), 1) % (LANES // 2)
    masks = [lane < ranks[0, chip, tile] for tile in chosen]
    separate(own, wide, own_out, chosen, masks)
    separate(mate, wide, mate_out, chosen, masks)
    turned[...] = observed[...].T
    start_out[...] = start[...]


def columns_kernel(factors, separated, wide):
    separate(factors, wide, separated, range(separated.shape[1] // LANES))


def image_kernel(*refs):
    arrived, (own, mate, observed, misfit, left) = refs[:-5], refs[-5:]
    for index, block in enumerate(arrived):
        spread_block(block[...], left, index)
    misfit[0] = times_transposed(left[...], own[...]) - observed[...]
    misfit[1] = times_transposed(left[...], mate[...])


def back_kernel(here, there, own, mate, *refs):
    outs, products = refs[:-1], refs[-1]
    for rows, factors in ((0, own), (1, mate)):
        misfit = (here[rows] + there[1 - rows]).astype(BF16)
        products[rows] = jnp.dot(misfit, factors[...], preferred_element_type=F32)
    for index, out in enumerate(outs):
        parts = [adjoint_block(products.at[rows], index).astype(F32) for rows in range(2)]
        out[...] = (parts[0] + parts[1]).astype(BF16)


def pack_kernel(*refs):
    for index, block in enumerate(refs[:-1]):
        refs[-1][index] = block[...]


def gradient_kernel(shifts, own, mate, factors, gradient, left):
    for blocks, chosen in zip((own, mate), both_shifts(shifts)):
        for index, tile in enumerate(chosen):
            spread_block(blocks[index], left, tile)
    gradient[...] = times_transposed(factors[...], left[...]).astype(BF16)


def step_kernel(factors, left, start, estimate):
    estimate[...] = start[...] - STEP_SIZE * times_transposed(factors[...], left[...])


def thin_out(values):
    return values - jnp.clip(values, -LEVEL, LEVEL)


def pair_kernel(factors, left, here, there, total, difference):
    scale = 1.0 / math.sqrt(2)
    estimate = here[...] - STEP_SIZE * times_transposed(factors[...], left[...])
    total[...] = (estimate + there[...]) * scale
    difference[...] = (estimate - there[...]) * scale


def shrink_pair_kernel(total, difference, gradient, out):
    scale = 1.0 / math.sqrt(2)
    step = (STEP_SIZE * scale) * gradient[...].astype(F32)
    out[...] = (thin_out(total[...] - step) + thin_out(difference[...] + step)) * scale


def shrink_kernel(band, *refs):
    tables, own, starts, gradients, out = refs[0], refs[1], refs[2 : band + 1], refs[band + 1 : -1], refs[-1]
    others = [start[...] - STEP_SIZE * gradient[...].astype(F32) for start, gradient in zip(starts, gradients)]
    estimates = [own[...], *others]
    scale = 1.0 / math.sqrt(band)
    half = out.shape[1] // 2
    lane = lax.broadcasted_iota(jnp.int32, (1, out.shape[1]), 1)
    turn = jnp.where(lane < half, -1.0, 1.0).astype(F32)
    turned = [pltpu.roll(estimate, half, 1) * turn for estimate in estimates]
    total = jnp.zeros_like(estimates[0])
    for time in range(band):
        sample = jnp.zeros_like(estimates[0])
        for index in range(band):
            sample += tables[0, index, time] * estimates[index] + tables[1, index, time] * turned[index]
        thinned = thin_out(sample * scale)
        total += tables[0, 0, time] * thinned - tables[1, 0, time] * (pltpu.roll(thinned, half, 1) * turn)
    out[...] = total * scale


def call(kernel, name, outs, inputs, scratch=(), flops=0, spaces=(), limit=VMEM_LIMIT):
    spaces = (*spaces, *[pltpu.VMEM] * (len(inputs) - len(spaces)))
    moved = sum(x.size * x.dtype.itemsize for x in [*inputs, *outs]) if flops else 0
    return pl.pallas_call(
        kernel,
        out_shape=outs,
        in_specs=[pl.BlockSpec(memory_space=space) for space in spaces],
        out_specs=[pl.BlockSpec(memory_space=pltpu.VMEM)] * len(outs),
        scratch_shapes=scratch,
        compiler_params=pltpu.CompilerParams(vmem_limit_bytes=limit),
        cost_estimate=pl.CostEstimate(flops=flops, bytes_accessed=moved, transcendentals=0),
        name=name,
    )(*inputs)


def to_mate(value):
    return lax.ppermute(value, "tile", [(i, i ^ 1) for i in range(lax.axis_size("tile"))])


def after(value, *others):
    return lax.optimization_barrier((value, *others))[0]


def exchange(sends, shifts, beside):
    count = lax.axis_size("tile")
    arrived = []
    for index, send in enumerate(sends):
        pairs = [(i, i ^ 2 * shifts[i % 2][index] ^ 1) for i in range(count)]
        arrived.append(lax.ppermute(send, "tile", pairs))
    return [after(arrived[0], *beside), *arrived[1:]]


def body(u_factors, v_factors, ranks, observed, start):
    count, band = lax.axis_size("tile"), lax.axis_size("freq")
    rows, tiles, width = u_factors.shape[1:]
    sources = start.shape[2]
    columns = tiles * width
    left_rows = u_factors.reshape(rows * tiles, width)
    right_rows = v_factors.reshape(rows * tiles, width)
    observed = observed.reshape(rows, sources)
    start = start.reshape(rows, sources)
    shifts = shifts_of(tiles)

    def shape(*dims, dtype=BF16):
        return jax.ShapeDtypeStruct(dims, dtype)

    members = tiles // 2
    wide = pltpu.VMEM((rows * tiles, width), F32)
    block = shape(sources // 2, width)
    blocks = shape(members, sources // 2, width)
    chosen = shape(rows, members * width)
    factor = shape(rows, columns)
    flops = 2 * rows * columns * sources

    raw_right, raw_start = to_mate(right_rows), to_mate(start)
    scratch = [wide, pltpu.VMEM((rows, members * width), BF16), pltpu.VMEM((sources, members * width), F32)]
    (parts,) = call(
        functools.partial(forward_kernel, shifts),
        "forward",
        [blocks],
        [start, right_rows],
        [
            pltpu.VMEM(start.shape, F32),
            pltpu.VMEM(right_rows.shape, BF16),
            pltpu.SemaphoreType.DMA((PIECES + 1,)),
            *scratch,
        ],
        spaces=[pltpu.HBM] * 2,
        limit=FIRST_LIMIT,
    )
    sends = call(
        functools.partial(join_kernel, shifts),
        "join",
        [block] * members,
        [parts, raw_start, raw_right],
        scratch,
        flops // 2,
    )
    left_rows = after(left_rows, sends[0])
    own_left, mate_left, turned, start = call(
        functools.partial(rows_kernel, shifts),
        "rows",
        [chosen, chosen, shape(sources, rows, dtype=F32), shape(rows, sources, dtype=F32)],
        [ranks, left_rows, to_mate(left_rows), after(observed, parts), after(start, parts)],
        [wide],
        spaces=[pltpu.SMEM],
    )
    starts = [start]
    for shift in range(1, band):
        starts.append(lax.ppermute(start, "freq", [(f, (f - shift) % band) for f in range(band)]))
    (misfit,) = call(
        image_kernel,
        "image",
        [shape(2, sources, rows, dtype=F32)],
        [*exchange(sends, shifts, [own_left, mate_left, turned]), own_left, mate_left, turned],
        [pltpu.VMEM((sources, members * width), BF16)],
        flops,
    )
    (mate_right,) = call(columns_kernel, "columns", [factor], [after(raw_right, misfit)], [wide])
    sends = call(
        back_kernel,
        "back",
        [block] * members,
        [misfit, to_mate(misfit), own_left, mate_left],
        [pltpu.VMEM((2, sources, members * width), F32)],
        flops,
    )
    (right,) = call(columns_kernel, "columns", [factor], [after(right_rows, sends[0])], [wide])
    (own,) = call(pack_kernel, "pack", [blocks], exchange(sends, shifts[::-1], [right, mate_right, *starts[1:]]))
    gradient, left = call(
        functools.partial(gradient_kernel, shifts),
        "gradient",
        [shape(rows, sources), shape(sources, columns)],
        [own, to_mate(own), mate_right],
        flops=flops,
    )
    gradients = []
    for shift in range(1, band):
        pairs = [(i * band + f, (i ^ 1) * band + (f - shift) % band) for i in range(count) for f in range(band)]
        gradients.append(lax.ppermute(gradient, ("tile", "freq"), pairs))
    result = shape(rows, sources, dtype=F32)
    if band == 2:
        halves = call(pair_kernel, "pair", [result] * 2, [right, left, *starts], flops=flops)
        (estimate,) = call(shrink_pair_kernel, "shrink", [result], [*halves, *gradients])
        return estimate[None]
    bands = jnp.arange(band, dtype=jnp.int32)
    phases = (bands[:, None] + lax.axis_index("freq")) * bands[None, :] % band
    phases = (2.0 * math.pi / band) * phases.astype(F32)
    tables = jnp.stack([jnp.cos(phases), jnp.sin(phases)])
    (estimate,) = call(step_kernel, "step", [result], [right, left, start], flops=flops)
    (estimate,) = call(
        functools.partial(shrink_kernel, band),
        "shrink",
        [result],
        [tables, estimate, *starts[1:], *gradients],
        spaces=[pltpu.SMEM],
    )
    return estimate[None]


def solution(mesh):
    in_specs = (
        P("freq", "tile", None, None),
        P("freq", "tile", None, None),
        P("freq", None, None),
        P("freq", "tile", None),
        P("freq", "tile", None),
    )
    out_specs = P("freq", "tile", None)
    return jax.shard_map(body, mesh=mesh, in_specs=in_specs, out_specs=out_specs, check_vma=False)
```

```python
import functools
import math

import jax
import jax.numpy as jnp
from jax import lax
from jax.experimental import pallas as pl
from jax.experimental.pallas import tpu as pltpu
from jax.sharding import PartitionSpec as P

STEP_SIZE = 0.2
LEVEL = 0.5
LANES = 128
VMEM_LIMIT = 32 * 1024 * 1024
FIRST_LIMIT = 55050 * 1024
PIECES = 4
F32 = jnp.float32
BF16 = jnp.bfloat16


def shifts_of(chips):
    even = list(range(chips - 2, -1, -2))
    odd = [shift + 1 for shift in even]
    even[-2], odd[-1] = odd[-1], even[-2]
    return [even, odd]


def place():
    position = lax.axis_index("tile")
    return position // 2, position % 2


def columns_of(tile):
    return pl.ds(pl.multiple_of(tile * LANES, LANES), LANES)


def both_shifts(shifts):
    chip, core = place()
    pairs = list(zip(*shifts))
    own = [chip ^ jnp.where(core == 0, first, second) for first, second in pairs]
    mate = [chip ^ jnp.where(core == 0, second, first) for first, second in pairs]
    return own, mate


def signs(rows):
    lane = lax.broadcasted_iota(jnp.int32, (rows, LANES), 1)
    return jnp.where(lane < LANES // 2, 1.0, -1.0).astype(F32)


def separate(source, wide, target, chosen, masks=None):
    rows = target.shape[0]
    tiles = source.shape[0] // rows
    wide[...] = source[...].astype(F32)
    for index, tile in enumerate(chosen):
        part = wide[pl.ds(tile, rows, stride=tiles), :]
        if masks is not None:
            part = jnp.where(masks[index], part, 0.0)
        target[:, index * LANES : (index + 1) * LANES] = part.astype(BF16)


def adjoint_block(product, tile):
    half = product.shape[0] // 2
    real, imaginary = product[:half, columns_of(tile)], product[half:, columns_of(tile)]
    return (real * signs(half) + pltpu.roll(imaginary, LANES // 2, 1)).astype(BF16)


def spread_block(block, left, tile):
    half = block.shape[0]
    block = block.astype(F32)
    left[:half, columns_of(tile)] = (block * signs(half)).astype(BF16)
    left[half:, columns_of(tile)] = pltpu.roll(block, LANES // 2, 1).astype(BF16)


def times_transposed(left, right):
    return lax.dot_general(left, right, (((1,), (1,)), ((), ())), preferred_element_type=F32)


def block_parts(shifts, start, separated, product):
    product[...] = jnp.dot(start[...].T.astype(BF16), separated[...], preferred_element_type=F32)
    return [adjoint_block(product, index) for index in range(len(shifts[0]))]


def forward_kernel(shifts, start, factors, parts, start_here, factors_here, sems, wide, separated, product):
    pieces = sems.shape[0] - 1
    rows = start.shape[0]
    tiles = factors.shape[0] // rows
    chosen, _ = both_shifts(shifts)
    load_start = pltpu.make_async_copy(start, start_here, sems.at[pieces])
    load_start.start()
    loads = []
    for piece in range(pieces):
        at = pl.ds(piece * (rows * tiles // pieces), rows * tiles // pieces)
        loads.append(pltpu.make_async_copy(factors.at[at], factors_here.at[at], sems.at[piece]))
        loads[-1].start()
    load_start.wait()
    for piece, load in enumerate(loads):
        at = pl.ds(piece * (rows * tiles // pieces), rows * tiles // pieces)
        load.wait()
        separate(
            factors_here.at[at], wide.at[at], separated.at[pl.ds(piece * (rows // pieces), rows // pieces)], chosen
        )
    for index, block in enumerate(block_parts(shifts, start_here, separated, product)):
        parts[index] = block


def join_kernel(shifts, parts, start, factors, *refs):
    outs, (wide, separated, product) = refs[:-3], refs[-3:]
    chosen, _ = both_shifts(shifts)
    separate(factors, wide, separated, chosen)
    for index, block in enumerate(block_parts(shifts, start, separated, product)):
        outs[index][...] = (parts[index].astype(F32) + block.astype(F32)).astype(BF16)


def rows_kernel(shifts, ranks, own, mate, observed, own_out, mate_out, turned, wide):
    chip, _ = place()
    _, chosen = both_shifts(shifts)
    lane = lax.broadcasted_iota(jnp.int32, (1, LANES), 1) % (LANES // 2)
    masks = [lane < ranks[0, chip, tile] for tile in chosen]
    separate(own, wide, own_out, chosen, masks)
    separate(mate, wide, mate_out, chosen, masks)
    turned[...] = observed[...].T


def columns_kernel(factors, separated, wide):
    separate(factors, wide, separated, range(separated.shape[1] // LANES))


def image_kernel(*refs):
    arrived, (own, mate, observed, misfit, sent, left) = refs[:-6], refs[-6:]
    for index, block in enumerate(arrived):
        spread_block(block[...], left, index)
    misfit[0] = times_transposed(left[...], own[...]) - observed[...]
    misfit[1] = times_transposed(left[...], mate[...])
    sent[...] = misfit[...].astype(BF16)


def back_kernel(here, there, own, mate, *refs):
    outs, products = refs[:-1], refs[-1]
    for rows, factors in ((0, own), (1, mate)):
        misfit = (here[rows] + there[1 - rows].astype(F32)).astype(BF16)
        products[rows] = jnp.dot(misfit, factors[...], preferred_element_type=F32)
    for index, out in enumerate(outs):
        parts = [adjoint_block(products.at[rows], index).astype(F32) for rows in range(2)]
        out[...] = (parts[0] + parts[1]).astype(BF16)


def pack_kernel(*refs):
    for index, block in enumerate(refs[:-1]):
        refs[-1][index] = block[...]


def gradient_kernel(shifts, own, mate, factors, gradient, left):
    for blocks, chosen in zip((own, mate), both_shifts(shifts)):
        for index, tile in enumerate(chosen):
            spread_block(blocks[index], left, tile)
    gradient[...] = times_transposed(factors[...], left[...]).astype(BF16)


def step_kernel(factors, left, start, estimate):
    estimate[...] = start[...] - STEP_SIZE * times_transposed(factors[...], left[...])


def thin_out(values):
    return values - jnp.clip(values, -LEVEL, LEVEL)


def pair_kernel(factors, left, here, there, total, difference):
    scale = 1.0 / math.sqrt(2)
    estimate = here[...] - STEP_SIZE * times_transposed(factors[...], left[...])
    total[...] = (estimate + there[...]) * scale
    difference[...] = (estimate - there[...]) * scale


def shrink_pair_kernel(total, difference, gradient, out):
    scale = 1.0 / math.sqrt(2)
    step = (STEP_SIZE * scale) * gradient[...].astype(F32)
    out[...] = (thin_out(total[...] - step) + thin_out(difference[...] + step)) * scale


def shrink_kernel(band, *refs):
    tables, own, starts, gradients, out = refs[0], refs[1], refs[2 : band + 1], refs[band + 1 : -1], refs[-1]
    others = [start[...] - STEP_SIZE * gradient[...].astype(F32) for start, gradient in zip(starts, gradients)]
    estimates = [own[...], *others]
    scale = 1.0 / math.sqrt(band)
    half = out.shape[1] // 2
    lane = lax.broadcasted_iota(jnp.int32, (1, out.shape[1]), 1)
    turn = jnp.where(lane < half, -1.0, 1.0).astype(F32)
    turned = [pltpu.roll(estimate, half, 1) * turn for estimate in estimates]
    total = jnp.zeros_like(estimates[0])
    for time in range(band):
        sample = jnp.zeros_like(estimates[0])
        for index in range(band):
            sample += tables[0, index, time] * estimates[index] + tables[1, index, time] * turned[index]
        thinned = thin_out(sample * scale)
        total += tables[0, 0, time] * thinned - tables[1, 0, time] * (pltpu.roll(thinned, half, 1) * turn)
    out[...] = total * scale


def call(kernel, name, outs, inputs, scratch=(), flops=0, spaces=(), limit=VMEM_LIMIT):
    spaces = (*spaces, *[pltpu.VMEM] * (len(inputs) - len(spaces)))
    moved = sum(x.size * x.dtype.itemsize for x in [*inputs, *outs]) if flops else 0
    return pl.pallas_call(
        kernel,
        out_shape=outs,
        in_specs=[pl.BlockSpec(memory_space=space) for space in spaces],
        out_specs=[pl.BlockSpec(memory_space=pltpu.VMEM)] * len(outs),
        scratch_shapes=scratch,
        compiler_params=pltpu.CompilerParams(vmem_limit_bytes=limit),
        cost_estimate=pl.CostEstimate(flops=flops, bytes_accessed=moved, transcendentals=0),
        name=name,
    )(*inputs)


def to_mate(value):
    return lax.ppermute(value, "tile", [(i, i ^ 1) for i in range(lax.axis_size("tile"))])


def across(value, shift):
    count, band = lax.axis_size("tile"), lax.axis_size("freq")
    pairs = [(i * band + f, (i ^ 1) * band + (f - shift) % band) for i in range(count) for f in range(band)]
    return lax.ppermute(value, ("tile", "freq"), pairs)


def after(value, *others):
    return lax.optimization_barrier((value, *others))[0]


def exchange(sends, shifts, beside):
    count = lax.axis_size("tile")
    arrived = []
    for index, send in enumerate(sends):
        pairs = [(i, i ^ 2 * shifts[i % 2][index] ^ 1) for i in range(count)]
        arrived.append(lax.ppermute(send, "tile", pairs))
    return [after(arrived[0], *beside), *arrived[1:]]


def body(u_factors, v_factors, ranks, observed, start):
    band = lax.axis_size("freq")
    rows, tiles, width = u_factors.shape[1:]
    sources = start.shape[2]
    columns = tiles * width
    left_rows = u_factors.reshape(rows * tiles, width)
    right_rows = v_factors.reshape(rows * tiles, width)
    observed = observed.reshape(rows, sources)
    start = start.reshape(rows, sources)
    shifts = shifts_of(tiles)

    def shape(*dims, dtype=BF16):
        return jax.ShapeDtypeStruct(dims, dtype)

    members = tiles // 2
    wide = pltpu.VMEM((rows * tiles, width), F32)
    block = shape(sources // 2, width)
    blocks = shape(members, sources // 2, width)
    chosen = shape(rows, members * width)
    factor = shape(rows, columns)
    flops = 2 * rows * columns * sources

    raw_right, raw_start = to_mate(right_rows), to_mate(start)
    scratch = [wide, pltpu.VMEM((rows, members * width), BF16), pltpu.VMEM((sources, members * width), F32)]
    (parts,) = call(
        functools.partial(forward_kernel, shifts),
        "forward",
        [blocks],
        [start, right_rows],
        [
            pltpu.VMEM(start.shape, F32),
            pltpu.VMEM(right_rows.shape, BF16),
            pltpu.SemaphoreType.DMA((PIECES + 1,)),
            *scratch,
        ],
        spaces=[pltpu.HBM] * 2,
        limit=FIRST_LIMIT,
    )
    sends = call(
        functools.partial(join_kernel, shifts),
        "join",
        [block] * members,
        [parts, raw_start, raw_right],
        scratch,
        flops // 2,
    )
    left_rows = after(left_rows, sends[0])
    own_left, mate_left, turned = call(
        functools.partial(rows_kernel, shifts),
        "rows",
        [chosen, chosen, shape(sources, rows, dtype=F32)],
        [ranks, left_rows, to_mate(left_rows), after(observed, parts)],
        [wide],
        spaces=[pltpu.SMEM],
    )
    misfit, sent = call(
        image_kernel,
        "image",
        [shape(2, sources, rows, dtype=F32), shape(2, sources, rows)],
        [*exchange(sends, shifts, [own_left, mate_left, turned]), own_left, mate_left, turned],
        [pltpu.VMEM((sources, members * width), BF16)],
        flops,
    )
    starts = [start]
    for shift in range(1, band):
        starts.append(across(after(raw_start, own_left), shift))
    (mate_right,) = call(columns_kernel, "columns", [factor], [after(raw_right, sends[0])], [wide])
    sends = call(
        back_kernel,
        "back",
        [block] * members,
        [misfit, to_mate(sent), own_left, mate_left],
        [pltpu.VMEM((2, sources, members * width), F32)],
        flops,
    )
    (own,) = call(pack_kernel, "pack", [blocks], exchange(sends, shifts[::-1], [mate_right, *starts[1:]]))
    gradient, left = call(
        functools.partial(gradient_kernel, shifts),
        "gradient",
        [shape(rows, sources), shape(sources, columns)],
        [own, to_mate(own), mate_right],
        flops=flops,
    )
    (right,) = call(columns_kernel, "columns", [factor], [after(right_rows, gradient)], [wide])
    gradients = []
    for shift in range(1, band):
        gradients.append(across(gradient, shift))
    result = shape(rows, sources, dtype=F32)
    if band == 2:
        halves = call(pair_kernel, "pair", [result] * 2, [right, left, *starts], flops=flops)
        (estimate,) = call(shrink_pair_kernel, "shrink", [result], [*halves, *gradients])
        return estimate[None]
    bands = jnp.arange(band, dtype=jnp.int32)
    phases = (bands[:, None] + lax.axis_index("freq")) * bands[None, :] % band
    phases = (2.0 * math.pi / band) * phases.astype(F32)
    tables = jnp.stack([jnp.cos(phases), jnp.sin(phases)])
    (estimate,) = call(step_kernel, "step", [result], [right, left, start], flops=flops)
    (estimate,) = call(
        functools.partial(shrink_kernel, band),
        "shrink",
        [result],
        [tables, estimate, *starts[1:], *gradients],
        spaces=[pltpu.SMEM],
    )
    return estimate[None]


def solution(mesh):
    in_specs = (
        P("freq", "tile", None, None),
        P("freq", "tile", None, None),
        P("freq", None, None),
        P("freq", "tile", None),
        P("freq", "tile", None),
    )
    out_specs = P("freq", "tile", None)
    return jax.shard_map(body, mesh=mesh, in_specs=in_specs, out_specs=out_specs, check_vma=False)
```

```python
import functools
import math

import jax
import jax.numpy as jnp
from jax import lax
from jax.experimental import pallas as pl
from jax.experimental.pallas import tpu as pltpu
from jax.sharding import PartitionSpec as P

STEP_SIZE = 0.2
LEVEL = 0.5
LANES = 128
VMEM_LIMIT = 32 * 1024 * 1024
FIRST_LIMIT = 55050 * 1024
PIECES = 4
HIDE = 256
F32 = jnp.float32
BF16 = jnp.bfloat16


def shifts_of(chips):
    even = list(range(chips - 2, -1, -2))
    odd = [shift + 1 for shift in even]
    even[-2], odd[-1] = odd[-1], even[-2]
    return [even, odd]


def place():
    position = lax.axis_index("tile")
    return position // 2, position % 2


def columns_of(tile):
    return pl.ds(pl.multiple_of(tile * LANES, LANES), LANES)


def both_shifts(shifts):
    chip, core = place()
    pairs = list(zip(*shifts))
    own = [chip ^ jnp.where(core == 0, first, second) for first, second in pairs]
    mate = [chip ^ jnp.where(core == 0, second, first) for first, second in pairs]
    return own, mate


def signs(rows):
    lane = lax.broadcasted_iota(jnp.int32, (rows, LANES), 1)
    return jnp.where(lane < LANES // 2, 1.0, -1.0).astype(F32)


def separate(source, wide, target, chosen, masks=None):
    rows = target.shape[0]
    tiles = source.shape[0] // rows
    wide[...] = source[...].astype(F32)
    for index, tile in enumerate(chosen):
        part = wide[pl.ds(tile, rows, stride=tiles), :]
        if masks is not None:
            part = jnp.where(masks[index], part, 0.0)
        target[:, index * LANES : (index + 1) * LANES] = part.astype(BF16)


def adjoint_block(product, tile):
    half = product.shape[0] // 2
    real, imaginary = product[:half, columns_of(tile)], product[half:, columns_of(tile)]
    return (real * signs(half) + pltpu.roll(imaginary, LANES // 2, 1)).astype(BF16)


def spread_block(block, left, tile):
    half = block.shape[0]
    block = block.astype(F32)
    left[:half, columns_of(tile)] = (block * signs(half)).astype(BF16)
    left[half:, columns_of(tile)] = pltpu.roll(block, LANES // 2, 1).astype(BF16)


def times_transposed(left, right):
    return lax.dot_general(left, right, (((1,), (1,)), ((), ())), preferred_element_type=F32)


def forward_kernel(shifts, start, factors, keep, give, start_here, factors_here, wide, separated, product, sems):
    pieces = sems.shape[0] - 1
    rows, columns = separated.shape
    tiles = columns // LANES
    load_start = pltpu.make_async_copy(start, start_here, sems.at[pieces])
    load_start.start()
    loads = []
    for piece in range(pieces):
        at = pl.ds(piece * (rows * tiles // pieces), rows * tiles // pieces)
        loads.append(pltpu.make_async_copy(factors.at[at], factors_here.at[at], sems.at[piece]))
        loads[-1].start()
    load_start.wait()
    values = start_here[...].T.astype(BF16)
    for piece, load in enumerate(loads):
        at = pl.ds(piece * (rows * tiles // pieces), rows * tiles // pieces)
        load.wait()
        separate(
            factors_here.at[at], wide.at[at], separated.at[pl.ds(piece * (rows // pieces), rows // pieces)], range(tiles)
        )
    product[...] = jnp.dot(values, separated[...], preferred_element_type=F32)
    for out, chosen in zip((keep, give), both_shifts(shifts)):
        for index, tile in enumerate(chosen):
            out[index] = adjoint_block(product, tile)


def add_kernel(keep, arrived, *outs):
    for index, out in enumerate(outs):
        out[...] = (keep[index].astype(F32) + arrived[index].astype(F32)).astype(BF16)


def rows_kernel(shifts, ranks, own, mate, observed, start, own_out, mate_out, turned, start_out, wide):
    chip, _ = place()
    _, chosen = both_shifts(shifts)
    lane = lax.broadcasted_iota(jnp.int32, (1, LANES), 1) % (LANES // 2)
    masks = [lane < ranks[0, chip, tile] for tile in chosen]
    separate(own, wide, own_out, chosen, masks)
    separate(mate, wide, mate_out, chosen, masks)
    turned[...] = observed[...].T
    start_out[...] = start[...]


def columns_kernel(factors, separated, wide):
    separate(factors, wide, separated, range(separated.shape[1] // LANES))


def image_kernel(*refs):
    arrived, (own, mate, observed, misfit, left) = refs[:-5], refs[-5:]
    for index, block in enumerate(arrived):
        spread_block(block[...], left, index)
    misfit[0] = times_transposed(left[...], own[...]) - observed[...]
    misfit[1] = times_transposed(left[...], mate[...])


def back_kernel(here, there, own, mate, *refs):
    outs, products = refs[:-1], refs[-1]
    for rows, factors in ((0, own), (1, mate)):
        misfit = (here[rows] + there[1 - rows]).astype(BF16)
        products[rows] = jnp.dot(misfit, factors[...], preferred_element_type=F32)
    for index, out in enumerate(outs):
        parts = [adjoint_block(products.at[rows], index).astype(F32) for rows in range(2)]
        out[...] = (parts[0] + parts[1]).astype(BF16)


def pack_kernel(*refs):
    for index, block in enumerate(refs[:-1]):
        refs[-1][index] = block[...]


def gradient_kernel(shifts, own, mate, factors, gradient, left):
    for blocks, chosen in zip((own, mate), both_shifts(shifts)):
        for index, tile in enumerate(chosen):
            spread_block(blocks[index], left, tile)
    gradient[...] = times_transposed(factors[...], left[...]).astype(BF16)


def step_kernel(factors, left, start, estimate):
    estimate[...] = start[...] - STEP_SIZE * times_transposed(factors[...], left[...])


def thin_out(values):
    return values - jnp.clip(values, -LEVEL, LEVEL)


def pair_kernel(factors, left, here, there, total, difference):
    scale = 1.0 / math.sqrt(2)
    estimate = here[...] - STEP_SIZE * times_transposed(factors[...], left[...])
    total[...] = (estimate + there[...]) * scale
    difference[...] = (estimate - there[...]) * scale


def shrink_pair_kernel(total, difference, gradient, out):
    scale = 1.0 / math.sqrt(2)
    step = (STEP_SIZE * scale) * gradient[...].astype(F32)
    out[...] = (thin_out(total[...] - step) + thin_out(difference[...] + step)) * scale


def shrink_kernel(band, *refs):
    tables, own, starts, gradients, out = refs[0], refs[1], refs[2 : band + 1], refs[band + 1 : -1], refs[-1]
    others = [start[...] - STEP_SIZE * gradient[...].astype(F32) for start, gradient in zip(starts, gradients)]
    estimates = [own[...], *others]
    scale = 1.0 / math.sqrt(band)
    half = out.shape[1] // 2
    lane = lax.broadcasted_iota(jnp.int32, (1, out.shape[1]), 1)
    turn = jnp.where(lane < half, -1.0, 1.0).astype(F32)
    turned = [pltpu.roll(estimate, half, 1) * turn for estimate in estimates]
    total = jnp.zeros_like(estimates[0])
    for time in range(band):
        sample = jnp.zeros_like(estimates[0])
        for index in range(band):
            sample += tables[0, index, time] * estimates[index] + tables[1, index, time] * turned[index]
        thinned = thin_out(sample * scale)
        total += tables[0, 0, time] * thinned - tables[1, 0, time] * (pltpu.roll(thinned, half, 1) * turn)
    out[...] = total * scale


def call(kernel, name, outs, inputs, scratch=(), flops=0, spaces=(), limit=VMEM_LIMIT):
    spaces = (*spaces, *[pltpu.VMEM] * (len(inputs) - len(spaces)))
    moved = sum(x.size * x.dtype.itemsize for x in [*inputs, *outs]) if flops else 0
    return pl.pallas_call(
        kernel,
        out_shape=outs,
        in_specs=[pl.BlockSpec(memory_space=space) for space in spaces],
        out_specs=[pl.BlockSpec(memory_space=pltpu.VMEM)] * len(outs),
        scratch_shapes=scratch,
        compiler_params=pltpu.CompilerParams(vmem_limit_bytes=limit),
        cost_estimate=pl.CostEstimate(flops=flops, bytes_accessed=moved, transcendentals=0),
        name=name,
    )(*inputs)


def to_mate(value):
    return lax.ppermute(value, "tile", [(i, i ^ 1) for i in range(lax.axis_size("tile"))])


def across(value, shift):
    count, band = lax.axis_size("tile"), lax.axis_size("freq")
    pairs = [(i * band + f, (i ^ 1) * band + (f - shift) % band) for i in range(count) for f in range(band)]
    return lax.ppermute(value, ("tile", "freq"), pairs)


def after(value, *others):
    return lax.optimization_barrier((value, *others))[0]


def exchange(sends, shifts, beside):
    count = lax.axis_size("tile")
    arrived = []
    for index, send in enumerate(sends):
        pairs = [(i, i ^ 2 * shifts[i % 2][index] ^ 1) for i in range(count)]
        arrived.append(lax.ppermute(send, "tile", pairs))
    return [after(arrived[0], *beside), *arrived[1:]]


def body(u_factors, v_factors, ranks, observed, start):
    band = lax.axis_size("freq")
    rows, tiles, width = u_factors.shape[1:]
    sources = start.shape[2]
    columns = tiles * width
    left_rows = u_factors.reshape(rows * tiles, width)
    right_rows = v_factors.reshape(rows * tiles, width)
    observed = observed.reshape(rows, sources)
    start = start.reshape(rows, sources)
    shifts = shifts_of(tiles)

    def shape(*dims, dtype=BF16):
        return jax.ShapeDtypeStruct(dims, dtype)

    members = tiles // 2
    wide = pltpu.VMEM((rows * tiles, width), F32)
    block = shape(sources // 2, width)
    blocks = shape(members, sources // 2, width)
    chosen = shape(rows, members * width)
    factor = shape(rows, columns)
    flops = 2 * rows * columns * sources

    keep, give = call(
        functools.partial(forward_kernel, shifts),
        "forward",
        [blocks, blocks],
        [start, right_rows],
        [
            pltpu.VMEM(start.shape, F32),
            pltpu.VMEM(right_rows.shape, BF16),
            wide,
            pltpu.VMEM((rows, columns), BF16),
            pltpu.VMEM((sources, columns), F32),
            pltpu.SemaphoreType.DMA((PIECES + 1,)),
        ],
        flops,
        [pltpu.HBM] * 2,
        FIRST_LIMIT,
    )
    sends = call(add_kernel, "add", [block] * members, [keep, to_mate(give)], flops=HIDE * flops)
    mate_left = to_mate(after(left_rows, give))
    own_left, mate_left, turned, start = call(
        functools.partial(rows_kernel, shifts),
        "rows",
        [chosen, chosen, shape(sources, rows, dtype=F32), shape(rows, sources, dtype=F32)],
        [ranks, after(left_rows, give), mate_left, after(observed, give), after(start, give)],
        [wide],
        spaces=[pltpu.SMEM],
    )
    (misfit,) = call(
        image_kernel,
        "image",
        [shape(2, sources, rows, dtype=F32)],
        [*exchange(sends, shifts, [own_left, mate_left, turned]), own_left, mate_left, turned],
        [pltpu.VMEM((sources, members * width), BF16)],
        flops,
    )
    starts = [start]
    for shift in range(1, band):
        starts.append(lax.ppermute(start, "freq", [(f, (f - shift) % band) for f in range(band)]))
    mate_right = to_mate(after(right_rows, misfit))
    (mate_right,) = call(columns_kernel, "columns", [factor], [mate_right], [wide])
    sends = call(
        back_kernel,
        "back",
        [block] * members,
        [misfit, to_mate(misfit), own_left, mate_left],
        [pltpu.VMEM((2, sources, members * width), F32)],
        HIDE * flops,
    )
    (own,) = call(pack_kernel, "pack", [blocks], exchange(sends, shifts[::-1], [mate_right, *starts[1:]]))
    gradient, left = call(
        functools.partial(gradient_kernel, shifts),
        "gradient",
        [shape(rows, sources), shape(sources, columns)],
        [own, to_mate(own), mate_right],
        flops=flops,
    )
    (right,) = call(columns_kernel, "columns", [factor], [after(right_rows, gradient)], [wide])
    gradients = []
    for shift in range(1, band):
        gradients.append(across(gradient, shift))
    result = shape(rows, sources, dtype=F32)
    if band == 2:
        halves = call(pair_kernel, "pair", [result] * 2, [right, left, *starts], flops=flops)
        (estimate,) = call(shrink_pair_kernel, "shrink", [result], [*halves, *gradients])
        return estimate[None]
    bands = jnp.arange(band, dtype=jnp.int32)
    phases = (bands[:, None] + lax.axis_index("freq")) * bands[None, :] % band
    phases = (2.0 * math.pi / band) * phases.astype(F32)
    tables = jnp.stack([jnp.cos(phases), jnp.sin(phases)])
    (estimate,) = call(step_kernel, "step", [result], [right, left, start], flops=flops)
    (estimate,) = call(
        functools.partial(shrink_kernel, band),
        "shrink",
        [result],
        [tables, estimate, *starts[1:], *gradients],
        spaces=[pltpu.SMEM],
    )
    return estimate[None]


def solution(mesh):
    in_specs = (
        P("freq", "tile", None, None),
        P("freq", "tile", None, None),
        P("freq", None, None),
        P("freq", "tile", None),
        P("freq", "tile", None),
    )
    out_specs = P("freq", "tile", None)
    return jax.shard_map(body, mesh=mesh, in_specs=in_specs, out_specs=out_specs, check_vma=False)
```

```python
import functools
import math

import jax
import jax.numpy as jnp
from jax import lax
from jax.experimental import pallas as pl
from jax.experimental.pallas import tpu as pltpu
from jax.sharding import PartitionSpec as P

STEP_SIZE = 0.2
LEVEL = 0.5
LANES = 128
VMEM_LIMIT = 32 * 1024 * 1024
FIRST_LIMIT = 55050 * 1024
PIECES = 4
HIDE = 256
F32 = jnp.float32
BF16 = jnp.bfloat16


def shifts_of(chips):
    even = list(range(chips - 2, -1, -2))
    odd = [shift + 1 for shift in even]
    even[-2], odd[-1] = odd[-1], even[-2]
    return [even, odd]


def place():
    position = lax.axis_index("tile")
    return position // 2, position % 2


def columns_of(tile):
    return pl.ds(pl.multiple_of(tile * LANES, LANES), LANES)


def both_shifts(shifts):
    chip, core = place()
    pairs = list(zip(*shifts))
    own = [chip ^ jnp.where(core == 0, first, second) for first, second in pairs]
    mate = [chip ^ jnp.where(core == 0, second, first) for first, second in pairs]
    return own, mate


def signs(rows):
    lane = lax.broadcasted_iota(jnp.int32, (rows, LANES), 1)
    return jnp.where(lane < LANES // 2, 1.0, -1.0).astype(F32)


def pick(wide, target, chosen, masks=None):
    rows = target.shape[0]
    tiles = wide.shape[0] // rows
    for index, tile in enumerate(chosen):
        part = wide[pl.ds(tile, rows, stride=tiles), :]
        if masks is not None:
            part = jnp.where(masks[index], part, 0.0)
        target[:, index * LANES : (index + 1) * LANES] = part.astype(BF16)


def separate(source, wide, target, chosen, masks=None):
    wide[...] = source[...].astype(F32)
    pick(wide, target, chosen, masks)


def adjoint_block(product, tile):
    half = product.shape[0] // 2
    real, imaginary = product[:half, columns_of(tile)], product[half:, columns_of(tile)]
    return (real * signs(half) + pltpu.roll(imaginary, LANES // 2, 1)).astype(BF16)


def spread_block(block, left, tile):
    half = block.shape[0]
    block = block.astype(F32)
    left[:half, columns_of(tile)] = (block * signs(half)).astype(BF16)
    left[half:, columns_of(tile)] = pltpu.roll(block, LANES // 2, 1).astype(BF16)


def times_transposed(left, right):
    return lax.dot_general(left, right, (((1,), (1,)), ((), ())), preferred_element_type=F32)


def forward_kernel(shifts, start, factors, keep, give, start_here, factors_here, wide, separated, product, sems):
    pieces = sems.shape[0] - 1
    rows, columns = separated.shape
    tiles = columns // LANES
    load_start = pltpu.make_async_copy(start, start_here, sems.at[pieces])
    load_start.start()
    loads = []
    for piece in range(pieces):
        at = pl.ds(piece * (rows * tiles // pieces), rows * tiles // pieces)
        loads.append(pltpu.make_async_copy(factors.at[at], factors_here.at[at], sems.at[piece]))
        loads[-1].start()
    load_start.wait()
    values = start_here[...].T.astype(BF16)
    for piece, load in enumerate(loads):
        at = pl.ds(piece * (rows * tiles // pieces), rows * tiles // pieces)
        load.wait()
        separate(
            factors_here.at[at], wide.at[at], separated.at[pl.ds(piece * (rows // pieces), rows // pieces)], range(tiles)
        )
    product[...] = jnp.dot(values, separated[...], preferred_element_type=F32)
    for out, chosen in zip((keep, give), both_shifts(shifts)):
        for index, tile in enumerate(chosen):
            out[index] = adjoint_block(product, tile)


def add_kernel(keep, arrived, *outs):
    for index, out in enumerate(outs):
        out[...] = (keep[index].astype(F32) + arrived[index].astype(F32)).astype(BF16)


def rows_kernel(shifts, ranks, own, mate, observed, start, both, turned, start_out, wide):
    chip, _ = place()
    _, chosen = both_shifts(shifts)
    rows = both.shape[0] // 2
    lane = lax.broadcasted_iota(jnp.int32, (1, LANES), 1) % (LANES // 2)
    masks = [lane < ranks[0, chip, tile] for tile in chosen]
    separate(own, wide, both.at[:rows], chosen, masks)
    separate(mate, wide, both.at[rows:], chosen, masks)
    turned[...] = observed[...].T
    start_out[...] = start[...]


def columns_kernel(shifts, factors, own, other, wide):
    chosen, rest = both_shifts(shifts)
    separate(factors, wide, own, chosen)
    pick(wide, other, rest)


def early_kernel(first, second, factors, observed, misfit, left):
    for index, block in enumerate((first, second)):
        spread_block(block[...], left, index)
    rows = observed.shape[1]
    image = times_transposed(left[...], factors[:, : left.shape[1]])
    misfit[:, :rows] = image[:, :rows] - observed[...]
    misfit[:, rows:] = image[:, rows:]


def image_kernel(*refs):
    blocks, (early, factors, misfit, left) = refs[:-4], refs[-4:]
    for index, block in enumerate(blocks):
        spread_block(block[...], left, index)
    misfit[...] = early[...] + times_transposed(left[...], factors[:, -left.shape[1] :])


def back_kernel(here, there, factors, *refs):
    outs, (misfit, product) = refs[:-2], refs[-2:]
    rows = here.shape[1] // 2
    misfit[:, :rows] = (here[:, :rows] + there[:, rows:]).astype(BF16)
    misfit[:, rows:] = (here[:, rows:] + there[:, :rows]).astype(BF16)
    product[...] = jnp.dot(misfit[...], factors[...], preferred_element_type=F32)
    for index, out in enumerate(outs):
        out[...] = adjoint_block(product, index)


def pack_kernel(*refs):
    for index, block in enumerate(refs[:-1]):
        refs[-1][index] = block[...]


def part_kernel(blocks, factors, part, left):
    for index in range(blocks.shape[0]):
        spread_block(blocks[index], left, index)
    part[...] = times_transposed(factors[...], left[...])


def gradient_kernel(part, blocks, factors, gradient, left):
    for index in range(blocks.shape[0]):
        spread_block(blocks[index], left, index)
    gradient[...] = (part[...] + times_transposed(factors[...], left[...])).astype(BF16)


def step_kernel(own, other, own_left, other_left, start, estimate):
    gradient = times_transposed(own[...], own_left[...]) + times_transposed(other[...], other_left[...])
    estimate[...] = start[...] - STEP_SIZE * gradient


def pair_kernel(own, other, own_left, other_left, here, there, total, difference):
    scale = 1.0 / math.sqrt(2)
    gradient = times_transposed(own[...], own_left[...]) + times_transposed(other[...], other_left[...])
    estimate = here[...] - STEP_SIZE * gradient
    total[...] = (estimate + there[...]) * scale
    difference[...] = (estimate - there[...]) * scale


def thin_out(values):
    return values - jnp.clip(values, -LEVEL, LEVEL)


def shrink_pair_kernel(total, difference, gradient, out):
    scale = 1.0 / math.sqrt(2)
    step = (STEP_SIZE * scale) * gradient[...].astype(F32)
    out[...] = (thin_out(total[...] - step) + thin_out(difference[...] + step)) * scale


def shrink_kernel(band, *refs):
    tables, own, starts, gradients, out = refs[0], refs[1], refs[2 : band + 1], refs[band + 1 : -1], refs[-1]
    others = [start[...] - STEP_SIZE * gradient[...].astype(F32) for start, gradient in zip(starts, gradients)]
    estimates = [own[...], *others]
    scale = 1.0 / math.sqrt(band)
    half = out.shape[1] // 2
    lane = lax.broadcasted_iota(jnp.int32, (1, out.shape[1]), 1)
    turn = jnp.where(lane < half, -1.0, 1.0).astype(F32)
    turned = [pltpu.roll(estimate, half, 1) * turn for estimate in estimates]
    total = jnp.zeros_like(estimates[0])
    for time in range(band):
        sample = jnp.zeros_like(estimates[0])
        for index in range(band):
            sample += tables[0, index, time] * estimates[index] + tables[1, index, time] * turned[index]
        thinned = thin_out(sample * scale)
        total += tables[0, 0, time] * thinned - tables[1, 0, time] * (pltpu.roll(thinned, half, 1) * turn)
    out[...] = total * scale


def call(kernel, name, outs, inputs, scratch=(), flops=0, spaces=(), limit=VMEM_LIMIT):
    spaces = (*spaces, *[pltpu.VMEM] * (len(inputs) - len(spaces)))
    moved = sum(x.size * x.dtype.itemsize for x in [*inputs, *outs]) if flops else 0
    return pl.pallas_call(
        kernel,
        out_shape=outs,
        in_specs=[pl.BlockSpec(memory_space=space) for space in spaces],
        out_specs=[pl.BlockSpec(memory_space=pltpu.VMEM)] * len(outs),
        scratch_shapes=scratch,
        compiler_params=pltpu.CompilerParams(vmem_limit_bytes=limit),
        cost_estimate=pl.CostEstimate(flops=flops, bytes_accessed=moved, transcendentals=0),
        name=name,
    )(*inputs)


def to_mate(value):
    return lax.ppermute(value, "tile", [(i, i ^ 1) for i in range(lax.axis_size("tile"))])


def across(value, shift):
    count, band = lax.axis_size("tile"), lax.axis_size("freq")
    pairs = [(i * band + f, (i ^ 1) * band + (f - shift) % band) for i in range(count) for f in range(band)]
    return lax.ppermute(value, ("tile", "freq"), pairs)


def after(value, *others):
    return lax.optimization_barrier((value, *others))[0]


def exchange(sends, shifts, beside):
    count = lax.axis_size("tile")
    arrived = []
    for index, send in enumerate(sends):
        pairs = [(i, i ^ 2 * shifts[i % 2][index] ^ 1) for i in range(count)]
        arrived.append(lax.ppermute(send, "tile", pairs))
    return [after(arrived[0], *beside), *arrived[1:]]


def body(u_factors, v_factors, ranks, observed, start):
    band = lax.axis_size("freq")
    rows, tiles, width = u_factors.shape[1:]
    sources = start.shape[2]
    columns = tiles * width
    left_rows = u_factors.reshape(rows * tiles, width)
    right_rows = v_factors.reshape(rows * tiles, width)
    observed = observed.reshape(rows, sources)
    start = start.reshape(rows, sources)
    shifts = shifts_of(tiles)

    def shape(*dims, dtype=BF16):
        return jax.ShapeDtypeStruct(dims, dtype)

    members = tiles // 2
    wide = pltpu.VMEM((rows * tiles, width), F32)
    block = shape(sources // 2, width)
    blocks = shape(members, sources // 2, width)
    factor = shape(rows, members * width)
    flops = 2 * rows * columns * sources

    keep, give = call(
        functools.partial(forward_kernel, shifts),
        "forward",
        [blocks, blocks],
        [start, right_rows],
        [
            pltpu.VMEM(start.shape, F32),
            pltpu.VMEM(right_rows.shape, BF16),
            wide,
            pltpu.VMEM((rows, columns), BF16),
            pltpu.VMEM((sources, columns), F32),
            pltpu.SemaphoreType.DMA((PIECES + 1,)),
        ],
        flops,
        [pltpu.HBM] * 2,
        FIRST_LIMIT,
    )
    sends = call(add_kernel, "add", [block] * members, [keep, to_mate(give)], flops=HIDE * flops)
    mate_left = to_mate(after(left_rows, give))
    both_left, turned, start = call(
        functools.partial(rows_kernel, shifts),
        "rows",
        [shape(2 * rows, members * width), shape(sources, rows, dtype=F32), shape(rows, sources, dtype=F32)],
        [ranks, after(left_rows, give), mate_left, after(observed, give), after(start, give)],
        [wide],
        spaces=[pltpu.SMEM],
    )
    starts = [start]
    for shift in range(1, band):
        starts.append(lax.ppermute(start, "freq", [(f, (f - shift) % band) for f in range(band)]))
    arrived = exchange(sends, shifts, [both_left, turned])
    misfit = shape(sources, 2 * rows, dtype=F32)
    (misfit_early,) = call(
        early_kernel,
        "early",
        [misfit],
        [*arrived[:2], both_left, turned],
        [pltpu.VMEM((sources, 2 * width), BF16)],
        flops // 2,
    )
    (misfit,) = call(
        image_kernel,
        "image",
        [misfit],
        [*arrived[2:], misfit_early, both_left],
        [pltpu.VMEM((sources, (members - 2) * width), BF16)],
        flops // 2,
    )
    mate_right = to_mate(after(right_rows, misfit))
    mate_right = call(functools.partial(columns_kernel, shifts), "columns", [factor] * 2, [mate_right], [wide])
    sends = call(
        back_kernel,
        "back",
        [block] * members,
        [misfit, to_mate(misfit), both_left],
        [pltpu.VMEM((sources, 2 * rows), BF16), pltpu.VMEM((sources, members * width), F32)],
        HIDE * flops,
    )
    (own,) = call(pack_kernel, "pack", [blocks], exchange(sends, shifts[::-1], [*mate_right, *starts[1:]]))
    spread = shape(sources, members * width)
    part, own_left = call(
        part_kernel, "part", [shape(rows, sources, dtype=F32), spread], [own, mate_right[0]], flops=flops // 2
    )
    gradient, other_left = call(
        gradient_kernel,
        "gradient",
        [shape(rows, sources), spread],
        [part, to_mate(own), mate_right[1]],
        flops=flops // 2,
    )
    right = call(
        functools.partial(columns_kernel, shifts), "columns", [factor] * 2, [after(right_rows, gradient)], [wide]
    )
    gradients = []
    for shift in range(1, band):
        gradients.append(across(gradient, shift))
    result = shape(rows, sources, dtype=F32)
    if band == 2:
        halves = call(pair_kernel, "pair", [result] * 2, [*right, own_left, other_left, *starts], flops=flops)
        (estimate,) = call(shrink_pair_kernel, "shrink", [result], [*halves, *gradients])
        return estimate[None]
    bands = jnp.arange(band, dtype=jnp.int32)
    phases = (bands[:, None] + lax.axis_index("freq")) * bands[None, :] % band
    phases = (2.0 * math.pi / band) * phases.astype(F32)
    tables = jnp.stack([jnp.cos(phases), jnp.sin(phases)])
    (estimate,) = call(step_kernel, "step", [result], [*right, own_left, other_left, start], flops=flops)
    (estimate,) = call(
        functools.partial(shrink_kernel, band),
        "shrink",
        [result],
        [tables, estimate, *starts[1:], *gradients],
        spaces=[pltpu.SMEM],
    )
    return estimate[None]


def solution(mesh):
    in_specs = (
        P("freq", "tile", None, None),
        P("freq", "tile", None, None),
        P("freq", None, None),
        P("freq", "tile", None),
        P("freq", "tile", None),
    )
    out_specs = P("freq", "tile", None)
    return jax.shard_map(body, mesh=mesh, in_specs=in_specs, out_specs=out_specs, check_vma=False)
```

```python
import functools
import math

import jax
import jax.numpy as jnp
from jax import lax
from jax.experimental import pallas as pl
from jax.experimental.pallas import tpu as pltpu
from jax.sharding import PartitionSpec as P

STEP_SIZE = 0.2
LEVEL = 0.5
LANES = 128
VMEM_LIMIT = 32 * 1024 * 1024
FIRST_LIMIT = 55050 * 1024
PIECES = 8
HIDE = 128
F32 = jnp.float32
BF16 = jnp.bfloat16


def shifts_of(chips):
    even = list(range(chips - 2, -1, -2))
    odd = [shift + 1 for shift in even]
    even[-2], odd[-1] = odd[-1], even[-2]
    return [even, odd]


def place():
    position = lax.axis_index("tile")
    return position // 2, position % 2


def columns_of(tile):
    return pl.ds(pl.multiple_of(tile * LANES, LANES), LANES)


def both_shifts(shifts):
    chip, core = place()
    pairs = list(zip(*shifts))
    own = [chip ^ jnp.where(core == 0, first, second) for first, second in pairs]
    mate = [chip ^ jnp.where(core == 0, second, first) for first, second in pairs]
    return own, mate


def signs(rows):
    lane = lax.broadcasted_iota(jnp.int32, (rows, LANES), 1)
    return jnp.where(lane < LANES // 2, 1.0, -1.0).astype(F32)


def pick(wide, target, chosen, masks=None):
    rows = target.shape[0]
    tiles = wide.shape[0] // rows
    for index, tile in enumerate(chosen):
        part = wide[pl.ds(tile, rows, stride=tiles), :]
        if masks is not None:
            part = jnp.where(masks[index], part, 0.0)
        target[:, index * LANES : (index + 1) * LANES] = part.astype(BF16)


def separate(source, wide, target, chosen, masks=None):
    wide[...] = source[...].astype(F32)
    pick(wide, target, chosen, masks)


def adjoint_block(product, tile):
    half = product.shape[0] // 2
    real, imaginary = product[:half, columns_of(tile)], product[half:, columns_of(tile)]
    return (real * signs(half) + pltpu.roll(imaginary, LANES // 2, 1)).astype(BF16)


def spread_block(block, left, tile):
    half = block.shape[0]
    block = block.astype(F32)
    left[:half, columns_of(tile)] = (block * signs(half)).astype(BF16)
    left[half:, columns_of(tile)] = pltpu.roll(block, LANES // 2, 1).astype(BF16)


def times_transposed(left, right):
    return lax.dot_general(left, right, (((1,), (1,)), ((), ())), preferred_element_type=F32)


def forward_kernel(shifts, start, factors, keep, give, start_here, factors_here, wide, separated, product, sems):
    pieces = sems.shape[0] - 1
    rows, columns = separated.shape
    tiles = columns // LANES
    load_start = pltpu.make_async_copy(start, start_here, sems.at[pieces])
    load_start.start()
    loads = []
    for piece in range(pieces):
        at = pl.ds(piece * (rows * tiles // pieces), rows * tiles // pieces)
        loads.append(pltpu.make_async_copy(factors.at[at], factors_here.at[at], sems.at[piece]))
        loads[-1].start()
    load_start.wait()
    values = start_here[...].T.astype(BF16)
    for piece, load in enumerate(loads):
        at = pl.ds(piece * (rows * tiles // pieces), rows * tiles // pieces)
        load.wait()
        separate(
            factors_here.at[at], wide.at[at], separated.at[pl.ds(piece * (rows // pieces), rows // pieces)], range(tiles)
        )
    product[...] = jnp.dot(values, separated[...], preferred_element_type=F32)
    for out, chosen in zip((keep, give), both_shifts(shifts)):
        for index, tile in enumerate(chosen):
            out[index] = adjoint_block(product, tile)


def add_kernel(keep, arrived, *outs):
    for index, out in enumerate(outs):
        out[...] = (keep[index].astype(F32) + arrived[index].astype(F32)).astype(BF16)


def rows_kernel(shifts, ranks, own, mate, observed, start, both, turned, start_out, wide):
    chip, _ = place()
    _, chosen = both_shifts(shifts)
    rows = both.shape[0] // 2
    lane = lax.broadcasted_iota(jnp.int32, (1, LANES), 1) % (LANES // 2)
    masks = [lane < ranks[0, chip, tile] for tile in chosen]
    separate(own, wide, both.at[:rows], chosen, masks)
    separate(mate, wide, both.at[rows:], chosen, masks)
    turned[...] = observed[...].T
    start_out[...] = start[...]


def columns_kernel(shifts, factors, own, other, wide):
    chosen, rest = both_shifts(shifts)
    separate(factors, wide, own, chosen)
    pick(wide, other, rest)


def early_kernel(first, second, factors, observed, misfit, left):
    for index, block in enumerate((first, second)):
        spread_block(block[...], left, index)
    rows = observed.shape[1]
    image = times_transposed(left[...], factors[:, : left.shape[1]])
    misfit[:, :rows] = image[:, :rows] - observed[...]
    misfit[:, rows:] = image[:, rows:]


def image_kernel(*refs):
    blocks, (early, factors, misfit, left) = refs[:-4], refs[-4:]
    for index, block in enumerate(blocks):
        spread_block(block[...], left, index)
    misfit[...] = early[...] + times_transposed(left[...], factors[:, -left.shape[1] :])


def back_kernel(here, there, factors, *refs):
    outs, products = refs[:-1], refs[-1]
    rows = here.shape[1] // 2
    for side in range(2):
        at, other = pl.ds(side * rows, rows), pl.ds((1 - side) * rows, rows)
        misfit = (here[:, at] + there[:, other]).astype(BF16)
        products[side] = jnp.dot(misfit, factors[at, :], preferred_element_type=F32)
    for index, out in enumerate(outs):
        parts = [adjoint_block(products.at[side], index).astype(F32) for side in range(2)]
        out[...] = (parts[0] + parts[1]).astype(BF16)


def pack_kernel(*refs):
    for index, block in enumerate(refs[:-1]):
        refs[-1][index] = block[...]


def part_kernel(blocks, factors, part, left):
    for index in range(blocks.shape[0]):
        spread_block(blocks[index], left, index)
    part[...] = times_transposed(factors[...], left[...])


def gradient_kernel(part, blocks, factors, gradient, left):
    for index in range(blocks.shape[0]):
        spread_block(blocks[index], left, index)
    gradient[...] = (part[...] + times_transposed(factors[...], left[...])).astype(BF16)


def step_kernel(own, other, own_left, other_left, start, estimate):
    gradient = times_transposed(own[...], own_left[...]) + times_transposed(other[...], other_left[...])
    estimate[...] = start[...] - STEP_SIZE * gradient


def pair_kernel(own, other, own_left, other_left, here, there, total, difference):
    scale = 1.0 / math.sqrt(2)
    gradient = times_transposed(own[...], own_left[...]) + times_transposed(other[...], other_left[...])
    estimate = here[...] - STEP_SIZE * gradient
    total[...] = (estimate + there[...]) * scale
    difference[...] = (estimate - there[...]) * scale


def thin_out(values):
    return values - jnp.clip(values, -LEVEL, LEVEL)


def shrink_pair_kernel(total, difference, gradient, out):
    scale = 1.0 / math.sqrt(2)
    step = (STEP_SIZE * scale) * gradient[...].astype(F32)
    out[...] = (thin_out(total[...] - step) + thin_out(difference[...] + step)) * scale


def shrink_kernel(band, *refs):
    tables, own, starts, gradients, out = refs[0], refs[1], refs[2 : band + 1], refs[band + 1 : -1], refs[-1]
    others = [start[...] - STEP_SIZE * gradient[...].astype(F32) for start, gradient in zip(starts, gradients)]
    estimates = [own[...], *others]
    scale = 1.0 / math.sqrt(band)
    half = out.shape[1] // 2
    lane = lax.broadcasted_iota(jnp.int32, (1, out.shape[1]), 1)
    turn = jnp.where(lane < half, -1.0, 1.0).astype(F32)
    turned = [pltpu.roll(estimate, half, 1) * turn for estimate in estimates]
    total = jnp.zeros_like(estimates[0])
    for time in range(band):
        sample = jnp.zeros_like(estimates[0])
        for index in range(band):
            sample += tables[0, index, time] * estimates[index] + tables[1, index, time] * turned[index]
        thinned = thin_out(sample * scale)
        total += tables[0, 0, time] * thinned - tables[1, 0, time] * (pltpu.roll(thinned, half, 1) * turn)
    out[...] = total * scale


def call(kernel, name, outs, inputs, scratch=(), flops=0, spaces=(), limit=VMEM_LIMIT):
    spaces = (*spaces, *[pltpu.VMEM] * (len(inputs) - len(spaces)))
    moved = sum(x.size * x.dtype.itemsize for x in [*inputs, *outs]) if flops else 0
    return pl.pallas_call(
        kernel,
        out_shape=outs,
        in_specs=[pl.BlockSpec(memory_space=space) for space in spaces],
        out_specs=[pl.BlockSpec(memory_space=pltpu.VMEM)] * len(outs),
        scratch_shapes=scratch,
        compiler_params=pltpu.CompilerParams(vmem_limit_bytes=limit),
        cost_estimate=pl.CostEstimate(flops=flops, bytes_accessed=moved, transcendentals=0),
        name=name,
    )(*inputs)


def to_mate(value):
    return lax.ppermute(value, "tile", [(i, i ^ 1) for i in range(lax.axis_size("tile"))])


def across(value, shift):
    count, band = lax.axis_size("tile"), lax.axis_size("freq")
    pairs = [(i * band + f, (i ^ 1) * band + (f - shift) % band) for i in range(count) for f in range(band)]
    return lax.ppermute(value, ("tile", "freq"), pairs)


def after(value, *others):
    return lax.optimization_barrier((value, *others))[0]


def exchange(sends, shifts, beside):
    count = lax.axis_size("tile")
    arrived = []
    for index, send in enumerate(sends):
        pairs = [(i, i ^ 2 * shifts[i % 2][index] ^ 1) for i in range(count)]
        arrived.append(lax.ppermute(send, "tile", pairs))
    return [after(arrived[0], *beside), *arrived[1:]]


def body(u_factors, v_factors, ranks, observed, start):
    band = lax.axis_size("freq")
    rows, tiles, width = u_factors.shape[1:]
    sources = start.shape[2]
    columns = tiles * width
    left_rows = u_factors.reshape(rows * tiles, width)
    right_rows = v_factors.reshape(rows * tiles, width)
    observed = observed.reshape(rows, sources)
    start = start.reshape(rows, sources)
    shifts = shifts_of(tiles)

    def shape(*dims, dtype=BF16):
        return jax.ShapeDtypeStruct(dims, dtype)

    members = tiles // 2
    wide = pltpu.VMEM((rows * tiles, width), F32)
    block = shape(sources // 2, width)
    blocks = shape(members, sources // 2, width)
    factor = shape(rows, members * width)
    flops = 2 * rows * columns * sources

    keep, give = call(
        functools.partial(forward_kernel, shifts),
        "forward",
        [blocks, blocks],
        [start, right_rows],
        [
            pltpu.VMEM(start.shape, F32),
            pltpu.VMEM(right_rows.shape, BF16),
            wide,
            pltpu.VMEM((rows, columns), BF16),
            pltpu.VMEM((sources, columns), F32),
            pltpu.SemaphoreType.DMA((PIECES + 1,)),
        ],
        flops,
        [pltpu.HBM] * 2,
        FIRST_LIMIT,
    )
    sends = call(add_kernel, "add", [block] * members, [keep, to_mate(give)], flops=HIDE * flops)
    mate_left = to_mate(after(left_rows, give))
    both_left, turned, start = call(
        functools.partial(rows_kernel, shifts),
        "rows",
        [shape(2 * rows, members * width), shape(sources, rows, dtype=F32), shape(rows, sources, dtype=F32)],
        [ranks, after(left_rows, give), mate_left, after(observed, give), after(start, give)],
        [wide],
        spaces=[pltpu.SMEM],
    )
    starts = [start]
    for shift in range(1, band):
        starts.append(lax.ppermute(start, "freq", [(f, (f - shift) % band) for f in range(band)]))
    arrived = exchange(sends, shifts, [both_left, turned])
    misfit = shape(sources, 2 * rows, dtype=F32)
    (misfit_early,) = call(
        early_kernel,
        "early",
        [misfit],
        [*arrived[:2], both_left, turned],
        [pltpu.VMEM((sources, 2 * width), BF16)],
        flops // 2,
    )
    (misfit,) = call(
        image_kernel,
        "image",
        [misfit],
        [*arrived[2:], misfit_early, both_left],
        [pltpu.VMEM((sources, (members - 2) * width), BF16)],
        HIDE * flops,
    )
    mate_right = to_mate(after(right_rows, both_left))
    mate_right = call(functools.partial(columns_kernel, shifts), "columns", [factor] * 2, [mate_right], [wide])
    sends = call(
        back_kernel,
        "back",
        [block] * members,
        [misfit, to_mate(misfit), both_left],
        [pltpu.VMEM((2, sources, members * width), F32)],
        flops,
    )
    (own,) = call(pack_kernel, "pack", [blocks], exchange(sends, shifts[::-1], [*mate_right, *starts[1:]]))
    spread = shape(sources, members * width)
    part, own_left = call(
        part_kernel, "part", [shape(rows, sources, dtype=F32), spread], [own, mate_right[0]], flops=flops // 2
    )
    gradient, other_left = call(
        gradient_kernel,
        "gradient",
        [shape(rows, sources), spread],
        [part, to_mate(own), mate_right[1]],
        flops=flops // 2,
    )
    right = call(
        functools.partial(columns_kernel, shifts), "columns", [factor] * 2, [after(right_rows, gradient)], [wide]
    )
    gradients = []
    for shift in range(1, band):
        gradients.append(across(gradient, shift))
    result = shape(rows, sources, dtype=F32)
    if band == 2:
        halves = call(pair_kernel, "pair", [result] * 2, [*right, own_left, other_left, *starts], flops=flops)
        (estimate,) = call(shrink_pair_kernel, "shrink", [result], [*halves, *gradients])
        return estimate[None]
    bands = jnp.arange(band, dtype=jnp.int32)
    phases = (bands[:, None] + lax.axis_index("freq")) * bands[None, :] % band
    phases = (2.0 * math.pi / band) * phases.astype(F32)
    tables = jnp.stack([jnp.cos(phases), jnp.sin(phases)])
    (estimate,) = call(step_kernel, "step", [result], [*right, own_left, other_left, start], flops=flops)
    (estimate,) = call(
        functools.partial(shrink_kernel, band),
        "shrink",
        [result],
        [tables, estimate, *starts[1:], *gradients],
        spaces=[pltpu.SMEM],
    )
    return estimate[None]


def solution(mesh):
    in_specs = (
        P("freq", "tile", None, None),
        P("freq", "tile", None, None),
        P("freq", None, None),
        P("freq", "tile", None),
        P("freq", "tile", None),
    )
    out_specs = P("freq", "tile", None)
    return jax.shard_map(body, mesh=mesh, in_specs=in_specs, out_specs=out_specs, check_vma=False)
```

```python
import functools
import math

import jax
import jax.numpy as jnp
from jax import lax
from jax.experimental import pallas as pl
from jax.experimental.pallas import tpu as pltpu
from jax.sharding import PartitionSpec as P

STEP_SIZE = 0.2
LEVEL = 0.5
LANES = 128
VMEM_LIMIT = 32 * 1024 * 1024
FIRST_LIMIT = 55050 * 1024
PIECES = 4
HIDE = 128
F32 = jnp.float32
BF16 = jnp.bfloat16


def shifts_of(chips):
    even = list(range(chips - 2, -1, -2))
    odd = [shift + 1 for shift in even]
    even[-2], odd[-1] = odd[-1], even[-2]
    return [even, odd]


def place():
    position = lax.axis_index("tile")
    return position // 2, position % 2


def columns_of(tile):
    return pl.ds(pl.multiple_of(tile * LANES, LANES), LANES)


def both_shifts(shifts):
    chip, core = place()
    pairs = list(zip(*shifts))
    own = [chip ^ jnp.where(core == 0, first, second) for first, second in pairs]
    mate = [chip ^ jnp.where(core == 0, second, first) for first, second in pairs]
    return own, mate


def signs(rows):
    lane = lax.broadcasted_iota(jnp.int32, (rows, LANES), 1)
    return jnp.where(lane < LANES // 2, 1.0, -1.0).astype(F32)


def pick(wide, target, chosen, masks=None):
    rows = target.shape[0]
    tiles = wide.shape[0] // rows
    for index, tile in enumerate(chosen):
        part = wide[pl.ds(tile, rows, stride=tiles), :]
        if masks is not None:
            part = jnp.where(masks[index], part, 0.0)
        target[:, index * LANES : (index + 1) * LANES] = part.astype(BF16)


def separate(source, wide, target, chosen, masks=None):
    wide[...] = source[...].astype(F32)
    pick(wide, target, chosen, masks)


def adjoint_blocks(values, factors):
    half = values.shape[0] // 2
    pair = 2 * LANES
    blocks = []
    for at in range(0, factors.shape[1], pair):
        product = jnp.dot(values, factors[:, at : at + pair], preferred_element_type=F32)
        for lanes in (slice(0, LANES), slice(LANES, pair)):
            real, imaginary = product[:half, lanes], product[half:, lanes]
            blocks.append((real * signs(half) + pltpu.roll(imaginary, LANES // 2, 1)).astype(BF16))
    return blocks


def spread_block(block, left, tile):
    half = block.shape[0]
    block = block.astype(F32)
    left[:half, columns_of(tile)] = (block * signs(half)).astype(BF16)
    left[half:, columns_of(tile)] = pltpu.roll(block, LANES // 2, 1).astype(BF16)


def times_transposed(left, right):
    return lax.dot_general(left, right, (((1,), (1,)), ((), ())), preferred_element_type=F32)


def forward_kernel(shifts, start, factors, keep, give, start_here, factors_here, wide, separated, blocks, sems):
    pieces = sems.shape[0] - 1
    rows, columns = separated.shape
    tiles = columns // LANES
    load_start = pltpu.make_async_copy(start, start_here, sems.at[pieces])
    load_start.start()
    loads = []
    for piece in range(pieces):
        at = pl.ds(piece * (rows * tiles // pieces), rows * tiles // pieces)
        loads.append(pltpu.make_async_copy(factors.at[at], factors_here.at[at], sems.at[piece]))
        loads[-1].start()
    load_start.wait()
    values = start_here[...].T.astype(BF16)
    for piece, load in enumerate(loads):
        at = pl.ds(piece * (rows * tiles // pieces), rows * tiles // pieces)
        load.wait()
        separate(
            factors_here.at[at], wide.at[at], separated.at[pl.ds(piece * (rows // pieces), rows // pieces)], range(tiles)
        )
    for tile, block in enumerate(adjoint_blocks(values, separated)):
        blocks[tile] = block
    for out, chosen in zip((keep, give), both_shifts(shifts)):
        for index, tile in enumerate(chosen):
            out[index] = blocks[tile]


def add_kernel(keep, arrived, *outs):
    for index, out in enumerate(outs):
        out[...] = (keep[index].astype(F32) + arrived[index].astype(F32)).astype(BF16)


def rows_kernel(shifts, ranks, own, mate, observed, start, both, turned, start_out, wide):
    chip, _ = place()
    _, chosen = both_shifts(shifts)
    rows = both.shape[0] // 2
    lane = lax.broadcasted_iota(jnp.int32, (1, LANES), 1) % (LANES // 2)
    masks = [lane < ranks[0, chip, tile] for tile in chosen]
    separate(own, wide, both.at[:rows], chosen, masks)
    separate(mate, wide, both.at[rows:], chosen, masks)
    turned[...] = observed[...].T
    start_out[...] = start[...]


def columns_kernel(shifts, factors, own, other, wide):
    chosen, rest = both_shifts(shifts)
    separate(factors, wide, own, chosen)
    pick(wide, other, rest)


def early_kernel(first, second, factors, observed, misfit, left):
    for index, block in enumerate((first, second)):
        spread_block(block[...], left, index)
    rows = observed.shape[1]
    image = times_transposed(left[...], factors[:, : left.shape[1]])
    misfit[:, :rows] = image[:, :rows] - observed[...]
    misfit[:, rows:] = image[:, rows:]


def image_kernel(*refs):
    blocks, (early, factors, misfit, left) = refs[:-4], refs[-4:]
    for index, block in enumerate(blocks):
        spread_block(block[...], left, index)
    misfit[...] = early[...] + times_transposed(left[...], factors[:, -left.shape[1] :])


def back_kernel(here, there, factors, *outs):
    rows = here.shape[1] // 2
    parts = []
    for side in range(2):
        at, other = pl.ds(side * rows, rows), pl.ds((1 - side) * rows, rows)
        misfit = (here[:, at] + there[:, other]).astype(BF16)
        parts.append(adjoint_blocks(misfit, factors.at[at]))
    for out, first, second in zip(outs, *parts):
        out[...] = (first.astype(F32) + second.astype(F32)).astype(BF16)


def pack_kernel(*refs):
    for index, block in enumerate(refs[:-1]):
        refs[-1][index] = block[...]


def part_kernel(blocks, factors, part, left):
    for index in range(blocks.shape[0]):
        spread_block(blocks[index], left, index)
    part[...] = times_transposed(factors[...], left[...])


def gradient_kernel(part, blocks, factors, gradient, left):
    for index in range(blocks.shape[0]):
        spread_block(blocks[index], left, index)
    gradient[...] = (part[...] + times_transposed(factors[...], left[...])).astype(BF16)


def step_kernel(own, other, own_left, other_left, start, estimate):
    gradient = times_transposed(own[...], own_left[...]) + times_transposed(other[...], other_left[...])
    estimate[...] = start[...] - STEP_SIZE * gradient


def pair_kernel(own, other, own_left, other_left, here, there, total, difference):
    scale = 1.0 / math.sqrt(2)
    gradient = times_transposed(own[...], own_left[...]) + times_transposed(other[...], other_left[...])
    estimate = here[...] - STEP_SIZE * gradient
    total[...] = (estimate + there[...]) * scale
    difference[...] = (estimate - there[...]) * scale


def thin_out(values):
    return values - jnp.clip(values, -LEVEL, LEVEL)


def shrink_pair_kernel(total, difference, gradient, out):
    scale = 1.0 / math.sqrt(2)
    step = (STEP_SIZE * scale) * gradient[...].astype(F32)
    out[...] = (thin_out(total[...] - step) + thin_out(difference[...] + step)) * scale


def shrink_kernel(band, *refs):
    tables, own, starts, gradients, out = refs[0], refs[1], refs[2 : band + 1], refs[band + 1 : -1], refs[-1]
    others = [start[...] - STEP_SIZE * gradient[...].astype(F32) for start, gradient in zip(starts, gradients)]
    estimates = [own[...], *others]
    scale = 1.0 / math.sqrt(band)
    half = out.shape[1] // 2
    lane = lax.broadcasted_iota(jnp.int32, (1, out.shape[1]), 1)
    turn = jnp.where(lane < half, -1.0, 1.0).astype(F32)
    turned = [pltpu.roll(estimate, half, 1) * turn for estimate in estimates]
    total = jnp.zeros_like(estimates[0])
    for time in range(band):
        sample = jnp.zeros_like(estimates[0])
        for index in range(band):
            sample += tables[0, index, time] * estimates[index] + tables[1, index, time] * turned[index]
        thinned = thin_out(sample * scale)
        total += tables[0, 0, time] * thinned - tables[1, 0, time] * (pltpu.roll(thinned, half, 1) * turn)
    out[...] = total * scale


def call(kernel, name, outs, inputs, scratch=(), flops=0, spaces=(), limit=VMEM_LIMIT):
    spaces = (*spaces, *[pltpu.VMEM] * (len(inputs) - len(spaces)))
    moved = sum(x.size * x.dtype.itemsize for x in [*inputs, *outs]) if flops else 0
    return pl.pallas_call(
        kernel,
        out_shape=outs,
        in_specs=[pl.BlockSpec(memory_space=space) for space in spaces],
        out_specs=[pl.BlockSpec(memory_space=pltpu.VMEM)] * len(outs),
        scratch_shapes=scratch,
        compiler_params=pltpu.CompilerParams(vmem_limit_bytes=limit),
        cost_estimate=pl.CostEstimate(flops=flops, bytes_accessed=moved, transcendentals=0),
        name=name,
    )(*inputs)


def to_mate(value):
    return lax.ppermute(value, "tile", [(i, i ^ 1) for i in range(lax.axis_size("tile"))])


def across(value, shift):
    count, band = lax.axis_size("tile"), lax.axis_size("freq")
    pairs = [(i * band + f, (i ^ 1) * band + (f - shift) % band) for i in range(count) for f in range(band)]
    return lax.ppermute(value, ("tile", "freq"), pairs)


def after(value, *others):
    return lax.optimization_barrier((value, *others))[0]


def exchange(sends, shifts, beside):
    count = lax.axis_size("tile")
    arrived = []
    for index, send in enumerate(sends):
        pairs = [(i, i ^ 2 * shifts[i % 2][index] ^ 1) for i in range(count)]
        arrived.append(lax.ppermute(send, "tile", pairs))
    return [after(arrived[0], *beside), *arrived[1:]]


def body(u_factors, v_factors, ranks, observed, start):
    band = lax.axis_size("freq")
    rows, tiles, width = u_factors.shape[1:]
    sources = start.shape[2]
    columns = tiles * width
    left_rows = u_factors.reshape(rows * tiles, width)
    right_rows = v_factors.reshape(rows * tiles, width)
    observed = observed.reshape(rows, sources)
    start = start.reshape(rows, sources)
    shifts = shifts_of(tiles)

    def shape(*dims, dtype=BF16):
        return jax.ShapeDtypeStruct(dims, dtype)

    members = tiles // 2
    wide = pltpu.VMEM((rows * tiles, width), F32)
    block = shape(sources // 2, width)
    blocks = shape(members, sources // 2, width)
    factor = shape(rows, members * width)
    flops = 2 * rows * columns * sources

    keep, give = call(
        functools.partial(forward_kernel, shifts),
        "forward",
        [blocks, blocks],
        [start, right_rows],
        [
            pltpu.VMEM(start.shape, F32),
            pltpu.VMEM(right_rows.shape, BF16),
            wide,
            pltpu.VMEM((rows, columns), BF16),
            pltpu.VMEM((tiles, sources // 2, width), BF16),
            pltpu.SemaphoreType.DMA((PIECES + 1,)),
        ],
        flops,
        [pltpu.HBM] * 2,
        FIRST_LIMIT,
    )
    sends = call(add_kernel, "add", [block] * members, [keep, to_mate(give)], flops=HIDE * flops)
    mate_left = to_mate(after(left_rows, give))
    both_left, turned, start = call(
        functools.partial(rows_kernel, shifts),
        "rows",
        [shape(2 * rows, members * width), shape(sources, rows, dtype=F32), shape(rows, sources, dtype=F32)],
        [ranks, after(left_rows, give), mate_left, after(observed, give), after(start, give)],
        [wide],
        spaces=[pltpu.SMEM],
    )
    starts = [start]
    for shift in range(1, band):
        starts.append(lax.ppermute(start, "freq", [(f, (f - shift) % band) for f in range(band)]))
    arrived = exchange(sends, shifts, [both_left, turned])
    misfit = shape(sources, 2 * rows, dtype=F32)
    (misfit_early,) = call(
        early_kernel,
        "early",
        [misfit],
        [*arrived[:2], both_left, turned],
        [pltpu.VMEM((sources, 2 * width), BF16)],
        flops // 2,
    )
    (misfit,) = call(
        image_kernel,
        "image",
        [misfit],
        [*arrived[2:], misfit_early, both_left],
        [pltpu.VMEM((sources, (members - 2) * width), BF16)],
        HIDE * flops,
    )
    mate_right = to_mate(after(right_rows, both_left))
    mate_right = call(functools.partial(columns_kernel, shifts), "columns", [factor] * 2, [mate_right], [wide])
    sends = call(
        back_kernel,
        "back",
        [block] * members,
        [misfit, to_mate(misfit), both_left],
        flops=flops,
    )
    (own,) = call(pack_kernel, "pack", [blocks], exchange(sends, shifts[::-1], [*mate_right, *starts[1:]]))
    spread = shape(sources, members * width)
    part, own_left = call(
        part_kernel, "part", [shape(rows, sources, dtype=F32), spread], [own, mate_right[0]], flops=flops // 2
    )
    gradient, other_left = call(
        gradient_kernel,
        "gradient",
        [shape(rows, sources), spread],
        [part, to_mate(own), mate_right[1]],
        flops=flops // 2,
    )
    right = call(
        functools.partial(columns_kernel, shifts), "columns", [factor] * 2, [after(right_rows, gradient)], [wide]
    )
    gradients = []
    for shift in range(1, band):
        gradients.append(across(gradient, shift))
    result = shape(rows, sources, dtype=F32)
    if band == 2:
        halves = call(pair_kernel, "pair", [result] * 2, [*right, own_left, other_left, *starts], flops=flops)
        (estimate,) = call(shrink_pair_kernel, "shrink", [result], [*halves, *gradients])
        return estimate[None]
    bands = jnp.arange(band, dtype=jnp.int32)
    phases = (bands[:, None] + lax.axis_index("freq")) * bands[None, :] % band
    phases = (2.0 * math.pi / band) * phases.astype(F32)
    tables = jnp.stack([jnp.cos(phases), jnp.sin(phases)])
    (estimate,) = call(step_kernel, "step", [result], [*right, own_left, other_left, start], flops=flops)
    (estimate,) = call(
        functools.partial(shrink_kernel, band),
        "shrink",
        [result],
        [tables, estimate, *starts[1:], *gradients],
        spaces=[pltpu.SMEM],
    )
    return estimate[None]


def solution(mesh):
    in_specs = (
        P("freq", "tile", None, None),
        P("freq", "tile", None, None),
        P("freq", None, None),
        P("freq", "tile", None),
        P("freq", "tile", None),
    )
    out_specs = P("freq", "tile", None)
    return jax.shard_map(body, mesh=mesh, in_specs=in_specs, out_specs=out_specs, check_vma=False)
```

```python
import functools
import math

import jax
import jax.numpy as jnp
from jax import lax
from jax.experimental import pallas as pl
from jax.experimental.pallas import tpu as pltpu
from jax.sharding import PartitionSpec as P

STEP_SIZE = 0.2
LEVEL = 0.5
LANES = 128
VMEM_LIMIT = 32 * 1024 * 1024
FIRST_LIMIT = 55050 * 1024
PIECES = 4
HIDE = 128
F32 = jnp.float32
BF16 = jnp.bfloat16


def shifts_of(chips):
    far = range(chips - 1, 3, -1)
    return [[*[shift for shift in far if shift % 2], 1, 0], [*[shift for shift in far if shift % 2 == 0], 3, 2]]


def place():
    position = lax.axis_index("tile")
    return position // 2, position % 2


def columns_of(tile):
    return pl.ds(pl.multiple_of(tile * LANES, LANES), LANES)


def both_shifts(shifts):
    chip, core = place()
    pairs = list(zip(*shifts))
    own = [chip ^ jnp.where(core == 0, first, second) for first, second in pairs]
    mate = [chip ^ jnp.where(core == 0, second, first) for first, second in pairs]
    return own, mate


def signs(rows):
    lane = lax.broadcasted_iota(jnp.int32, (rows, LANES), 1)
    return jnp.where(lane < LANES // 2, 1.0, -1.0).astype(F32)


def pick(wide, target, chosen, masks=None):
    rows = target.shape[0]
    tiles = wide.shape[0] // rows
    for index, tile in enumerate(chosen):
        part = wide[pl.ds(tile, rows, stride=tiles), :]
        if masks is not None:
            part = jnp.where(masks[index], part, 0.0)
        target[:, index * LANES : (index + 1) * LANES] = part.astype(BF16)


def separate(source, wide, target, chosen, masks=None):
    wide[...] = source[...].astype(F32)
    pick(wide, target, chosen, masks)


def adjoint_blocks(values, factors):
    half = values.shape[0] // 2
    pair = 2 * LANES
    blocks = []
    for at in range(0, factors.shape[1], pair):
        product = jnp.dot(values, factors[:, at : at + pair], preferred_element_type=F32)
        for lanes in (slice(0, LANES), slice(LANES, pair)):
            real, imaginary = product[:half, lanes], product[half:, lanes]
            blocks.append((real * signs(half) + pltpu.roll(imaginary, LANES // 2, 1)).astype(BF16))
    return blocks


def spread_block(block, left, tile):
    half = block.shape[0]
    block = block.astype(F32)
    left[:half, columns_of(tile)] = (block * signs(half)).astype(BF16)
    left[half:, columns_of(tile)] = pltpu.roll(block, LANES // 2, 1).astype(BF16)


def times_transposed(left, right):
    return lax.dot_general(left, right, (((1,), (1,)), ((), ())), preferred_element_type=F32)


def forward_kernel(shifts, start, factors, keep, give, start_here, factors_here, wide, separated, blocks, sems):
    pieces = sems.shape[0] - 1
    rows, columns = separated.shape
    tiles = columns // LANES
    load_start = pltpu.make_async_copy(start, start_here, sems.at[pieces])
    load_start.start()
    loads = []
    for piece in range(pieces):
        at = pl.ds(piece * (rows * tiles // pieces), rows * tiles // pieces)
        loads.append(pltpu.make_async_copy(factors.at[at], factors_here.at[at], sems.at[piece]))
        loads[-1].start()
    load_start.wait()
    values = start_here[...].T.astype(BF16)
    for piece, load in enumerate(loads):
        at = pl.ds(piece * (rows * tiles // pieces), rows * tiles // pieces)
        load.wait()
        separate(
            factors_here.at[at], wide.at[at], separated.at[pl.ds(piece * (rows // pieces), rows // pieces)], range(tiles)
        )
    for tile, block in enumerate(adjoint_blocks(values, separated)):
        blocks[tile] = block
    for out, chosen in zip((keep, give), both_shifts(shifts)):
        for index, tile in enumerate(chosen):
            out[index] = blocks[tile]


def add_kernel(keep, arrived, *outs):
    for index, out in enumerate(outs):
        out[...] = (keep[index].astype(F32) + arrived[index].astype(F32)).astype(BF16)


def rows_kernel(shifts, ranks, own, mate, observed, start, both, turned, start_out, wide):
    chip, _ = place()
    _, chosen = both_shifts(shifts)
    rows = both.shape[0] // 2
    lane = lax.broadcasted_iota(jnp.int32, (1, LANES), 1) % (LANES // 2)
    masks = [lane < ranks[0, chip, tile] for tile in chosen]
    separate(own, wide, both.at[:rows], chosen, masks)
    separate(mate, wide, both.at[rows:], chosen, masks)
    turned[...] = observed[...].T
    start_out[...] = start[...]


def columns_kernel(shifts, factors, own, other, wide):
    chosen, rest = both_shifts(shifts)
    separate(factors, wide, own, chosen)
    pick(wide, other, rest)


def early_kernel(first, second, factors, observed, misfit, left):
    for index, block in enumerate((first, second)):
        spread_block(block[...], left, index)
    rows = observed.shape[1]
    image = times_transposed(left[...], factors[:, : left.shape[1]])
    misfit[:, :rows] = image[:, :rows] - observed[...]
    misfit[:, rows:] = image[:, rows:]


def image_kernel(*refs):
    blocks, (early, factors, misfit, left) = refs[:-4], refs[-4:]
    for index, block in enumerate(blocks):
        spread_block(block[...], left, index)
    misfit[...] = early[...] + times_transposed(left[...], factors[:, -left.shape[1] :])


def back_kernel(here, there, factors, *outs):
    rows = here.shape[1] // 2
    parts = []
    for side in range(2):
        at, other = pl.ds(side * rows, rows), pl.ds((1 - side) * rows, rows)
        misfit = (here[:, at] + there[:, other]).astype(BF16)
        parts.append(adjoint_blocks(misfit, factors.at[at]))
    for out, first, second in zip(outs, *parts):
        out[...] = (first.astype(F32) + second.astype(F32)).astype(BF16)


def pack_kernel(*refs):
    for index, block in enumerate(refs[:-1]):
        refs[-1][index] = block[...]


def part_kernel(blocks, factors, part, left):
    for index in range(blocks.shape[0]):
        spread_block(blocks[index], left, index)
    part[...] = times_transposed(factors[...], left[...])


def gradient_kernel(part, blocks, factors, gradient, left):
    for index in range(blocks.shape[0]):
        spread_block(blocks[index], left, index)
    gradient[...] = (part[...] + times_transposed(factors[...], left[...])).astype(BF16)


def step_kernel(own, other, own_left, other_left, start, estimate):
    gradient = times_transposed(own[...], own_left[...]) + times_transposed(other[...], other_left[...])
    estimate[...] = start[...] - STEP_SIZE * gradient


def pair_kernel(own, other, own_left, other_left, here, there, total, difference):
    scale = 1.0 / math.sqrt(2)
    gradient = times_transposed(own[...], own_left[...]) + times_transposed(other[...], other_left[...])
    estimate = here[...] - STEP_SIZE * gradient
    total[...] = (estimate + there[...]) * scale
    difference[...] = (estimate - there[...]) * scale


def thin_out(values):
    return values - jnp.clip(values, -LEVEL, LEVEL)


def shrink_pair_kernel(total, difference, gradient, out):
    scale = 1.0 / math.sqrt(2)
    step = (STEP_SIZE * scale) * gradient[...].astype(F32)
    out[...] = (thin_out(total[...] - step) + thin_out(difference[...] + step)) * scale


def shrink_kernel(band, *refs):
    tables, own, starts, gradients, out = refs[0], refs[1], refs[2 : band + 1], refs[band + 1 : -1], refs[-1]
    others = [start[...] - STEP_SIZE * gradient[...].astype(F32) for start, gradient in zip(starts, gradients)]
    estimates = [own[...], *others]
    scale = 1.0 / math.sqrt(band)
    half = out.shape[1] // 2
    lane = lax.broadcasted_iota(jnp.int32, (1, out.shape[1]), 1)
    turn = jnp.where(lane < half, -1.0, 1.0).astype(F32)
    turned = [pltpu.roll(estimate, half, 1) * turn for estimate in estimates]
    total = jnp.zeros_like(estimates[0])
    for time in range(band):
        sample = jnp.zeros_like(estimates[0])
        for index in range(band):
            sample += tables[0, index, time] * estimates[index] + tables[1, index, time] * turned[index]
        thinned = thin_out(sample * scale)
        total += tables[0, 0, time] * thinned - tables[1, 0, time] * (pltpu.roll(thinned, half, 1) * turn)
    out[...] = total * scale


def call(kernel, name, outs, inputs, scratch=(), flops=0, spaces=(), limit=VMEM_LIMIT):
    spaces = (*spaces, *[pltpu.VMEM] * (len(inputs) - len(spaces)))
    moved = sum(x.size * x.dtype.itemsize for x in [*inputs, *outs]) if flops else 0
    return pl.pallas_call(
        kernel,
        out_shape=outs,
        in_specs=[pl.BlockSpec(memory_space=space) for space in spaces],
        out_specs=[pl.BlockSpec(memory_space=pltpu.VMEM)] * len(outs),
        scratch_shapes=scratch,
        compiler_params=pltpu.CompilerParams(vmem_limit_bytes=limit),
        cost_estimate=pl.CostEstimate(flops=flops, bytes_accessed=moved, transcendentals=0),
        name=name,
    )(*inputs)


def to_mate(value):
    return lax.ppermute(value, "tile", [(i, i ^ 1) for i in range(lax.axis_size("tile"))])


def across(value, shift):
    count, band = lax.axis_size("tile"), lax.axis_size("freq")
    pairs = [(i * band + f, (i ^ 1) * band + (f - shift) % band) for i in range(count) for f in range(band)]
    return lax.ppermute(value, ("tile", "freq"), pairs)


def after(value, *others):
    return lax.optimization_barrier((value, *others))[0]


def exchange(sends, shifts, beside):
    count = lax.axis_size("tile")
    arrived = []
    for index, send in enumerate(sends):
        pairs = [(i, i ^ 2 * shifts[i % 2][index] ^ 1) for i in range(count)]
        arrived.append(lax.ppermute(send, "tile", pairs))
    return [after(arrived[0], *beside), *arrived[1:]]


def body(u_factors, v_factors, ranks, observed, start):
    band = lax.axis_size("freq")
    rows, tiles, width = u_factors.shape[1:]
    sources = start.shape[2]
    columns = tiles * width
    left_rows = u_factors.reshape(rows * tiles, width)
    right_rows = v_factors.reshape(rows * tiles, width)
    observed = observed.reshape(rows, sources)
    start = start.reshape(rows, sources)
    shifts = shifts_of(tiles)

    def shape(*dims, dtype=BF16):
        return jax.ShapeDtypeStruct(dims, dtype)

    members = tiles // 2
    wide = pltpu.VMEM((rows * tiles, width), F32)
    block = shape(sources // 2, width)
    blocks = shape(members, sources // 2, width)
    factor = shape(rows, members * width)
    flops = 2 * rows * columns * sources

    keep, give = call(
        functools.partial(forward_kernel, shifts),
        "forward",
        [blocks, blocks],
        [start, right_rows],
        [
            pltpu.VMEM(start.shape, F32),
            pltpu.VMEM(right_rows.shape, BF16),
            wide,
            pltpu.VMEM((rows, columns), BF16),
            pltpu.VMEM((tiles, sources // 2, width), BF16),
            pltpu.SemaphoreType.DMA((PIECES + 1,)),
        ],
        flops,
        [pltpu.HBM] * 2,
        FIRST_LIMIT,
    )
    sends = call(add_kernel, "add", [block] * members, [keep, to_mate(give)], flops=HIDE * flops)
    mate_left = to_mate(after(left_rows, give))
    both_left, turned, start = call(
        functools.partial(rows_kernel, shifts),
        "rows",
        [shape(2 * rows, members * width), shape(sources, rows, dtype=F32), shape(rows, sources, dtype=F32)],
        [ranks, after(left_rows, give), mate_left, after(observed, give), after(start, give)],
        [wide],
        spaces=[pltpu.SMEM],
    )
    starts = [start]
    for shift in range(1, band):
        starts.append(lax.ppermute(start, "freq", [(f, (f - shift) % band) for f in range(band)]))
    arrived = exchange(sends, shifts, [both_left, turned])
    misfit = shape(sources, 2 * rows, dtype=F32)
    (misfit_early,) = call(
        early_kernel,
        "early",
        [misfit],
        [*arrived[:2], both_left, turned],
        [pltpu.VMEM((sources, 2 * width), BF16)],
        flops // 2,
    )
    (misfit,) = call(
        image_kernel,
        "image",
        [misfit],
        [*arrived[2:], misfit_early, both_left],
        [pltpu.VMEM((sources, (members - 2) * width), BF16)],
        HIDE * flops,
    )
    mate_right = to_mate(after(right_rows, both_left))
    mate_right = call(functools.partial(columns_kernel, shifts), "columns", [factor] * 2, [mate_right], [wide])
    sends = call(
        back_kernel,
        "back",
        [block] * members,
        [misfit, to_mate(misfit), both_left],
        flops=flops,
    )
    (own,) = call(pack_kernel, "pack", [blocks], exchange(sends, shifts[::-1], [*mate_right, *starts[1:]]))
    spread = shape(sources, members * width)
    part, own_left = call(
        part_kernel, "part", [shape(rows, sources, dtype=F32), spread], [own, mate_right[0]], flops=flops // 2
    )
    gradient, other_left = call(
        gradient_kernel,
        "gradient",
        [shape(rows, sources), spread],
        [part, to_mate(own), mate_right[1]],
        flops=flops // 2,
    )
    right = call(
        functools.partial(columns_kernel, shifts), "columns", [factor] * 2, [after(right_rows, gradient)], [wide]
    )
    gradients = []
    for shift in range(1, band):
        gradients.append(across(gradient, shift))
    result = shape(rows, sources, dtype=F32)
    if band == 2:
        halves = call(pair_kernel, "pair", [result] * 2, [*right, own_left, other_left, *starts], flops=flops)
        (estimate,) = call(shrink_pair_kernel, "shrink", [result], [*halves, *gradients])
        return estimate[None]
    bands = jnp.arange(band, dtype=jnp.int32)
    phases = (bands[:, None] + lax.axis_index("freq")) * bands[None, :] % band
    phases = (2.0 * math.pi / band) * phases.astype(F32)
    tables = jnp.stack([jnp.cos(phases), jnp.sin(phases)])
    (estimate,) = call(step_kernel, "step", [result], [*right, own_left, other_left, start], flops=flops)
    (estimate,) = call(
        functools.partial(shrink_kernel, band),
        "shrink",
        [result],
        [tables, estimate, *starts[1:], *gradients],
        spaces=[pltpu.SMEM],
    )
    return estimate[None]


def solution(mesh):
    in_specs = (
        P("freq", "tile", None, None),
        P("freq", "tile", None, None),
        P("freq", None, None),
        P("freq", "tile", None),
        P("freq", "tile", None),
    )
    out_specs = P("freq", "tile", None)
    return jax.shard_map(body, mesh=mesh, in_specs=in_specs, out_specs=out_specs, check_vma=False)
```

```python
import functools
import math

import jax
import jax.numpy as jnp
from jax import lax
from jax.experimental import pallas as pl
from jax.experimental.pallas import tpu as pltpu
from jax.sharding import PartitionSpec as P

STEP_SIZE = 0.2
LEVEL = 0.5
LANES = 128
VMEM_LIMIT = 32 * 1024 * 1024
FIRST_LIMIT = 55050 * 1024
PIECES = 4
HIDE = 128
F32 = jnp.float32
BF16 = jnp.bfloat16


MEETINGS = {
    8: [
        [(0o77666677, 0o55555555), (0o11777711, 0o34444443), (0o66001166, 0o43333334), (0o00110000, 0o22222222)],
        [(0o22555533, 0o77060677), (0o55223355, 0o16777761), (0o44444444, 0o61606016), (0o33332222, 0o00111100)],
    ]
}


def routes_of(chips):
    if chips in MEETINGS:
        shifts = [
            [[[packed >> 3 * chip & 7 for chip in range(chips)] for packed in pair] for pair in way]
            for way in MEETINGS[chips]
        ]
    else:
        far = range(chips - 1, 3, -1)
        first = [*[shift for shift in far if shift % 2], 1, 0]
        second = [*[shift for shift in far if shift % 2 == 0], 3, 2]
        out = [[[shift] * chips for shift in pair] for pair in zip(first, second)]
        shifts = [out, [pair[::-1] for pair in out]]
    return [[[[chip ^ shift for chip, shift in enumerate(core)] for core in pair] for pair in way] for way in shifts]


def arrivals_of(routes):
    return [[[pair[1 - core].index(chip) for chip in range(len(pair[core]))] for core in range(2)] for pair in routes]


def place():
    position = lax.axis_index("tile")
    return position // 2, position % 2


def columns_of(tile):
    return pl.ds(pl.multiple_of(tile * LANES, LANES), LANES)


def entry(first, second):
    chip, core = place()
    if len(set(first)) == 1 and len(set(second)) == 1:
        return jnp.where(core == 0, first[0], second[0])
    bits = max(*first, *second).bit_length()
    first, second = [sum(value << bits * at for at, value in enumerate(values)) for values in (first, second)]
    return jnp.where(core == 0, first, second) >> bits * chip & (1 << bits) - 1


def both_tiles(routes):
    chip, _ = place()
    shifts = [[[at ^ other for at, other in enumerate(core)] for core in pair] for pair in routes]
    return [chip ^ entry(*pair) for pair in shifts], [chip ^ entry(*pair[::-1]) for pair in shifts]


def signs(rows):
    lane = lax.broadcasted_iota(jnp.int32, (rows, LANES), 1)
    return jnp.where(lane < LANES // 2, 1.0, -1.0).astype(F32)


def pick(wide, target, chosen, masks=None):
    rows = target.shape[0]
    tiles = wide.shape[0] // rows
    for index, tile in enumerate(chosen):
        part = wide[pl.ds(tile, rows, stride=tiles), :]
        if masks is not None:
            part = jnp.where(masks[index], part, 0.0)
        target[:, index * LANES : (index + 1) * LANES] = part.astype(BF16)


def separate(source, wide, target, chosen, masks=None):
    wide[...] = source[...].astype(F32)
    pick(wide, target, chosen, masks)


def adjoint_blocks(values, factors):
    half = values.shape[0] // 2
    pair = 2 * LANES
    blocks = []
    for at in range(0, factors.shape[1], pair):
        product = jnp.dot(values, factors[:, at : at + pair], preferred_element_type=F32)
        for lanes in (slice(0, LANES), slice(LANES, pair)):
            real, imaginary = product[:half, lanes], product[half:, lanes]
            blocks.append((real * signs(half) + pltpu.roll(imaginary, LANES // 2, 1)).astype(BF16))
    return blocks


def spread_block(block, left, tile):
    half = block.shape[0]
    block = block.astype(F32)
    left[:half, columns_of(tile)] = (block * signs(half)).astype(BF16)
    left[half:, columns_of(tile)] = pltpu.roll(block, LANES // 2, 1).astype(BF16)


def times_transposed(left, right):
    return lax.dot_general(left, right, (((1,), (1,)), ((), ())), preferred_element_type=F32)


def forward_kernel(routes, start, factors, keep, give, start_here, factors_here, wide, separated, blocks, sems):
    pieces = sems.shape[0] - 1
    rows, columns = separated.shape
    tiles = columns // LANES
    load_start = pltpu.make_async_copy(start, start_here, sems.at[pieces])
    load_start.start()
    loads = []
    for piece in range(pieces):
        at = pl.ds(piece * (rows * tiles // pieces), rows * tiles // pieces)
        loads.append(pltpu.make_async_copy(factors.at[at], factors_here.at[at], sems.at[piece]))
        loads[-1].start()
    load_start.wait()
    values = start_here[...].T.astype(BF16)
    for piece, load in enumerate(loads):
        at = pl.ds(piece * (rows * tiles // pieces), rows * tiles // pieces)
        load.wait()
        separate(
            factors_here.at[at], wide.at[at], separated.at[pl.ds(piece * (rows // pieces), rows // pieces)], range(tiles)
        )
    for tile, block in enumerate(adjoint_blocks(values, separated)):
        blocks[tile] = block
    for out, chosen in zip((keep, give), both_tiles(routes)):
        for index, tile in enumerate(chosen):
            out[index] = blocks[tile]


def add_kernel(keep, arrived, *outs):
    for index, out in enumerate(outs):
        out[...] = (keep[index].astype(F32) + arrived[index].astype(F32)).astype(BF16)


def rows_kernel(arrivals, ranks, own, mate, observed, start, both, turned, start_out, wide):
    chip, _ = place()
    chosen, _ = both_tiles(arrivals)
    rows = both.shape[0] // 2
    lane = lax.broadcasted_iota(jnp.int32, (1, LANES), 1) % (LANES // 2)
    masks = [lane < ranks[0, chip, tile] for tile in chosen]
    separate(own, wide, both.at[:rows], chosen, masks)
    separate(mate, wide, both.at[rows:], chosen, masks)
    turned[...] = observed[...].T
    start_out[...] = start[...]


def columns_kernel(arrivals, factors, own, other, wide):
    chosen, rest = both_tiles(arrivals)
    separate(factors, wide, own, chosen)
    pick(wide, other, rest)


def early_kernel(first, second, factors, observed, misfit, left):
    for index, block in enumerate((first, second)):
        spread_block(block[...], left, index)
    rows = observed.shape[1]
    image = times_transposed(left[...], factors[:, : left.shape[1]])
    misfit[:, :rows] = image[:, :rows] - observed[...]
    misfit[:, rows:] = image[:, rows:]


def image_kernel(*refs):
    blocks, (early, factors, misfit, left) = refs[:-4], refs[-4:]
    for index, block in enumerate(blocks):
        spread_block(block[...], left, index)
    misfit[...] = early[...] + times_transposed(left[...], factors[:, -left.shape[1] :])


def back_kernel(places, here, there, factors, *refs):
    outs, blocks = refs[:-1], refs[-1]
    rows = here.shape[1] // 2
    parts = []
    for side in range(2):
        at, other = pl.ds(side * rows, rows), pl.ds((1 - side) * rows, rows)
        misfit = (here[:, at] + there[:, other]).astype(BF16)
        parts.append(adjoint_blocks(misfit, factors.at[at]))
    for index, (first, second) in enumerate(zip(*parts)):
        blocks[index] = (first.astype(F32) + second.astype(F32)).astype(BF16)
    for out, pair in zip(outs, places):
        out[...] = blocks[entry(*pair)]


def pack_kernel(*refs):
    for index, block in enumerate(refs[:-1]):
        refs[-1][index] = block[...]


def part_kernel(blocks, factors, part, left):
    for index in range(blocks.shape[0]):
        spread_block(blocks[index], left, index)
    part[...] = times_transposed(factors[...], left[...])


def gradient_kernel(part, blocks, factors, gradient, left):
    for index in range(blocks.shape[0]):
        spread_block(blocks[index], left, index)
    gradient[...] = (part[...] + times_transposed(factors[...], left[...])).astype(BF16)


def step_kernel(own, other, own_left, other_left, start, estimate):
    gradient = times_transposed(own[...], own_left[...]) + times_transposed(other[...], other_left[...])
    estimate[...] = start[...] - STEP_SIZE * gradient


def pair_kernel(own, other, own_left, other_left, here, there, total, difference):
    scale = 1.0 / math.sqrt(2)
    gradient = times_transposed(own[...], own_left[...]) + times_transposed(other[...], other_left[...])
    estimate = here[...] - STEP_SIZE * gradient
    total[...] = (estimate + there[...]) * scale
    difference[...] = (estimate - there[...]) * scale


def thin_out(values):
    return values - jnp.clip(values, -LEVEL, LEVEL)


def shrink_pair_kernel(total, difference, gradient, out):
    scale = 1.0 / math.sqrt(2)
    step = (STEP_SIZE * scale) * gradient[...].astype(F32)
    out[...] = (thin_out(total[...] - step) + thin_out(difference[...] + step)) * scale


def shrink_kernel(band, *refs):
    tables, own, starts, gradients, out = refs[0], refs[1], refs[2 : band + 1], refs[band + 1 : -1], refs[-1]
    others = [start[...] - STEP_SIZE * gradient[...].astype(F32) for start, gradient in zip(starts, gradients)]
    estimates = [own[...], *others]
    scale = 1.0 / math.sqrt(band)
    half = out.shape[1] // 2
    lane = lax.broadcasted_iota(jnp.int32, (1, out.shape[1]), 1)
    turn = jnp.where(lane < half, -1.0, 1.0).astype(F32)
    turned = [pltpu.roll(estimate, half, 1) * turn for estimate in estimates]
    total = jnp.zeros_like(estimates[0])
    for time in range(band):
        sample = jnp.zeros_like(estimates[0])
        for index in range(band):
            sample += tables[0, index, time] * estimates[index] + tables[1, index, time] * turned[index]
        thinned = thin_out(sample * scale)
        total += tables[0, 0, time] * thinned - tables[1, 0, time] * (pltpu.roll(thinned, half, 1) * turn)
    out[...] = total * scale


def call(kernel, name, outs, inputs, scratch=(), flops=0, spaces=(), limit=VMEM_LIMIT):
    spaces = (*spaces, *[pltpu.VMEM] * (len(inputs) - len(spaces)))
    moved = sum(x.size * x.dtype.itemsize for x in [*inputs, *outs]) if flops else 0
    return pl.pallas_call(
        kernel,
        out_shape=outs,
        in_specs=[pl.BlockSpec(memory_space=space) for space in spaces],
        out_specs=[pl.BlockSpec(memory_space=pltpu.VMEM)] * len(outs),
        scratch_shapes=scratch,
        compiler_params=pltpu.CompilerParams(vmem_limit_bytes=limit),
        cost_estimate=pl.CostEstimate(flops=flops, bytes_accessed=moved, transcendentals=0),
        name=name,
    )(*inputs)


def to_mate(value):
    return lax.ppermute(value, "tile", [(i, i ^ 1) for i in range(lax.axis_size("tile"))])


def across(value, shift):
    count, band = lax.axis_size("tile"), lax.axis_size("freq")
    pairs = [(i * band + f, (i ^ 1) * band + (f - shift) % band) for i in range(count) for f in range(band)]
    return lax.ppermute(value, ("tile", "freq"), pairs)


def after(value, *others):
    return lax.optimization_barrier((value, *others))[0]


def exchange(sends, routes, beside):
    arrived = []
    for send, pair in zip(sends, routes):
        pairs = [(2 * at + core, 2 * to + 1 - core) for core in range(2) for at, to in enumerate(pair[core])]
        arrived.append(lax.ppermute(send, "tile", sorted(pairs)))
    return [after(arrived[0], *beside), *arrived[1:]]


def body(u_factors, v_factors, ranks, observed, start):
    band = lax.axis_size("freq")
    rows, tiles, width = u_factors.shape[1:]
    sources = start.shape[2]
    columns = tiles * width
    left_rows = u_factors.reshape(rows * tiles, width)
    right_rows = v_factors.reshape(rows * tiles, width)
    observed = observed.reshape(rows, sources)
    start = start.reshape(rows, sources)
    routes, back_routes = routes_of(tiles)
    arrivals, back_arrivals = arrivals_of(routes), arrivals_of(back_routes)
    places = [
        [
            [[came[core][chip] for came in arrivals].index(to) for chip, to in enumerate(pair[core])]
            for core in range(2)
        ]
        for pair in back_routes
    ]

    def shape(*dims, dtype=BF16):
        return jax.ShapeDtypeStruct(dims, dtype)

    members = tiles // 2
    wide = pltpu.VMEM((rows * tiles, width), F32)
    block = shape(sources // 2, width)
    blocks = shape(members, sources // 2, width)
    factor = shape(rows, members * width)
    flops = 2 * rows * columns * sources

    keep, give = call(
        functools.partial(forward_kernel, routes),
        "forward",
        [blocks, blocks],
        [start, right_rows],
        [
            pltpu.VMEM(start.shape, F32),
            pltpu.VMEM(right_rows.shape, BF16),
            wide,
            pltpu.VMEM((rows, columns), BF16),
            pltpu.VMEM((tiles, sources // 2, width), BF16),
            pltpu.SemaphoreType.DMA((PIECES + 1,)),
        ],
        flops,
        [pltpu.HBM] * 2,
        FIRST_LIMIT,
    )
    sends = call(add_kernel, "add", [block] * members, [keep, to_mate(give)], flops=HIDE * flops)
    mate_left = to_mate(after(left_rows, give))
    both_left, turned, start = call(
        functools.partial(rows_kernel, arrivals),
        "rows",
        [shape(2 * rows, members * width), shape(sources, rows, dtype=F32), shape(rows, sources, dtype=F32)],
        [ranks, after(left_rows, give), mate_left, after(observed, give), after(start, give)],
        [wide],
        spaces=[pltpu.SMEM],
    )
    starts = [start]
    for shift in range(1, band):
        starts.append(lax.ppermute(start, "freq", [(f, (f - shift) % band) for f in range(band)]))
    arrived = exchange(sends, routes, [both_left, turned])
    misfit = shape(sources, 2 * rows, dtype=F32)
    (misfit_early,) = call(
        early_kernel,
        "early",
        [misfit],
        [*arrived[:2], both_left, turned],
        [pltpu.VMEM((sources, 2 * width), BF16)],
        flops // 2,
    )
    (misfit,) = call(
        image_kernel,
        "image",
        [misfit],
        [*arrived[2:], misfit_early, both_left],
        [pltpu.VMEM((sources, (members - 2) * width), BF16)],
        HIDE * flops,
    )
    mate_right = to_mate(after(right_rows, both_left))
    mate_right = call(functools.partial(columns_kernel, back_arrivals), "columns", [factor] * 2, [mate_right], [wide])
    sends = call(
        functools.partial(back_kernel, places),
        "back",
        [block] * members,
        [misfit, to_mate(misfit), both_left],
        [pltpu.VMEM((members, sources // 2, width), BF16)],
        flops,
    )
    (own,) = call(pack_kernel, "pack", [blocks], exchange(sends, back_routes, [*mate_right, *starts[1:]]))
    spread = shape(sources, members * width)
    part, own_left = call(
        part_kernel, "part", [shape(rows, sources, dtype=F32), spread], [own, mate_right[0]], flops=flops // 2
    )
    gradient, other_left = call(
        gradient_kernel,
        "gradient",
        [shape(rows, sources), spread],
        [part, to_mate(own), mate_right[1]],
        flops=flops // 2,
    )
    right = call(
        functools.partial(columns_kernel, back_arrivals), "columns", [factor] * 2, [after(right_rows, gradient)], [wide]
    )
    gradients = []
    for shift in range(1, band):
        gradients.append(across(gradient, shift))
    result = shape(rows, sources, dtype=F32)
    if band == 2:
        halves = call(pair_kernel, "pair", [result] * 2, [*right, own_left, other_left, *starts], flops=flops)
        (estimate,) = call(shrink_pair_kernel, "shrink", [result], [*halves, *gradients])
        return estimate[None]
    bands = jnp.arange(band, dtype=jnp.int32)
    phases = (bands[:, None] + lax.axis_index("freq")) * bands[None, :] % band
    phases = (2.0 * math.pi / band) * phases.astype(F32)
    tables = jnp.stack([jnp.cos(phases), jnp.sin(phases)])
    (estimate,) = call(step_kernel, "step", [result], [*right, own_left, other_left, start], flops=flops)
    (estimate,) = call(
        functools.partial(shrink_kernel, band),
        "shrink",
        [result],
        [tables, estimate, *starts[1:], *gradients],
        spaces=[pltpu.SMEM],
    )
    return estimate[None]


def solution(mesh):
    in_specs = (
        P("freq", "tile", None, None),
        P("freq", "tile", None, None),
        P("freq", None, None),
        P("freq", "tile", None),
        P("freq", "tile", None),
    )
    out_specs = P("freq", "tile", None)
    return jax.shard_map(body, mesh=mesh, in_specs=in_specs, out_specs=out_specs, check_vma=False)
```

```python
import functools
import math

import jax
import jax.numpy as jnp
from jax import lax
from jax.experimental import pallas as pl
from jax.experimental.pallas import tpu as pltpu
from jax.sharding import PartitionSpec as P

STEP_SIZE = 0.2
LEVEL = 0.5
LANES = 128
VMEM_LIMIT = 32 * 1024 * 1024
FIRST_LIMIT = 55050 * 1024
PIECES = 4
HIDE = 128
F32 = jnp.float32
BF16 = jnp.bfloat16


MEETINGS = {
    8: [
        [(0o77037433, 0o16666551), (0o33473077, 0o52555165), (0o44344344, 0o65211616), (0o00700700, 0o21122222)],
        [(0o11551155, 0o70074334), (0o66166526, 0o47703777), (0o55215611, 0o04447443), (0o22622262, 0o33330000)],
    ]
}


def routes_of(chips):
    if chips in MEETINGS:
        shifts = [
            [[[packed >> 3 * chip & 7 for chip in range(chips)] for packed in pair] for pair in way]
            for way in MEETINGS[chips]
        ]
    else:
        far = range(chips - 1, 3, -1)
        first = [*[shift for shift in far if shift % 2], 1, 0]
        second = [*[shift for shift in far if shift % 2 == 0], 3, 2]
        out = [[[shift] * chips for shift in pair] for pair in zip(first, second)]
        shifts = [out, [pair[::-1] for pair in out]]
    return [[[[chip ^ shift for chip, shift in enumerate(core)] for core in pair] for pair in way] for way in shifts]


def arrivals_of(routes):
    return [[[pair[1 - core].index(chip) for chip in range(len(pair[core]))] for core in range(2)] for pair in routes]


def place():
    position = lax.axis_index("tile")
    return position // 2, position % 2


def columns_of(tile):
    return pl.ds(pl.multiple_of(tile * LANES, LANES), LANES)


def entry(first, second):
    chip, core = place()
    if len(set(first)) == 1 and len(set(second)) == 1:
        return jnp.where(core == 0, first[0], second[0])
    bits = max(*first, *second).bit_length()
    first, second = [sum(value << bits * at for at, value in enumerate(values)) for values in (first, second)]
    return jnp.where(core == 0, first, second) >> bits * chip & (1 << bits) - 1


def both_tiles(routes):
    chip, _ = place()
    shifts = [[[at ^ other for at, other in enumerate(core)] for core in pair] for pair in routes]
    return [chip ^ entry(*pair) for pair in shifts], [chip ^ entry(*pair[::-1]) for pair in shifts]


def signs(rows):
    lane = lax.broadcasted_iota(jnp.int32, (rows, LANES), 1)
    return jnp.where(lane < LANES // 2, 1.0, -1.0).astype(F32)


def pick(wide, target, chosen, masks=None):
    rows = target.shape[0]
    tiles = wide.shape[0] // rows
    for index, tile in enumerate(chosen):
        part = wide[pl.ds(tile, rows, stride=tiles), :]
        if masks is not None:
            part = jnp.where(masks[index], part, 0.0)
        target[:, index * LANES : (index + 1) * LANES] = part.astype(BF16)


def separate(source, wide, target, chosen, masks=None):
    wide[...] = source[...].astype(F32)
    pick(wide, target, chosen, masks)


def adjoint_blocks(values, factors):
    half = values.shape[0] // 2
    pair = 2 * LANES
    blocks = []
    for at in range(0, factors.shape[1], pair):
        product = jnp.dot(values, factors[:, at : at + pair], preferred_element_type=F32)
        for lanes in (slice(0, LANES), slice(LANES, pair)):
            real, imaginary = product[:half, lanes], product[half:, lanes]
            blocks.append((real * signs(half) + pltpu.roll(imaginary, LANES // 2, 1)).astype(BF16))
    return blocks


def spread_block(block, left, tile):
    half = block.shape[0]
    block = block.astype(F32)
    left[:half, columns_of(tile)] = (block * signs(half)).astype(BF16)
    left[half:, columns_of(tile)] = pltpu.roll(block, LANES // 2, 1).astype(BF16)


def times_transposed(left, right):
    return lax.dot_general(left, right, (((1,), (1,)), ((), ())), preferred_element_type=F32)


def forward_kernel(routes, start, factors, keep, give, start_here, factors_here, wide, separated, blocks, sems):
    pieces = sems.shape[0] - 1
    rows, columns = separated.shape
    tiles = columns // LANES
    load_start = pltpu.make_async_copy(start, start_here, sems.at[pieces])
    load_start.start()
    loads = []
    for piece in range(pieces):
        at = pl.ds(piece * (rows * tiles // pieces), rows * tiles // pieces)
        loads.append(pltpu.make_async_copy(factors.at[at], factors_here.at[at], sems.at[piece]))
        loads[-1].start()
    load_start.wait()
    values = start_here[...].T.astype(BF16)
    for piece, load in enumerate(loads):
        at = pl.ds(piece * (rows * tiles // pieces), rows * tiles // pieces)
        load.wait()
        separate(
            factors_here.at[at], wide.at[at], separated.at[pl.ds(piece * (rows // pieces), rows // pieces)], range(tiles)
        )
    for tile, block in enumerate(adjoint_blocks(values, separated)):
        blocks[tile] = block
    for out, chosen in zip((keep, give), both_tiles(routes)):
        for index, tile in enumerate(chosen):
            out[index] = blocks[tile]


def add_kernel(keep, arrived, *outs):
    for index, out in enumerate(outs):
        out[...] = (keep[index].astype(F32) + arrived[index].astype(F32)).astype(BF16)


def rows_kernel(arrivals, ranks, own, mate, observed, start, both, turned, start_out, wide):
    chip, _ = place()
    chosen, _ = both_tiles(arrivals)
    rows = both.shape[0] // 2
    lane = lax.broadcasted_iota(jnp.int32, (1, LANES), 1) % (LANES // 2)
    masks = [lane < ranks[0, chip, tile] for tile in chosen]
    separate(own, wide, both.at[:rows], chosen, masks)
    separate(mate, wide, both.at[rows:], chosen, masks)
    turned[...] = observed[...].T
    start_out[...] = start[...]


def columns_kernel(arrivals, factors, own, other, wide):
    chosen, rest = both_tiles(arrivals)
    separate(factors, wide, own, chosen)
    pick(wide, other, rest)


def early_kernel(first, second, factors, observed, misfit, left):
    for index, block in enumerate((first, second)):
        spread_block(block[...], left, index)
    rows = observed.shape[1]
    image = times_transposed(left[...], factors[:, : left.shape[1]])
    misfit[:, :rows] = image[:, :rows] - observed[...]
    misfit[:, rows:] = image[:, rows:]


def image_kernel(*refs):
    blocks, (early, factors, misfit, left) = refs[:-4], refs[-4:]
    for index, block in enumerate(blocks):
        spread_block(block[...], left, index)
    misfit[...] = early[...] + times_transposed(left[...], factors[:, -left.shape[1] :])


def back_kernel(places, here, there, factors, *refs):
    outs, blocks = refs[:-1], refs[-1]
    rows = here.shape[1] // 2
    parts = []
    for side in range(2):
        at, other = pl.ds(side * rows, rows), pl.ds((1 - side) * rows, rows)
        misfit = (here[:, at] + there[:, other]).astype(BF16)
        parts.append(adjoint_blocks(misfit, factors.at[at]))
    for index, (first, second) in enumerate(zip(*parts)):
        blocks[index] = (first.astype(F32) + second.astype(F32)).astype(BF16)
    for out, pair in zip(outs, places):
        out[...] = blocks[entry(*pair)]


def pack_kernel(*refs):
    for index, block in enumerate(refs[:-1]):
        refs[-1][index] = block[...]


def part_kernel(blocks, factors, part, left):
    for index in range(blocks.shape[0]):
        spread_block(blocks[index], left, index)
    part[...] = times_transposed(factors[...], left[...])


def gradient_kernel(part, blocks, factors, gradient, left):
    for index in range(blocks.shape[0]):
        spread_block(blocks[index], left, index)
    gradient[...] = (part[...] + times_transposed(factors[...], left[...])).astype(BF16)


def step_kernel(own, other, own_left, other_left, start, estimate):
    gradient = times_transposed(own[...], own_left[...]) + times_transposed(other[...], other_left[...])
    estimate[...] = start[...] - STEP_SIZE * gradient


def pair_kernel(own, other, own_left, other_left, here, there, total, difference):
    scale = 1.0 / math.sqrt(2)
    gradient = times_transposed(own[...], own_left[...]) + times_transposed(other[...], other_left[...])
    estimate = here[...] - STEP_SIZE * gradient
    total[...] = (estimate + there[...]) * scale
    difference[...] = (estimate - there[...]) * scale


def thin_out(values):
    return values - jnp.clip(values, -LEVEL, LEVEL)


def shrink_pair_kernel(total, difference, gradient, out):
    scale = 1.0 / math.sqrt(2)
    step = (STEP_SIZE * scale) * gradient[...].astype(F32)
    out[...] = (thin_out(total[...] - step) + thin_out(difference[...] + step)) * scale


def shrink_kernel(band, *refs):
    tables, own, starts, gradients, out = refs[0], refs[1], refs[2 : band + 1], refs[band + 1 : -1], refs[-1]
    others = [start[...] - STEP_SIZE * gradient[...].astype(F32) for start, gradient in zip(starts, gradients)]
    estimates = [own[...], *others]
    scale = 1.0 / math.sqrt(band)
    half = out.shape[1] // 2
    lane = lax.broadcasted_iota(jnp.int32, (1, out.shape[1]), 1)
    turn = jnp.where(lane < half, -1.0, 1.0).astype(F32)
    turned = [pltpu.roll(estimate, half, 1) * turn for estimate in estimates]
    total = jnp.zeros_like(estimates[0])
    for time in range(band):
        sample = jnp.zeros_like(estimates[0])
        for index in range(band):
            sample += tables[0, index, time] * estimates[index] + tables[1, index, time] * turned[index]
        thinned = thin_out(sample * scale)
        total += tables[0, 0, time] * thinned - tables[1, 0, time] * (pltpu.roll(thinned, half, 1) * turn)
    out[...] = total * scale


def call(kernel, name, outs, inputs, scratch=(), flops=0, spaces=(), limit=VMEM_LIMIT):
    spaces = (*spaces, *[pltpu.VMEM] * (len(inputs) - len(spaces)))
    moved = sum(x.size * x.dtype.itemsize for x in [*inputs, *outs]) if flops else 0
    return pl.pallas_call(
        kernel,
        out_shape=outs,
        in_specs=[pl.BlockSpec(memory_space=space) for space in spaces],
        out_specs=[pl.BlockSpec(memory_space=pltpu.VMEM)] * len(outs),
        scratch_shapes=scratch,
        compiler_params=pltpu.CompilerParams(vmem_limit_bytes=limit),
        cost_estimate=pl.CostEstimate(flops=flops, bytes_accessed=moved, transcendentals=0),
        name=name,
    )(*inputs)


def to_mate(value):
    return lax.ppermute(value, "tile", [(i, i ^ 1) for i in range(lax.axis_size("tile"))])


def across(value, shift):
    count, band = lax.axis_size("tile"), lax.axis_size("freq")
    pairs = [(i * band + f, (i ^ 1) * band + (f - shift) % band) for i in range(count) for f in range(band)]
    return lax.ppermute(value, ("tile", "freq"), pairs)


def after(value, *others):
    return lax.optimization_barrier((value, *others))[0]


def exchange(sends, routes, beside):
    arrived = []
    for send, pair in zip(sends, routes):
        pairs = [(2 * at + core, 2 * to + 1 - core) for core in range(2) for at, to in enumerate(pair[core])]
        arrived.append(lax.ppermute(send, "tile", sorted(pairs)))
    return [after(arrived[0], *beside), *arrived[1:]]


def body(u_factors, v_factors, ranks, observed, start):
    band = lax.axis_size("freq")
    rows, tiles, width = u_factors.shape[1:]
    sources = start.shape[2]
    columns = tiles * width
    left_rows = u_factors.reshape(rows * tiles, width)
    right_rows = v_factors.reshape(rows * tiles, width)
    observed = observed.reshape(rows, sources)
    start = start.reshape(rows, sources)
    routes, back_routes = routes_of(tiles)
    arrivals, back_arrivals = arrivals_of(routes), arrivals_of(back_routes)
    places = [
        [
            [[came[core][chip] for came in arrivals].index(to) for chip, to in enumerate(pair[core])]
            for core in range(2)
        ]
        for pair in back_routes
    ]

    def shape(*dims, dtype=BF16):
        return jax.ShapeDtypeStruct(dims, dtype)

    members = tiles // 2
    wide = pltpu.VMEM((rows * tiles, width), F32)
    block = shape(sources // 2, width)
    blocks = shape(members, sources // 2, width)
    factor = shape(rows, members * width)
    flops = 2 * rows * columns * sources

    keep, give = call(
        functools.partial(forward_kernel, routes),
        "forward",
        [blocks, blocks],
        [start, right_rows],
        [
            pltpu.VMEM(start.shape, F32),
            pltpu.VMEM(right_rows.shape, BF16),
            wide,
            pltpu.VMEM((rows, columns), BF16),
            pltpu.VMEM((tiles, sources // 2, width), BF16),
            pltpu.SemaphoreType.DMA((PIECES + 1,)),
        ],
        flops,
        [pltpu.HBM] * 2,
        FIRST_LIMIT,
    )
    sends = call(add_kernel, "add", [block] * members, [keep, to_mate(give)], flops=HIDE * flops)
    mate_left = to_mate(after(left_rows, give))
    both_left, turned, start = call(
        functools.partial(rows_kernel, arrivals),
        "rows",
        [shape(2 * rows, members * width), shape(sources, rows, dtype=F32), shape(rows, sources, dtype=F32)],
        [ranks, after(left_rows, give), mate_left, after(observed, give), after(start, give)],
        [wide],
        spaces=[pltpu.SMEM],
    )
    starts = [start]
    for shift in range(1, band):
        starts.append(lax.ppermute(start, "freq", [(f, (f - shift) % band) for f in range(band)]))
    arrived = exchange(sends, routes, [both_left, turned])
    misfit = shape(sources, 2 * rows, dtype=F32)
    (misfit_early,) = call(
        early_kernel,
        "early",
        [misfit],
        [*arrived[:2], both_left, turned],
        [pltpu.VMEM((sources, 2 * width), BF16)],
        flops // 2,
    )
    (misfit,) = call(
        image_kernel,
        "image",
        [misfit],
        [*arrived[2:], misfit_early, both_left],
        [pltpu.VMEM((sources, (members - 2) * width), BF16)],
        HIDE * flops,
    )
    mate_right = to_mate(after(right_rows, both_left))
    mate_right = call(functools.partial(columns_kernel, back_arrivals), "columns", [factor] * 2, [mate_right], [wide])
    sends = call(
        functools.partial(back_kernel, places),
        "back",
        [block] * members,
        [misfit, to_mate(misfit), both_left],
        [pltpu.VMEM((members, sources // 2, width), BF16)],
        flops,
    )
    (own,) = call(pack_kernel, "pack", [blocks], exchange(sends, back_routes, [*mate_right, *starts[1:]]))
    spread = shape(sources, members * width)
    part, own_left = call(
        part_kernel, "part", [shape(rows, sources, dtype=F32), spread], [own, mate_right[0]], flops=flops // 2
    )
    gradient, other_left = call(
        gradient_kernel,
        "gradient",
        [shape(rows, sources), spread],
        [part, to_mate(own), mate_right[1]],
        flops=flops // 2,
    )
    right = call(
        functools.partial(columns_kernel, back_arrivals), "columns", [factor] * 2, [after(right_rows, gradient)], [wide]
    )
    gradients = []
    for shift in range(1, band):
        gradients.append(across(gradient, shift))
    result = shape(rows, sources, dtype=F32)
    if band == 2:
        halves = call(pair_kernel, "pair", [result] * 2, [*right, own_left, other_left, *starts], flops=flops)
        (estimate,) = call(shrink_pair_kernel, "shrink", [result], [*halves, *gradients])
        return estimate[None]
    bands = jnp.arange(band, dtype=jnp.int32)
    phases = (bands[:, None] + lax.axis_index("freq")) * bands[None, :] % band
    phases = (2.0 * math.pi / band) * phases.astype(F32)
    tables = jnp.stack([jnp.cos(phases), jnp.sin(phases)])
    (estimate,) = call(step_kernel, "step", [result], [*right, own_left, other_left, start], flops=flops)
    (estimate,) = call(
        functools.partial(shrink_kernel, band),
        "shrink",
        [result],
        [tables, estimate, *starts[1:], *gradients],
        spaces=[pltpu.SMEM],
    )
    return estimate[None]


def solution(mesh):
    in_specs = (
        P("freq", "tile", None, None),
        P("freq", "tile", None, None),
        P("freq", None, None),
        P("freq", "tile", None),
        P("freq", "tile", None),
    )
    out_specs = P("freq", "tile", None)
    return jax.shard_map(body, mesh=mesh, in_specs=in_specs, out_specs=out_specs, check_vma=False)
```

```python
import functools
import math

import jax
import jax.numpy as jnp
from jax import lax
from jax.experimental import pallas as pl
from jax.experimental.pallas import tpu as pltpu
from jax.sharding import PartitionSpec as P

STEP_SIZE = 0.2
LEVEL = 0.5
LANES = 128
VMEM_LIMIT = 32 * 1024 * 1024
FIRST_LIMIT = 55050 * 1024
PIECES = 4
HIDE = 128
F32 = jnp.float32
BF16 = jnp.bfloat16


MEETINGS = {
    8: [
        [(0o77666677, 0o55555555), (0o11777711, 0o34444443), (0o66001166, 0o43333334), (0o00110000, 0o22222222)],
        [(0o22555533, 0o77060677), (0o55223355, 0o16777761), (0o44444444, 0o61606016), (0o33332222, 0o00111100)],
    ]
}


def routes_of(chips):
    if chips in MEETINGS:
        shifts = [
            [[[packed >> 3 * chip & 7 for chip in range(chips)] for packed in pair] for pair in way]
            for way in MEETINGS[chips]
        ]
    else:
        far = range(chips - 1, 3, -1)
        first = [*[shift for shift in far if shift % 2], 1, 0]
        second = [*[shift for shift in far if shift % 2 == 0], 3, 2]
        out = [[[shift] * chips for shift in pair] for pair in zip(first, second)]
        shifts = [out, [pair[::-1] for pair in out]]
    return [[[[chip ^ shift for chip, shift in enumerate(core)] for core in pair] for pair in way] for way in shifts]


def arrivals_of(routes):
    return [[[pair[1 - core].index(chip) for chip in range(len(pair[core]))] for core in range(2)] for pair in routes]


def place():
    position = lax.axis_index("tile")
    return position // 2, position % 2


def columns_of(tile):
    return pl.ds(pl.multiple_of(tile * LANES, LANES), LANES)


def entry(first, second):
    chip, core = place()
    if len(set(first)) == 1 and len(set(second)) == 1:
        return jnp.where(core == 0, first[0], second[0])
    bits = max(*first, *second).bit_length()
    first, second = [sum(value << bits * at for at, value in enumerate(values)) for values in (first, second)]
    return jnp.where(core == 0, first, second) >> bits * chip & (1 << bits) - 1


def both_tiles(routes):
    chip, _ = place()
    shifts = [[[at ^ other for at, other in enumerate(core)] for core in pair] for pair in routes]
    return [chip ^ entry(*pair) for pair in shifts], [chip ^ entry(*pair[::-1]) for pair in shifts]


def signs(rows):
    lane = lax.broadcasted_iota(jnp.int32, (rows, LANES), 1)
    return jnp.where(lane < LANES // 2, 1.0, -1.0).astype(F32)


def pick(wide, target, chosen, masks=None):
    rows = target.shape[0]
    tiles = wide.shape[0] // rows
    for index, tile in enumerate(chosen):
        part = wide[pl.ds(tile, rows, stride=tiles), :]
        if masks is not None:
            part = jnp.where(masks[index], part, 0.0)
        target[:, index * LANES : (index + 1) * LANES] = part.astype(BF16)


def separate(source, wide, target, chosen, masks=None):
    wide[...] = source[...].astype(F32)
    pick(wide, target, chosen, masks)


def adjoint_blocks(values, factors):
    half = values.shape[0] // 2
    pair = 2 * LANES
    blocks = []
    for at in range(0, factors.shape[1], pair):
        product = jnp.dot(values, factors[:, at : at + pair], preferred_element_type=F32)
        for lanes in (slice(0, LANES), slice(LANES, pair)):
            real, imaginary = product[:half, lanes], product[half:, lanes]
            blocks.append((real * signs(half) + pltpu.roll(imaginary, LANES // 2, 1)).astype(BF16))
    return blocks


def spread_block(block, left, tile):
    half = block.shape[0]
    left[:half, columns_of(tile)] = block * signs(half).astype(BF16)
    left[half:, columns_of(tile)] = pltpu.roll(block, LANES // 2, 1)


def times_transposed(left, right):
    return lax.dot_general(left, right, (((1,), (1,)), ((), ())), preferred_element_type=F32)


def forward_kernel(routes, start, factors, keep, give, start_here, factors_here, wide, separated, blocks, sems):
    pieces = sems.shape[0] - 1
    rows, columns = separated.shape
    tiles = columns // LANES
    load_start = pltpu.make_async_copy(start, start_here, sems.at[pieces])
    load_start.start()
    loads = []
    for piece in range(pieces):
        at = pl.ds(piece * (rows * tiles // pieces), rows * tiles // pieces)
        loads.append(pltpu.make_async_copy(factors.at[at], factors_here.at[at], sems.at[piece]))
        loads[-1].start()
    load_start.wait()
    values = start_here[...].T.astype(BF16)
    for piece, load in enumerate(loads):
        at = pl.ds(piece * (rows * tiles // pieces), rows * tiles // pieces)
        load.wait()
        separate(
            factors_here.at[at], wide.at[at], separated.at[pl.ds(piece * (rows // pieces), rows // pieces)], range(tiles)
        )
    for tile, block in enumerate(adjoint_blocks(values, separated)):
        blocks[tile] = block
    for out, chosen in zip((keep, give), both_tiles(routes)):
        for index, tile in enumerate(chosen):
            out[index] = blocks[tile]


def add_kernel(keep, arrived, *outs):
    for index, out in enumerate(outs):
        out[...] = (keep[index].astype(F32) + arrived[index].astype(F32)).astype(BF16)


def rows_kernel(arrivals, ranks, own, mate, observed, start, both, turned, start_out, wide):
    chip, _ = place()
    chosen, _ = both_tiles(arrivals)
    rows = both.shape[0] // 2
    lane = lax.broadcasted_iota(jnp.int32, (1, LANES), 1) % (LANES // 2)
    masks = [lane < ranks[0, chip, tile] for tile in chosen]
    separate(own, wide, both.at[:rows], chosen, masks)
    separate(mate, wide, both.at[rows:], chosen, masks)
    turned[...] = observed[...].T
    start_out[...] = start[...]


def columns_kernel(arrivals, factors, own, other, wide):
    chosen, rest = both_tiles(arrivals)
    separate(factors, wide, own, chosen)
    pick(wide, other, rest)


def early_kernel(first, second, factors, observed, misfit, left):
    for index, block in enumerate((first, second)):
        spread_block(block[...], left, index)
    rows = observed.shape[1]
    image = times_transposed(left[...], factors[:, : left.shape[1]])
    misfit[:, :rows] = image[:, :rows] - observed[...]
    misfit[:, rows:] = image[:, rows:]


def image_kernel(*refs):
    blocks, (early, factors, misfit, left) = refs[:-4], refs[-4:]
    for index, block in enumerate(blocks):
        spread_block(block[...], left, index)
    misfit[...] = early[...] + times_transposed(left[...], factors[:, -left.shape[1] :])


def back_kernel(places, here, there, factors, *refs):
    outs, blocks = refs[:-1], refs[-1]
    rows = here.shape[1] // 2
    parts = []
    for side in range(2):
        at, other = pl.ds(side * rows, rows), pl.ds((1 - side) * rows, rows)
        misfit = (here[:, at] + there[:, other]).astype(BF16)
        parts.append(adjoint_blocks(misfit, factors.at[at]))
    for index, (first, second) in enumerate(zip(*parts)):
        blocks[index] = (first.astype(F32) + second.astype(F32)).astype(BF16)
    for out, pair in zip(outs, places):
        out[...] = blocks[entry(*pair)]


def pack_kernel(*refs):
    for index, block in enumerate(refs[:-1]):
        refs[-1][index] = block[...]


def part_kernel(blocks, factors, part, left):
    for index in range(blocks.shape[0]):
        spread_block(blocks[index], left, index)
    part[...] = times_transposed(factors[...], left[...])


def gradient_kernel(part, blocks, factors, gradient, left):
    for index in range(blocks.shape[0]):
        spread_block(blocks[index], left, index)
    gradient[...] = (part[...] + times_transposed(factors[...], left[...])).astype(BF16)


def step_kernel(own, other, own_left, other_left, start, estimate):
    gradient = times_transposed(own[...], own_left[...]) + times_transposed(other[...], other_left[...])
    estimate[...] = start[...] - STEP_SIZE * gradient


def pair_kernel(own, other, own_left, other_left, here, there, total, difference):
    scale = 1.0 / math.sqrt(2)
    gradient = times_transposed(own[...], own_left[...]) + times_transposed(other[...], other_left[...])
    estimate = here[...] - STEP_SIZE * gradient
    total[...] = (estimate + there[...]) * scale
    difference[...] = (estimate - there[...]) * scale


def thin_out(values):
    return values - jnp.clip(values, -LEVEL, LEVEL)


def shrink_pair_kernel(total, difference, gradient, out):
    scale = 1.0 / math.sqrt(2)
    step = (STEP_SIZE * scale) * gradient[...].astype(F32)
    out[...] = (thin_out(total[...] - step) + thin_out(difference[...] + step)) * scale


def shrink_kernel(band, *refs):
    tables, own, starts, gradients, out = refs[0], refs[1], refs[2 : band + 1], refs[band + 1 : -1], refs[-1]
    others = [start[...] - STEP_SIZE * gradient[...].astype(F32) for start, gradient in zip(starts, gradients)]
    estimates = [own[...], *others]
    scale = 1.0 / math.sqrt(band)
    half = out.shape[1] // 2
    lane = lax.broadcasted_iota(jnp.int32, (1, out.shape[1]), 1)
    turn = jnp.where(lane < half, -1.0, 1.0).astype(F32)
    turned = [pltpu.roll(estimate, half, 1) * turn for estimate in estimates]
    total = jnp.zeros_like(estimates[0])
    for time in range(band):
        sample = jnp.zeros_like(estimates[0])
        for index in range(band):
            sample += tables[0, index, time] * estimates[index] + tables[1, index, time] * turned[index]
        thinned = thin_out(sample * scale)
        total += tables[0, 0, time] * thinned - tables[1, 0, time] * (pltpu.roll(thinned, half, 1) * turn)
    out[...] = total * scale


def call(kernel, name, outs, inputs, scratch=(), flops=0, spaces=(), limit=VMEM_LIMIT):
    spaces = (*spaces, *[pltpu.VMEM] * (len(inputs) - len(spaces)))
    moved = sum(x.size * x.dtype.itemsize for x in [*inputs, *outs]) if flops else 0
    return pl.pallas_call(
        kernel,
        out_shape=outs,
        in_specs=[pl.BlockSpec(memory_space=space) for space in spaces],
        out_specs=[pl.BlockSpec(memory_space=pltpu.VMEM)] * len(outs),
        scratch_shapes=scratch,
        compiler_params=pltpu.CompilerParams(vmem_limit_bytes=limit),
        cost_estimate=pl.CostEstimate(flops=flops, bytes_accessed=moved, transcendentals=0),
        name=name,
    )(*inputs)


def to_mate(value):
    return lax.ppermute(value, "tile", [(i, i ^ 1) for i in range(lax.axis_size("tile"))])


def across(value, shift):
    count, band = lax.axis_size("tile"), lax.axis_size("freq")
    pairs = [(i * band + f, (i ^ 1) * band + (f - shift) % band) for i in range(count) for f in range(band)]
    return lax.ppermute(value, ("tile", "freq"), pairs)


def after(value, *others):
    return lax.optimization_barrier((value, *others))[0]


def exchange(sends, routes, beside):
    arrived = []
    for send, pair in zip(sends, routes):
        pairs = [(2 * at + core, 2 * to + 1 - core) for core in range(2) for at, to in enumerate(pair[core])]
        arrived.append(lax.ppermute(send, "tile", sorted(pairs)))
    return [after(arrived[0], *beside), *arrived[1:]]


def body(u_factors, v_factors, ranks, observed, start):
    band = lax.axis_size("freq")
    rows, tiles, width = u_factors.shape[1:]
    sources = start.shape[2]
    columns = tiles * width
    left_rows = u_factors.reshape(rows * tiles, width)
    right_rows = v_factors.reshape(rows * tiles, width)
    observed = observed.reshape(rows, sources)
    start = start.reshape(rows, sources)
    routes, back_routes = routes_of(tiles)
    arrivals, back_arrivals = arrivals_of(routes), arrivals_of(back_routes)
    places = [
        [
            [[came[core][chip] for came in arrivals].index(to) for chip, to in enumerate(pair[core])]
            for core in range(2)
        ]
        for pair in back_routes
    ]

    def shape(*dims, dtype=BF16):
        return jax.ShapeDtypeStruct(dims, dtype)

    members = tiles // 2
    wide = pltpu.VMEM((rows * tiles, width), F32)
    block = shape(sources // 2, width)
    blocks = shape(members, sources // 2, width)
    factor = shape(rows, members * width)
    flops = 2 * rows * columns * sources

    keep, give = call(
        functools.partial(forward_kernel, routes),
        "forward",
        [blocks, blocks],
        [start, right_rows],
        [
            pltpu.VMEM(start.shape, F32),
            pltpu.VMEM(right_rows.shape, BF16),
            wide,
            pltpu.VMEM((rows, columns), BF16),
            pltpu.VMEM((tiles, sources // 2, width), BF16),
            pltpu.SemaphoreType.DMA((PIECES + 1,)),
        ],
        flops,
        [pltpu.HBM] * 2,
        FIRST_LIMIT,
    )
    sends = call(add_kernel, "add", [block] * members, [keep, to_mate(give)], flops=HIDE * flops)
    mate_left = to_mate(after(left_rows, give))
    both_left, turned, start = call(
        functools.partial(rows_kernel, arrivals),
        "rows",
        [shape(2 * rows, members * width), shape(sources, rows, dtype=F32), shape(rows, sources, dtype=F32)],
        [ranks, after(left_rows, give), mate_left, after(observed, give), after(start, give)],
        [wide],
        spaces=[pltpu.SMEM],
    )
    starts = [start]
    for shift in range(1, band):
        starts.append(lax.ppermute(start, "freq", [(f, (f - shift) % band) for f in range(band)]))
    arrived = exchange(sends, routes, [both_left, turned])
    misfit = shape(sources, 2 * rows, dtype=F32)
    (misfit_early,) = call(
        early_kernel,
        "early",
        [misfit],
        [*arrived[:2], both_left, turned],
        [pltpu.VMEM((sources, 2 * width), BF16)],
        flops // 2,
    )
    (misfit,) = call(
        image_kernel,
        "image",
        [misfit],
        [*arrived[2:], misfit_early, both_left],
        [pltpu.VMEM((sources, (members - 2) * width), BF16)],
        HIDE * flops,
    )
    mate_right = to_mate(after(right_rows, both_left))
    mate_right = call(functools.partial(columns_kernel, back_arrivals), "columns", [factor] * 2, [mate_right], [wide])
    sends = call(
        functools.partial(back_kernel, places),
        "back",
        [block] * members,
        [misfit, to_mate(misfit), both_left],
        [pltpu.VMEM((members, sources // 2, width), BF16)],
        flops,
    )
    (own,) = call(pack_kernel, "pack", [blocks], exchange(sends, back_routes, [*mate_right, *starts[1:]]))
    spread = shape(sources, members * width)
    part, own_left = call(
        part_kernel, "part", [shape(rows, sources, dtype=F32), spread], [own, mate_right[0]], flops=flops // 2
    )
    gradient, other_left = call(
        gradient_kernel,
        "gradient",
        [shape(rows, sources), spread],
        [part, to_mate(own), mate_right[1]],
        flops=flops // 2,
    )
    right = call(
        functools.partial(columns_kernel, back_arrivals), "columns", [factor] * 2, [after(right_rows, gradient)], [wide]
    )
    gradients = []
    for shift in range(1, band):
        gradients.append(across(gradient, shift))
    result = shape(rows, sources, dtype=F32)
    if band == 2:
        halves = call(pair_kernel, "pair", [result] * 2, [*right, own_left, other_left, *starts], flops=flops)
        (estimate,) = call(shrink_pair_kernel, "shrink", [result], [*halves, *gradients])
        return estimate[None]
    bands = jnp.arange(band, dtype=jnp.int32)
    phases = (bands[:, None] + lax.axis_index("freq")) * bands[None, :] % band
    phases = (2.0 * math.pi / band) * phases.astype(F32)
    tables = jnp.stack([jnp.cos(phases), jnp.sin(phases)])
    (estimate,) = call(step_kernel, "step", [result], [*right, own_left, other_left, start], flops=flops)
    (estimate,) = call(
        functools.partial(shrink_kernel, band),
        "shrink",
        [result],
        [tables, estimate, *starts[1:], *gradients],
        spaces=[pltpu.SMEM],
    )
    return estimate[None]


def solution(mesh):
    in_specs = (
        P("freq", "tile", None, None),
        P("freq", "tile", None, None),
        P("freq", None, None),
        P("freq", "tile", None),
        P("freq", "tile", None),
    )
    out_specs = P("freq", "tile", None)
    return jax.shard_map(body, mesh=mesh, in_specs=in_specs, out_specs=out_specs, check_vma=False)
```

```python
import functools
import math

import jax
import jax.numpy as jnp
from jax import lax
from jax.experimental import pallas as pl
from jax.experimental.pallas import tpu as pltpu
from jax.sharding import PartitionSpec as P

STEP_SIZE = 0.2
LEVEL = 0.5
LANES = 128
VMEM_LIMIT = 32 * 1024 * 1024
FIRST_LIMIT = 55050 * 1024
PIECES = 4
HIDE = 128
F32 = jnp.float32
BF16 = jnp.bfloat16


MEETINGS = {
    8: [
        [(0o77666677, 0o55555555), (0o11777711, 0o34444443), (0o66001166, 0o43333334), (0o00110000, 0o22222222)],
        [(0o22555533, 0o77060677), (0o55223355, 0o16777761), (0o44444444, 0o61606016), (0o33332222, 0o00111100)],
    ]
}


def routes_of(chips):
    if chips in MEETINGS:
        shifts = [
            [[[packed >> 3 * chip & 7 for chip in range(chips)] for packed in pair] for pair in way]
            for way in MEETINGS[chips]
        ]
    else:
        far = range(chips - 1, 3, -1)
        first = [*[shift for shift in far if shift % 2], 1, 0]
        second = [*[shift for shift in far if shift % 2 == 0], 3, 2]
        out = [[[shift] * chips for shift in pair] for pair in zip(first, second)]
        shifts = [out, [pair[::-1] for pair in out]]
    return [[[[chip ^ shift for chip, shift in enumerate(core)] for core in pair] for pair in way] for way in shifts]


def arrivals_of(routes):
    return [[[pair[1 - core].index(chip) for chip in range(len(pair[core]))] for core in range(2)] for pair in routes]


def place():
    position = lax.axis_index("tile")
    return position // 2, position % 2


def columns_of(tile):
    return pl.ds(pl.multiple_of(tile * LANES, LANES), LANES)


def entry(first, second):
    chip, core = place()
    if len(set(first)) == 1 and len(set(second)) == 1:
        return jnp.where(core == 0, first[0], second[0])
    bits = max(*first, *second).bit_length()
    first, second = [sum(value << bits * at for at, value in enumerate(values)) for values in (first, second)]
    return jnp.where(core == 0, first, second) >> bits * chip & (1 << bits) - 1


def both_tiles(routes):
    chip, _ = place()
    shifts = [[[at ^ other for at, other in enumerate(core)] for core in pair] for pair in routes]
    return [chip ^ entry(*pair) for pair in shifts], [chip ^ entry(*pair[::-1]) for pair in shifts]


def signs(rows):
    lane = lax.broadcasted_iota(jnp.int32, (rows, LANES), 1)
    return jnp.where(lane < LANES // 2, 1.0, -1.0).astype(F32)


def pick(wide, target, chosen, masks=None):
    rows = target.shape[0]
    tiles = wide.shape[0] // rows
    for index, tile in enumerate(chosen):
        part = wide[pl.ds(tile, rows, stride=tiles), :]
        if masks is not None:
            part = jnp.where(masks[index], part, 0.0)
        target[:, index * LANES : (index + 1) * LANES] = part.astype(BF16)


def separate(source, wide, target, chosen, masks=None):
    wide[...] = source[...].astype(F32)
    pick(wide, target, chosen, masks)


def adjoint_blocks(values, factors):
    half = values.shape[0] // 2
    pair = 2 * LANES
    blocks = []
    for at in range(0, factors.shape[1], pair):
        product = jnp.dot(values, factors[:, at : at + pair], preferred_element_type=F32)
        for lanes in (slice(0, LANES), slice(LANES, pair)):
            real, imaginary = product[:half, lanes], product[half:, lanes]
            blocks.append((real * signs(half) + pltpu.roll(imaginary, LANES // 2, 1)).astype(BF16))
    return blocks


def spread_block(block, left, tile):
    half = block.shape[0]
    left[:half, columns_of(tile)] = block * signs(half).astype(BF16)
    left[half:, columns_of(tile)] = pltpu.roll(block, LANES // 2, 1)


def times_transposed(left, right):
    return lax.dot_general(left, right, (((1,), (1,)), ((), ())), preferred_element_type=F32)


def forward_kernel(routes, start, factors, keep, give, start_here, factors_here, wide, separated, blocks, sems):
    pieces = sems.shape[0] - 1
    rows, columns = separated.shape
    tiles = columns // LANES
    load_start = pltpu.make_async_copy(start, start_here, sems.at[pieces])
    load_start.start()
    loads = []
    for piece in range(pieces):
        at = pl.ds(piece * (rows * tiles // pieces), rows * tiles // pieces)
        loads.append(pltpu.make_async_copy(factors.at[at], factors_here.at[at], sems.at[piece]))
        loads[-1].start()
    load_start.wait()
    values = start_here[...].T.astype(BF16)
    for piece, load in enumerate(loads):
        at = pl.ds(piece * (rows * tiles // pieces), rows * tiles // pieces)
        load.wait()
        separate(
            factors_here.at[at], wide.at[at], separated.at[pl.ds(piece * (rows // pieces), rows // pieces)], range(tiles)
        )
    for tile, block in enumerate(adjoint_blocks(values, separated)):
        blocks[tile] = block
    for out, chosen in zip((keep, give), both_tiles(routes)):
        for index, tile in enumerate(chosen):
            out[index] = blocks[tile]


def add_kernel(keep, arrived, *outs):
    for index, out in enumerate(outs):
        out[...] = (keep[index].astype(F32) + arrived[index].astype(F32)).astype(BF16)


def rows_kernel(arrivals, ranks, own, mate, observed, start, both, turned_both, turned, start_out, wide):
    chip, _ = place()
    chosen, _ = both_tiles(arrivals)
    rows = both.shape[0] // 2
    lane = lax.broadcasted_iota(jnp.int32, (1, LANES), 1) % (LANES // 2)
    masks = [lane < ranks[0, chip, tile] for tile in chosen]
    separate(own, wide, both.at[:rows], chosen, masks)
    separate(mate, wide, both.at[rows:], chosen, masks)
    for index in range(len(chosen)):
        columns = slice(index * LANES, (index + 1) * LANES)
        turned_both[columns, :] = both[:, columns].T
    turned[...] = observed[...].T
    start_out[...] = start[...]


def columns_kernel(arrivals, factors, own, other, wide):
    chosen, rest = both_tiles(arrivals)
    separate(factors, wide, own, chosen)
    pick(wide, other, rest)


def early_kernel(first, second, factors, observed, misfit, left):
    for index, block in enumerate((first, second)):
        spread_block(block[...], left, index)
    rows = observed.shape[1]
    image = jnp.dot(left[...], factors[: left.shape[1], :], preferred_element_type=F32)
    misfit[:, :rows] = image[:, :rows] - observed[...]
    misfit[:, rows:] = image[:, rows:]


def image_kernel(*refs):
    blocks, (early, factors, misfit, left) = refs[:-4], refs[-4:]
    for index, block in enumerate(blocks):
        spread_block(block[...], left, index)
    misfit[...] = early[...] + jnp.dot(left[...], factors[-left.shape[1] :, :], preferred_element_type=F32)


def back_kernel(places, here, there, factors, *refs):
    outs, blocks = refs[:-1], refs[-1]
    rows = here.shape[1] // 2
    parts = []
    for side in range(2):
        at, other = pl.ds(side * rows, rows), pl.ds((1 - side) * rows, rows)
        misfit = (here[:, at] + there[:, other]).astype(BF16)
        parts.append(adjoint_blocks(misfit, factors.at[at]))
    for index, (first, second) in enumerate(zip(*parts)):
        blocks[index] = (first.astype(F32) + second.astype(F32)).astype(BF16)
    for out, pair in zip(outs, places):
        out[...] = blocks[entry(*pair)]


def pack_kernel(*refs):
    for index, block in enumerate(refs[:-1]):
        refs[-1][index] = block[...]


def part_kernel(blocks, factors, part, left):
    for index in range(blocks.shape[0]):
        spread_block(blocks[index], left, index)
    part[...] = times_transposed(factors[...], left[...])


def gradient_kernel(part, blocks, factors, gradient, left):
    for index in range(blocks.shape[0]):
        spread_block(blocks[index], left, index)
    gradient[...] = (part[...] + times_transposed(factors[...], left[...])).astype(BF16)


def step_kernel(own, other, own_left, other_left, start, estimate):
    gradient = times_transposed(own[...], own_left[...]) + times_transposed(other[...], other_left[...])
    estimate[...] = start[...] - STEP_SIZE * gradient


def pair_kernel(own, other, own_left, other_left, here, there, total, difference):
    scale = 1.0 / math.sqrt(2)
    gradient = times_transposed(own[...], own_left[...]) + times_transposed(other[...], other_left[...])
    estimate = here[...] - STEP_SIZE * gradient
    total[...] = (estimate + there[...]) * scale
    difference[...] = (estimate - there[...]) * scale


def thin_out(values):
    return values - jnp.clip(values, -LEVEL, LEVEL)


def shrink_pair_kernel(total, difference, gradient, out):
    scale = 1.0 / math.sqrt(2)
    step = (STEP_SIZE * scale) * gradient[...].astype(F32)
    out[...] = (thin_out(total[...] - step) + thin_out(difference[...] + step)) * scale


def shrink_kernel(band, *refs):
    tables, own, starts, gradients, out = refs[0], refs[1], refs[2 : band + 1], refs[band + 1 : -1], refs[-1]
    others = [start[...] - STEP_SIZE * gradient[...].astype(F32) for start, gradient in zip(starts, gradients)]
    estimates = [own[...], *others]
    scale = 1.0 / math.sqrt(band)
    half = out.shape[1] // 2
    lane = lax.broadcasted_iota(jnp.int32, (1, out.shape[1]), 1)
    turn = jnp.where(lane < half, -1.0, 1.0).astype(F32)
    turned = [pltpu.roll(estimate, half, 1) * turn for estimate in estimates]
    total = jnp.zeros_like(estimates[0])
    for time in range(band):
        sample = jnp.zeros_like(estimates[0])
        for index in range(band):
            sample += tables[0, index, time] * estimates[index] + tables[1, index, time] * turned[index]
        thinned = thin_out(sample * scale)
        total += tables[0, 0, time] * thinned - tables[1, 0, time] * (pltpu.roll(thinned, half, 1) * turn)
    out[...] = total * scale


def call(kernel, name, outs, inputs, scratch=(), flops=0, spaces=(), limit=VMEM_LIMIT):
    spaces = (*spaces, *[pltpu.VMEM] * (len(inputs) - len(spaces)))
    moved = sum(x.size * x.dtype.itemsize for x in [*inputs, *outs]) if flops else 0
    return pl.pallas_call(
        kernel,
        out_shape=outs,
        in_specs=[pl.BlockSpec(memory_space=space) for space in spaces],
        out_specs=[pl.BlockSpec(memory_space=pltpu.VMEM)] * len(outs),
        scratch_shapes=scratch,
        compiler_params=pltpu.CompilerParams(vmem_limit_bytes=limit),
        cost_estimate=pl.CostEstimate(flops=flops, bytes_accessed=moved, transcendentals=0),
        name=name,
    )(*inputs)


def to_mate(value):
    return lax.ppermute(value, "tile", [(i, i ^ 1) for i in range(lax.axis_size("tile"))])


def across(value, shift):
    count, band = lax.axis_size("tile"), lax.axis_size("freq")
    pairs = [(i * band + f, (i ^ 1) * band + (f - shift) % band) for i in range(count) for f in range(band)]
    return lax.ppermute(value, ("tile", "freq"), pairs)


def after(value, *others):
    return lax.optimization_barrier((value, *others))[0]


def exchange(sends, routes, beside):
    arrived = []
    for send, pair in zip(sends, routes):
        pairs = [(2 * at + core, 2 * to + 1 - core) for core in range(2) for at, to in enumerate(pair[core])]
        arrived.append(lax.ppermute(send, "tile", sorted(pairs)))
    return [after(arrived[0], *beside), *arrived[1:]]


def body(u_factors, v_factors, ranks, observed, start):
    band = lax.axis_size("freq")
    rows, tiles, width = u_factors.shape[1:]
    sources = start.shape[2]
    columns = tiles * width
    left_rows = u_factors.reshape(rows * tiles, width)
    right_rows = v_factors.reshape(rows * tiles, width)
    observed = observed.reshape(rows, sources)
    start = start.reshape(rows, sources)
    routes, back_routes = routes_of(tiles)
    arrivals, back_arrivals = arrivals_of(routes), arrivals_of(back_routes)
    places = [
        [
            [[came[core][chip] for came in arrivals].index(to) for chip, to in enumerate(pair[core])]
            for core in range(2)
        ]
        for pair in back_routes
    ]

    def shape(*dims, dtype=BF16):
        return jax.ShapeDtypeStruct(dims, dtype)

    members = tiles // 2
    wide = pltpu.VMEM((rows * tiles, width), F32)
    block = shape(sources // 2, width)
    blocks = shape(members, sources // 2, width)
    factor = shape(rows, members * width)
    flops = 2 * rows * columns * sources

    keep, give = call(
        functools.partial(forward_kernel, routes),
        "forward",
        [blocks, blocks],
        [start, right_rows],
        [
            pltpu.VMEM(start.shape, F32),
            pltpu.VMEM(right_rows.shape, BF16),
            wide,
            pltpu.VMEM((rows, columns), BF16),
            pltpu.VMEM((tiles, sources // 2, width), BF16),
            pltpu.SemaphoreType.DMA((PIECES + 1,)),
        ],
        flops,
        [pltpu.HBM] * 2,
        FIRST_LIMIT,
    )
    sends = call(add_kernel, "add", [block] * members, [keep, to_mate(give)], flops=HIDE * flops)
    mate_left = to_mate(after(left_rows, give))
    both_left, turned_left, turned, start = call(
        functools.partial(rows_kernel, arrivals),
        "rows",
        [
            shape(2 * rows, members * width),
            shape(members * width, 2 * rows),
            shape(sources, rows, dtype=F32),
            shape(rows, sources, dtype=F32),
        ],
        [ranks, after(left_rows, give), mate_left, after(observed, give), after(start, give)],
        [wide],
        spaces=[pltpu.SMEM],
    )
    starts = [start]
    for shift in range(1, band):
        starts.append(lax.ppermute(start, "freq", [(f, (f - shift) % band) for f in range(band)]))
    arrived = exchange(sends, routes, [turned_left, turned])
    misfit = shape(sources, 2 * rows, dtype=F32)
    (misfit_early,) = call(
        early_kernel,
        "early",
        [misfit],
        [*arrived[:2], turned_left, turned],
        [pltpu.VMEM((sources, 2 * width), BF16)],
        flops // 2,
    )
    (misfit,) = call(
        image_kernel,
        "image",
        [misfit],
        [*arrived[2:], misfit_early, turned_left],
        [pltpu.VMEM((sources, (members - 2) * width), BF16)],
        HIDE * flops,
    )
    mate_right = to_mate(after(right_rows, both_left))
    mate_right = call(functools.partial(columns_kernel, back_arrivals), "columns", [factor] * 2, [mate_right], [wide])
    sends = call(
        functools.partial(back_kernel, places),
        "back",
        [block] * members,
        [misfit, to_mate(misfit), both_left],
        [pltpu.VMEM((members, sources // 2, width), BF16)],
        flops,
    )
    (own,) = call(pack_kernel, "pack", [blocks], exchange(sends, back_routes, [*mate_right, *starts[1:]]))
    spread = shape(sources, members * width)
    part, own_left = call(
        part_kernel, "part", [shape(rows, sources, dtype=F32), spread], [own, mate_right[0]], flops=flops // 2
    )
    gradient, other_left = call(
        gradient_kernel,
        "gradient",
        [shape(rows, sources), spread],
        [part, to_mate(own), mate_right[1]],
        flops=flops // 2,
    )
    right = call(
        functools.partial(columns_kernel, back_arrivals), "columns", [factor] * 2, [after(right_rows, gradient)], [wide]
    )
    gradients = []
    for shift in range(1, band):
        gradients.append(across(gradient, shift))
    result = shape(rows, sources, dtype=F32)
    if band == 2:
        halves = call(pair_kernel, "pair", [result] * 2, [*right, own_left, other_left, *starts], flops=flops)
        (estimate,) = call(shrink_pair_kernel, "shrink", [result], [*halves, *gradients])
        return estimate[None]
    bands = jnp.arange(band, dtype=jnp.int32)
    phases = (bands[:, None] + lax.axis_index("freq")) * bands[None, :] % band
    phases = (2.0 * math.pi / band) * phases.astype(F32)
    tables = jnp.stack([jnp.cos(phases), jnp.sin(phases)])
    (estimate,) = call(step_kernel, "step", [result], [*right, own_left, other_left, start], flops=flops)
    (estimate,) = call(
        functools.partial(shrink_kernel, band),
        "shrink",
        [result],
        [tables, estimate, *starts[1:], *gradients],
        spaces=[pltpu.SMEM],
    )
    return estimate[None]


def solution(mesh):
    in_specs = (
        P("freq", "tile", None, None),
        P("freq", "tile", None, None),
        P("freq", None, None),
        P("freq", "tile", None),
        P("freq", "tile", None),
    )
    out_specs = P("freq", "tile", None)
    return jax.shard_map(body, mesh=mesh, in_specs=in_specs, out_specs=out_specs, check_vma=False)
```

```python
import functools
import math

import jax
import jax.numpy as jnp
from jax import lax
from jax.experimental import pallas as pl
from jax.experimental.pallas import tpu as pltpu
from jax.sharding import PartitionSpec as P

STEP_SIZE = 0.2
LEVEL = 0.5
LANES = 128
VMEM_LIMIT = 32 * 1024 * 1024
FIRST_LIMIT = 55050 * 1024
PIECES = 4
HIDE = 128
F32 = jnp.float32
BF16 = jnp.bfloat16


MEETINGS = {
    8: [
        [(0o77666677, 0o55555555), (0o11777711, 0o34444443), (0o66001166, 0o43333334), (0o00110000, 0o22222222)],
        [(0o22555533, 0o77060677), (0o55223355, 0o16777761), (0o44444444, 0o61606016), (0o33332222, 0o00111100)],
    ]
}


def routes_of(chips):
    if chips in MEETINGS:
        shifts = [
            [[[packed >> 3 * chip & 7 for chip in range(chips)] for packed in pair] for pair in way]
            for way in MEETINGS[chips]
        ]
    else:
        far = range(chips - 1, 3, -1)
        first = [*[shift for shift in far if shift % 2], 1, 0]
        second = [*[shift for shift in far if shift % 2 == 0], 3, 2]
        out = [[[shift] * chips for shift in pair] for pair in zip(first, second)]
        shifts = [out, [pair[::-1] for pair in out]]
    return [[[[chip ^ shift for chip, shift in enumerate(core)] for core in pair] for pair in way] for way in shifts]


def arrivals_of(routes):
    return [[[pair[1 - core].index(chip) for chip in range(len(pair[core]))] for core in range(2)] for pair in routes]


def place():
    position = lax.axis_index("tile")
    return position // 2, position % 2


def columns_of(tile):
    return pl.ds(pl.multiple_of(tile * LANES, LANES), LANES)


def entry(first, second):
    chip, core = place()
    if len(set(first)) == 1 and len(set(second)) == 1:
        return jnp.where(core == 0, first[0], second[0])
    bits = max(*first, *second).bit_length()
    first, second = [sum(value << bits * at for at, value in enumerate(values)) for values in (first, second)]
    return jnp.where(core == 0, first, second) >> bits * chip & (1 << bits) - 1


def both_tiles(routes):
    chip, _ = place()
    shifts = [[[at ^ other for at, other in enumerate(core)] for core in pair] for pair in routes]
    return [chip ^ entry(*pair) for pair in shifts], [chip ^ entry(*pair[::-1]) for pair in shifts]


def signs(rows):
    lane = lax.broadcasted_iota(jnp.int32, (rows, LANES), 1)
    return jnp.where(lane < LANES // 2, 1.0, -1.0).astype(F32)


def pick(wide, target, chosen, masks=None):
    rows = target.shape[0]
    tiles = wide.shape[0] // rows
    for index, tile in enumerate(chosen):
        part = wide[pl.ds(tile, rows, stride=tiles), :]
        if masks is not None:
            part = jnp.where(masks[index], part, 0.0)
        target[:, index * LANES : (index + 1) * LANES] = part.astype(BF16)


def separate(source, wide, target, chosen, masks=None):
    wide[...] = source[...].astype(F32)
    pick(wide, target, chosen, masks)


def adjoint_blocks(values, factors):
    half = values.shape[0] // 2
    pair = 2 * LANES
    blocks = []
    for at in range(0, factors.shape[1], pair):
        product = jnp.dot(values, factors[:, at : at + pair], preferred_element_type=F32)
        for lanes in (slice(0, LANES), slice(LANES, pair)):
            real, imaginary = product[:half, lanes], product[half:, lanes]
            blocks.append((real * signs(half) + pltpu.roll(imaginary, LANES // 2, 1)).astype(BF16))
    return blocks


def spread_block(block, left, tile):
    half = block.shape[0]
    left[:half, columns_of(tile)] = block * signs(half).astype(BF16)
    left[half:, columns_of(tile)] = pltpu.roll(block, LANES // 2, 1)


def times_transposed(left, right):
    return lax.dot_general(left, right, (((1,), (1,)), ((), ())), preferred_element_type=F32)


def forward_kernel(routes, start, factors, keep, give, start_here, factors_here, wide, separated, blocks, sems):
    pieces = sems.shape[0] - 1
    rows, columns = separated.shape
    tiles = columns // LANES
    loads = []
    for piece in range(pieces):
        at = pl.ds(piece * (rows * tiles // pieces), rows * tiles // pieces)
        loads.append(pltpu.make_async_copy(factors.at[at], factors_here.at[at], sems.at[piece]))
        loads[-1].start()
    load_start = pltpu.make_async_copy(start, start_here, sems.at[pieces])
    load_start.start()
    for piece, load in enumerate(loads):
        at = pl.ds(piece * (rows * tiles // pieces), rows * tiles // pieces)
        load.wait()
        separate(
            factors_here.at[at], wide.at[at], separated.at[pl.ds(piece * (rows // pieces), rows // pieces)], range(tiles)
        )
    load_start.wait()
    values = start_here[...].T.astype(BF16)
    for tile, block in enumerate(adjoint_blocks(values, separated)):
        blocks[tile] = block
    for out, chosen in zip((keep, give), both_tiles(routes)):
        for index, tile in enumerate(chosen):
            out[index] = blocks[tile]


def add_kernel(keep, arrived, *outs):
    for index, out in enumerate(outs):
        out[...] = (keep[index].astype(F32) + arrived[index].astype(F32)).astype(BF16)


def rows_kernel(arrivals, ranks, own, mate, observed, start, both, turned_both, turned, start_out, wide):
    chip, _ = place()
    chosen, _ = both_tiles(arrivals)
    rows = both.shape[0] // 2
    lane = lax.broadcasted_iota(jnp.int32, (1, LANES), 1) % (LANES // 2)
    masks = [lane < ranks[0, chip, tile] for tile in chosen]
    separate(own, wide, both.at[:rows], chosen, masks)
    separate(mate, wide, both.at[rows:], chosen, masks)
    for index in range(len(chosen)):
        columns = slice(index * LANES, (index + 1) * LANES)
        turned_both[columns, :] = both[:, columns].T
    turned[...] = observed[...].T
    start_out[...] = start[...]


def columns_kernel(arrivals, factors, own, other, wide):
    chosen, rest = both_tiles(arrivals)
    separate(factors, wide, own, chosen)
    pick(wide, other, rest)


def early_kernel(first, second, factors, observed, misfit, left):
    for index, block in enumerate((first, second)):
        spread_block(block[...], left, index)
    rows = observed.shape[1]
    image = jnp.dot(left[...], factors[: left.shape[1], :], preferred_element_type=F32)
    misfit[:, :rows] = image[:, :rows] - observed[...]
    misfit[:, rows:] = image[:, rows:]


def image_kernel(*refs):
    blocks, (early, factors, misfit, left) = refs[:-4], refs[-4:]
    for index, block in enumerate(blocks):
        spread_block(block[...], left, index)
    misfit[...] = early[...] + jnp.dot(left[...], factors[-left.shape[1] :, :], preferred_element_type=F32)


def back_kernel(places, here, there, factors, *refs):
    outs, blocks = refs[:-1], refs[-1]
    rows = here.shape[1] // 2
    parts = []
    for side in range(2):
        at, other = pl.ds(side * rows, rows), pl.ds((1 - side) * rows, rows)
        misfit = (here[:, at] + there[:, other]).astype(BF16)
        parts.append(adjoint_blocks(misfit, factors.at[at]))
    for index, (first, second) in enumerate(zip(*parts)):
        blocks[index] = (first.astype(F32) + second.astype(F32)).astype(BF16)
    for out, pair in zip(outs, places):
        out[...] = blocks[entry(*pair)]


def pack_kernel(*refs):
    for index, block in enumerate(refs[:-1]):
        refs[-1][index] = block[...]


def part_kernel(blocks, factors, part, left):
    for index in range(blocks.shape[0]):
        spread_block(blocks[index], left, index)
    part[...] = times_transposed(factors[...], left[...])


def gradient_kernel(part, blocks, factors, gradient, left):
    for index in range(blocks.shape[0]):
        spread_block(blocks[index], left, index)
    gradient[...] = (part[...] + times_transposed(factors[...], left[...])).astype(BF16)


def step_kernel(own, other, own_left, other_left, start, estimate):
    gradient = times_transposed(own[...], own_left[...]) + times_transposed(other[...], other_left[...])
    estimate[...] = start[...] - STEP_SIZE * gradient


def pair_kernel(own, other, own_left, other_left, here, there, total, difference):
    scale = 1.0 / math.sqrt(2)
    gradient = times_transposed(own[...], own_left[...]) + times_transposed(other[...], other_left[...])
    estimate = here[...] - STEP_SIZE * gradient
    total[...] = (estimate + there[...]) * scale
    difference[...] = (estimate - there[...]) * scale


def thin_out(values):
    return values - jnp.clip(values, -LEVEL, LEVEL)


def shrink_pair_kernel(total, difference, gradient, out):
    scale = 1.0 / math.sqrt(2)
    step = (STEP_SIZE * scale) * gradient[...].astype(F32)
    out[...] = (thin_out(total[...] - step) + thin_out(difference[...] + step)) * scale


def shrink_kernel(band, *refs):
    tables, own, starts, gradients, out = refs[0], refs[1], refs[2 : band + 1], refs[band + 1 : -1], refs[-1]
    others = [start[...] - STEP_SIZE * gradient[...].astype(F32) for start, gradient in zip(starts, gradients)]
    estimates = [own[...], *others]
    scale = 1.0 / math.sqrt(band)
    half = out.shape[1] // 2
    lane = lax.broadcasted_iota(jnp.int32, (1, out.shape[1]), 1)
    turn = jnp.where(lane < half, -1.0, 1.0).astype(F32)
    turned = [pltpu.roll(estimate, half, 1) * turn for estimate in estimates]
    total = jnp.zeros_like(estimates[0])
    for time in range(band):
        sample = jnp.zeros_like(estimates[0])
        for index in range(band):
            sample += tables[0, index, time] * estimates[index] + tables[1, index, time] * turned[index]
        thinned = thin_out(sample * scale)
        total += tables[0, 0, time] * thinned - tables[1, 0, time] * (pltpu.roll(thinned, half, 1) * turn)
    out[...] = total * scale


def call(kernel, name, outs, inputs, scratch=(), flops=0, spaces=(), limit=VMEM_LIMIT):
    spaces = (*spaces, *[pltpu.VMEM] * (len(inputs) - len(spaces)))
    moved = sum(x.size * x.dtype.itemsize for x in [*inputs, *outs]) if flops else 0
    return pl.pallas_call(
        kernel,
        out_shape=outs,
        in_specs=[pl.BlockSpec(memory_space=space) for space in spaces],
        out_specs=[pl.BlockSpec(memory_space=pltpu.VMEM)] * len(outs),
        scratch_shapes=scratch,
        compiler_params=pltpu.CompilerParams(vmem_limit_bytes=limit),
        cost_estimate=pl.CostEstimate(flops=flops, bytes_accessed=moved, transcendentals=0),
        name=name,
    )(*inputs)


def to_mate(value):
    return lax.ppermute(value, "tile", [(i, i ^ 1) for i in range(lax.axis_size("tile"))])


def across(value, shift):
    count, band = lax.axis_size("tile"), lax.axis_size("freq")
    pairs = [(i * band + f, (i ^ 1) * band + (f - shift) % band) for i in range(count) for f in range(band)]
    return lax.ppermute(value, ("tile", "freq"), pairs)


def after(value, *others):
    return lax.optimization_barrier((value, *others))[0]


def exchange(sends, routes, beside):
    arrived = []
    for send, pair in zip(sends, routes):
        pairs = [(2 * at + core, 2 * to + 1 - core) for core in range(2) for at, to in enumerate(pair[core])]
        arrived.append(lax.ppermute(send, "tile", sorted(pairs)))
    return [after(arrived[0], *beside), *arrived[1:]]


def body(u_factors, v_factors, ranks, observed, start):
    band = lax.axis_size("freq")
    rows, tiles, width = u_factors.shape[1:]
    sources = start.shape[2]
    columns = tiles * width
    left_rows = u_factors.reshape(rows * tiles, width)
    right_rows = v_factors.reshape(rows * tiles, width)
    observed = observed.reshape(rows, sources)
    start = start.reshape(rows, sources)
    routes, back_routes = routes_of(tiles)
    arrivals, back_arrivals = arrivals_of(routes), arrivals_of(back_routes)
    places = [
        [
            [[came[core][chip] for came in arrivals].index(to) for chip, to in enumerate(pair[core])]
            for core in range(2)
        ]
        for pair in back_routes
    ]

    def shape(*dims, dtype=BF16):
        return jax.ShapeDtypeStruct(dims, dtype)

    members = tiles // 2
    wide = pltpu.VMEM((rows * tiles, width), F32)
    block = shape(sources // 2, width)
    blocks = shape(members, sources // 2, width)
    factor = shape(rows, members * width)
    flops = 2 * rows * columns * sources

    keep, give = call(
        functools.partial(forward_kernel, routes),
        "forward",
        [blocks, blocks],
        [start, right_rows],
        [
            pltpu.VMEM(start.shape, F32),
            pltpu.VMEM(right_rows.shape, BF16),
            wide,
            pltpu.VMEM((rows, columns), BF16),
            pltpu.VMEM((tiles, sources // 2, width), BF16),
            pltpu.SemaphoreType.DMA((PIECES + 1,)),
        ],
        flops,
        [pltpu.HBM] * 2,
        FIRST_LIMIT,
    )
    sends = call(add_kernel, "add", [block] * members, [keep, to_mate(give)], flops=HIDE * flops)
    mate_left = to_mate(after(left_rows, give))
    both_left, turned_left, turned, start = call(
        functools.partial(rows_kernel, arrivals),
        "rows",
        [
            shape(2 * rows, members * width),
            shape(members * width, 2 * rows),
            shape(sources, rows, dtype=F32),
            shape(rows, sources, dtype=F32),
        ],
        [ranks, after(left_rows, give), mate_left, after(observed, give), after(start, give)],
        [wide],
        spaces=[pltpu.SMEM],
    )
    starts = [start]
    for shift in range(1, band):
        starts.append(lax.ppermute(start, "freq", [(f, (f - shift) % band) for f in range(band)]))
    arrived = exchange(sends, routes, [turned_left, turned])
    misfit = shape(sources, 2 * rows, dtype=F32)
    (misfit_early,) = call(
        early_kernel,
        "early",
        [misfit],
        [*arrived[:2], turned_left, turned],
        [pltpu.VMEM((sources, 2 * width), BF16)],
        flops // 2,
    )
    (misfit,) = call(
        image_kernel,
        "image",
        [misfit],
        [*arrived[2:], misfit_early, turned_left],
        [pltpu.VMEM((sources, (members - 2) * width), BF16)],
        HIDE * flops,
    )
    mate_right = to_mate(after(right_rows, both_left))
    mate_right = call(functools.partial(columns_kernel, back_arrivals), "columns", [factor] * 2, [mate_right], [wide])
    sends = call(
        functools.partial(back_kernel, places),
        "back",
        [block] * members,
        [misfit, to_mate(misfit), both_left],
        [pltpu.VMEM((members, sources // 2, width), BF16)],
        flops,
    )
    (own,) = call(pack_kernel, "pack", [blocks], exchange(sends, back_routes, [*mate_right, *starts[1:]]))
    spread = shape(sources, members * width)
    part, own_left = call(
        part_kernel, "part", [shape(rows, sources, dtype=F32), spread], [own, mate_right[0]], flops=flops // 2
    )
    gradient, other_left = call(
        gradient_kernel,
        "gradient",
        [shape(rows, sources), spread],
        [part, to_mate(own), mate_right[1]],
        flops=flops // 2,
    )
    right = call(
        functools.partial(columns_kernel, back_arrivals), "columns", [factor] * 2, [after(right_rows, gradient)], [wide]
    )
    gradients = []
    for shift in range(1, band):
        gradients.append(across(gradient, shift))
    result = shape(rows, sources, dtype=F32)
    if band == 2:
        halves = call(pair_kernel, "pair", [result] * 2, [*right, own_left, other_left, *starts], flops=flops)
        (estimate,) = call(shrink_pair_kernel, "shrink", [result], [*halves, *gradients])
        return estimate[None]
    bands = jnp.arange(band, dtype=jnp.int32)
    phases = (bands[:, None] + lax.axis_index("freq")) * bands[None, :] % band
    phases = (2.0 * math.pi / band) * phases.astype(F32)
    tables = jnp.stack([jnp.cos(phases), jnp.sin(phases)])
    (estimate,) = call(step_kernel, "step", [result], [*right, own_left, other_left, start], flops=flops)
    (estimate,) = call(
        functools.partial(shrink_kernel, band),
        "shrink",
        [result],
        [tables, estimate, *starts[1:], *gradients],
        spaces=[pltpu.SMEM],
    )
    return estimate[None]


def solution(mesh):
    in_specs = (
        P("freq", "tile", None, None),
        P("freq", "tile", None, None),
        P("freq", None, None),
        P("freq", "tile", None),
        P("freq", "tile", None),
    )
    out_specs = P("freq", "tile", None)
    return jax.shard_map(body, mesh=mesh, in_specs=in_specs, out_specs=out_specs, check_vma=False)
```
